32 devices in a mesh: dp: 8 (over z, x), tensor: 4 (over y, core).
Axes of the slice: x: 2, y: 2, z: 4, core: 2. Of those that a mesh axis runs over, the one named last changes fastest.
Arguments:
- tokens: bfloat16 [16384, 1024], P('dp'), may hold values from -6 to 6
- cotangent: bfloat16 [16384, 1024], P('dp'), may hold values from -6 to 6
- segments: int32 [8, 2048], P('dp'), may hold values from 0 to 3, never falling along the last dimension, each value on 1 to 1024 neighbouring positions
- w_in_master: float32 [1024, 7, 1024], P('dp', None, 'tensor'), may hold values from -0.1875 to 0.1875
- w_out_master: float32 [5, 1024, 1024], P(None, 'tensor', 'dp'), may hold values from -0.6 to 0.6
- vec_master: float32 [5, 1024], replicated, may hold values from -1.2 to 1.5, as said below
- bias_in_master: float32 [7, 1024], P(None, 'tensor'), may hold values from -1.5 to 1.5
- w_in_mom: float32 [1024, 7, 1024], P('dp', None, 'tensor'), may hold values from -6 to 6
- w_out_mom: float32 [5, 1024, 1024], P(None, 'tensor', 'dp'), may hold values from -6 to 6
- vec_mom: float32 [5, 1024], P(None, 'tensor'), may hold values from -48 to 48
- bias_in_mom: float32 [7, 1024], P(None, 'tensor'), may hold values from -24 to 24
- w_in_error: float32 [8, 1024, 7, 1024], P('dp', None, None, 'tensor'), may hold values from -128 to 128
- w_out_error: float32 [8, 5, 1024, 1024], P('dp', None, 'tensor'), may hold values from -128 to 128
- q_in: float32 [7, 1024, 8], P(None, 'tensor'), may hold values from -6 to 6
- q_out: float32 [5, 1024, 8], P(None, 'tensor'), may hold values from -6 to 6
Outputs:
- block_out: bfloat16 [16384, 1024], P('dp', 'tensor')
- input_grad: float32 [16384, 1024], P('dp', 'tensor')
- w_in_new: float32 [1024, 7, 1024], P('dp', None, 'tensor')
- w_out_new: float32 [5, 1024, 1024], P(None, 'tensor', 'dp')
- vec_new: float32 [5, 1024], P(None, 'tensor')
- bias_in_new: float32 [7, 1024], P(None, 'tensor')
- w_in_mom_new: float32 [1024, 7, 1024], P('dp', None, 'tensor')
- w_out_mom_new: float32 [5, 1024, 1024], P(None, 'tensor', 'dp')
- vec_mom_new: float32 [5, 1024], P(None, 'tensor')
- bias_in_mom_new: float32 [7, 1024], P(None, 'tensor')
- w_in_error_new: float32 [8, 1024, 7, 1024], P('dp', None, None, 'tensor')
- w_out_error_new: float32 [8, 5, 1024, 1024], P('dp', None, 'tensor')
- q_in_new: float32 [7, 1024, 8], P(None, 'tensor')
- q_out_new: float32 [5, 1024, 8], P(None, 'tensor')
The draws below stay inside these ranges and needn't reach their ends.
Inputs may be any that keep to these rules, and one draw needn't show every extreme that they name: `segments`: segment numbers never fall along a sequence; a document is a run of equal numbers of at most 1024 tokens, and one document of each sequence has exactly that many. `vec_master`: rows 0 and 2 are gains, rows 1, 3 and 4 biases.
All inputs are finite; a program needn't handle non-finite values.
Results may differ from the reference program's by a relative error of at most 0.011.
Values may be sent and summed in bfloat16 or wider, within the bound.
A program may use at most 192 MiB of HBM per device.

```python
import math
import jax
import jax.numpy as jnp
import numpy as np
from jax import lax

D = 1024
HEADS = 16
FF = 4096
HEAD_DIM = 64
ROT = 16
RANK = 8
SEQ_LEN = 2048
SEQS_DEV = 1
WORKERS = 8
SEQS = 8
TOKENS = 16384
N_TENSOR = 4


def draw_w_out_master(key, part):
    key = jax.random.fold_in(key, 12)
    slot_index = jnp.arange(5)[:, None, None]
    factor = jnp.where(slot_index == 0, 0.15, 1.5 / FF ** 0.5)
    base = jnp.clip(jax.random.normal(key, (5, D, D)), -4.0, 4.0)
    return (base * factor).astype(jnp.float32)


def draw_vec_master(key, part):
    key = jax.random.fold_in(key, 11)
    subkeys = jax.random.split(key, 2)
    row_index = jnp.arange(5)[:, None]
    is_gain = (row_index == 0) | (row_index == 2)
    gain_rows = 1.0 + 0.25 * jax.random.uniform(subkeys[0], (5, D), minval=-1.0, maxval=1.0)
    others = 0.3 * jnp.clip(jax.random.normal(subkeys[1], (5, D)), -4.0, 4.0)
    return jnp.where(is_gain, gain_rows, others).astype(jnp.float32)


def level_of(own_key, extent, cuts, smallest, high):
    def one(dim, blocks):
        steps = jax.random.uniform(jax.random.fold_in(jax.random.fold_in(own_key, 6), dim), (blocks,), jnp.float32, smallest / len(cuts), high / len(cuts))
        return jnp.repeat(jnp.exp(steps), extent[dim] // blocks).reshape((-1,) + (1,) * (len(extent) - dim - 1))

    factor_of = one(*cuts[0])
    for cut in cuts[1:]:
        factor_of = factor_of * one(*cut)
    return factor_of


def length_profile(amount, total, reach, slope):
    weights = [(1 << 20) // math.isqrt(rank ** slope) + 1 for rank in range(2, amount + 1)]
    spare, counts = total - reach - (amount - 1), [1] * (amount - 1)
    while spare > 0:
        candidates = [i for i in range(amount - 1) if counts[i] < reach]
        whole, left = sum([weights[i] for i in candidates]), spare
        for i in candidates:
            extra = min(reach - counts[i], max(1, left * weights[i] // whole), spare)
            counts[i] = counts[i] + extra
            spare = spare - extra
    return np.array([reach] + counts)


def ragged(rng, number_of, total, bound, skew):
    if number_of == 2:
        one = jax.random.randint(rng, (), max(1, total - bound), min(bound, total - 1) + 1)
        return jnp.stack([one, total - one])
    lengths = jnp.asarray(length_profile(number_of, total, bound, skew), jnp.int32)
    couples = (number_of - 1) // 2
    donor, receiver = lengths[1:1 + 2 * couples:2], lengths[2:2 + 2 * couples:2]
    room = jnp.minimum(donor - 1, bound - receiver)
    moved = jax.random.randint(jax.random.fold_in(rng, 1), (couples,), 0, 1 << 20) % (room + 1)
    lengths = lengths.at[1:1 + 2 * couples:2].set(donor - moved).at[2:2 + 2 * couples:2].set(receiver + moved)
    return lengths[jax.random.permutation(jax.random.fold_in(rng, 2), number_of)]


def gaussian(key, dims, width, bound, cuts=(), kind=jnp.bfloat16):
    level = level_of(key, dims, cuts, -0.22, 0.18) if cuts else 1.0
    entries = jax.random.normal(key, dims, jnp.float32) * width * level
    return jnp.minimum(jnp.maximum(entries, -bound), bound).astype(kind)


def setup_inputs(seed: int = 0) -> dict:
    streams_of = jax.random.split(jax.random.key(seed), 16)
    tokens = gaussian(streams_of[0], (TOKENS, D), 1.0, 6.0, ((0, 8),))
    cotangent = gaussian(streams_of[1], (TOKENS, D), 1.0, 6.0, ((0, 8),))
    segments = jax.vmap(lambda own: jnp.searchsorted(jnp.cumsum(ragged(own, 4, SEQ_LEN, SEQ_LEN // 2, 0)), jnp.arange(SEQ_LEN), side="right"))(jax.random.split(streams_of[2], SEQS)).reshape((SEQS, SEQ_LEN)).astype(jnp.int32)
    w_in_master = gaussian(streams_of[3], (D, 7, D), D ** -0.5, 0.1875, ((0, 8), (2, 4)), jnp.float32)
    w_out_master = draw_w_out_master(jax.random.fold_in(streams_of[15], 71), 0)
    vec_master = draw_vec_master(jax.random.fold_in(streams_of[15], 71), 0)
    bias_in_master = gaussian(streams_of[6], (7, D), 0.3, 1.5, ((1, 4),), jnp.float32)
    w_in_mom = gaussian(streams_of[7], (D, 7, D), ((SEQS_DEV * SEQ_LEN * RANK / (D * WORKERS)) ** 0.5), 6.0, ((0, 8), (2, 4)), jnp.float32)
    w_out_mom = gaussian(streams_of[8], (5, D, D), ((SEQS_DEV * SEQ_LEN * RANK / (D * WORKERS)) ** 0.5), 6.0, ((1, 4), (2, 8)), jnp.float32)
    vec_mom = gaussian(streams_of[9], (5, D), ((SEQS_DEV * SEQ_LEN / WORKERS) ** 0.5 / 2), 48.0, ((1, 4),), jnp.float32)
    bias_in_mom = gaussian(streams_of[10], (7, D), ((SEQS_DEV * SEQ_LEN / WORKERS) ** 0.5 / 4), 24.0, ((1, 4),), jnp.float32)
    w_in_error = gaussian(streams_of[11], (WORKERS, D, 7, D), ((SEQS_DEV * SEQ_LEN) ** 0.5 / 2), 128.0, ((0, 8), (3, 4)), jnp.float32)
    w_out_error = gaussian(streams_of[12], (WORKERS, 5, D, D), ((SEQS_DEV * SEQ_LEN) ** 0.5 / 2), 128.0, ((0, 8), (2, 4)), jnp.float32)
    q_in = gaussian(streams_of[13], (7, D, RANK), 1.0, 6.0, ((1, 4),), jnp.float32)
    q_out = gaussian(streams_of[14], (5, D, RANK), 1.0, 6.0, ((1, 4),), jnp.float32)
    return dict(tokens=tokens, cotangent=cotangent, segments=segments, w_in_master=w_in_master, w_out_master=w_out_master, vec_master=vec_master, bias_in_master=bias_in_master, w_in_mom=w_in_mom, w_out_mom=w_out_mom, vec_mom=vec_mom, bias_in_mom=bias_in_mom, w_in_error=w_in_error, w_out_error=w_out_error, q_in=q_in, q_out=q_out)


@jax.custom_vjp
def low(v):
    return lax.optimization_barrier(v.astype(jnp.bfloat16)).astype(jnp.float32)

@jax.custom_vjp
def low_back(v):
    return v

def low_keep(v):
    return (low(v), None)

def low_pass(kept, grad):
    return (grad,)

def back_keep(v):
    return (v, None)

def back_low(kept, grad):
    return (low(grad),)
low.defvjp(low_keep, low_pass)
low_back.defvjp(back_keep, back_low)
EPSILON = 1e-05
SCORE_SCALE = 0.125
MASKED_SCORE = -1000000000.0
MOMENTUM_DECAY = 0.9
LEARN_RATE = 0.05
VECTOR_RATE = 0.05
PRECISE = lax.Precision.HIGHEST

def layer_norm(values, gain, bias):
    center = lax.optimization_barrier(jnp.mean(values, -1, keepdims=True))
    shifted = values - center
    spread = lax.optimization_barrier(jnp.mean(shifted * shifted, -1, keepdims=True))
    return shifted * lax.rsqrt(spread + EPSILON) * gain + bias

def positions_of(segs):
    length = segs.shape[0]
    index = jnp.arange(length, dtype=jnp.int32)
    change = jnp.concatenate([jnp.ones((1,), dtype=bool), segs[1:] != segs[:-1]])
    return index - lax.cummax(jnp.where(change, index, 0), axis=0)

def rotary_tables(positions):
    half = ROT // 2
    inverse = 10000.0 ** (-jnp.arange(half, dtype=jnp.float32) * 2.0 / ROT)
    angles = positions.astype(jnp.float32)[:, None] * inverse[None, :]
    angles = jnp.concatenate([angles, angles], 1)
    return (jnp.cos(angles), jnp.sin(angles))

def rotate(values, cosine, sine):
    half = ROT // 2
    part = values[..., :ROT]
    turned = jnp.concatenate([-part[..., half:], part[..., :half]], -1)
    mixed = part * cosine[:, None, :] + turned * sine[:, None, :]
    return jnp.concatenate([mixed, values[..., ROT:]], -1)

def attend(block, segs):
    length = segs.shape[0]
    cosine, sine = rotary_tables(positions_of(segs))
    query = low(rotate(block[:, 0], cosine, sine))
    key = low(rotate(block[:, 1], cosine, sine))
    value = low(block[:, 2])
    rows = min(512, length)
    count = length // rows
    index = jnp.arange(length, dtype=jnp.int32)

    def one_block(item):
        query_rows, seg_rows, index_rows = item
        scores = low_back(jnp.einsum('qhe,khe->hqk', query_rows, key, precision=PRECISE) * SCORE_SCALE)
        allowed = (seg_rows[:, None] == segs[None, :]) & (index_rows[:, None] >= index[None, :])
        scores = jnp.where(allowed[None], scores, MASKED_SCORE)
        top_score = lax.optimization_barrier(jnp.max(scores, -1, keepdims=True))
        weights = jnp.exp(scores - top_score)
        probs = low(weights / lax.optimization_barrier(jnp.sum(weights, -1, keepdims=True)))
        return jnp.einsum('hqk,khe->qhe', probs, value, precision=PRECISE)
    outputs = lax.map(jax.checkpoint(one_block), (query.reshape(count, rows, HEADS, HEAD_DIM), segs.reshape(count, rows), index.reshape(count, rows)))
    return outputs.reshape(length, D)

def forward(inputs, w_in, w_out, vectors, bias_in, segs):
    norm_one = low(layer_norm(inputs, vectors[0], vectors[1]))
    norm_two = low(layer_norm(inputs, vectors[2], vectors[3]))
    w_in_low = low(w_in)
    w_out_low = low(w_out)
    qkv = jnp.dot(norm_one, w_in_low[:, :3, :].reshape(D, 3 * D), precision=PRECISE) + bias_in[:3].reshape(3 * D)
    qkv = low_back(qkv)
    up_proj = jnp.dot(norm_two, w_in_low[:, 3:, :].reshape(D, FF), precision=PRECISE) + bias_in[3:].reshape(FF)
    up_proj = low_back(up_proj)
    hidden = low(jax.nn.gelu(up_proj, approximate=False))
    blocks = qkv.reshape(SEQS_DEV, SEQ_LEN, 3, HEADS, HEAD_DIM)
    attended = lax.map(lambda item: attend(item[0], item[1]), (blocks, segs))
    attended = low_back(low(attended.reshape(SEQS_DEV * SEQ_LEN, D)))
    mixed = jnp.concatenate([attended, hidden], 1)
    return inputs + jnp.dot(mixed, w_out_low.reshape(5 * D, D), precision=PRECISE) + vectors[4]

def orthonormal(matrix):
    columns = []
    for column_id in range(matrix.shape[1]):
        column = matrix[:, column_id]
        for previous in columns:
            column = column - jnp.sum(previous * column) * previous
        column = column * lax.rsqrt(jnp.sum(column * column) + 1e-06)
        columns.append(column)
    return jnp.stack(columns, 1)

def reference(tokens, cotangent, segments, w_in_master, w_out_master, vec_master, bias_in_master, w_in_mom, w_out_mom, vec_mom, bias_in_mom, w_in_error, w_out_error, q_in, q_out):
    local_tokens = SEQS_DEV * SEQ_LEN
    inputs_all = tokens.astype(jnp.float32).reshape(WORKERS, local_tokens, D)
    cot_all = cotangent.astype(jnp.float32).reshape(WORKERS, local_tokens, D)
    seg_all = segments.reshape(WORKERS, SEQS_DEV, SEQ_LEN)

    def worker(item):
        inputs, cot, segs = item
        result, pullback = jax.vjp(lambda a, b, c, e, f: forward(a, b, c, e, f, segs), inputs, w_in_master, w_out_master, vec_master, bias_in_master)
        grads = pullback(cot)
        return (result,) + tuple(grads)
    outputs, input_grads, grad_in, grad_out, grad_vec, grad_bias = lax.map(worker, (inputs_all, cot_all, seg_all))
    matrix_in = grad_in + w_in_error
    matrix_out = grad_out + w_out_error
    share = D // N_TENSOR
    approx_in_parts, approx_out_parts, right_in_parts, right_out_parts = ([], [], [], [])
    for block_id in range(N_TENSOR):
        first_col = block_id * share
        last_col = first_col + share
        part_in = matrix_in[:, :, :, first_col:last_col]
        left = jnp.einsum('wdsj,sjr->dr', part_in, q_in[:, first_col:last_col], precision=PRECISE) / WORKERS
        basis = orthonormal(left)
        right = jnp.einsum('wdsj,dr->sjr', part_in, basis, precision=PRECISE) / WORKERS
        approx_in_parts.append(jnp.einsum('dr,sjr->dsj', basis, right, precision=PRECISE))
        right_in_parts.append(right)
        part_out = matrix_out[:, :, first_col:last_col, :]
        left = jnp.einsum('wsjd,sjr->dr', part_out, q_out[:, first_col:last_col], precision=PRECISE) / WORKERS
        basis = orthonormal(left)
        right = jnp.einsum('wsjd,dr->sjr', part_out, basis, precision=PRECISE) / WORKERS
        approx_out_parts.append(jnp.einsum('dr,sjr->sjd', basis, right, precision=PRECISE))
        right_out_parts.append(right)
    approx_in = jnp.concatenate(approx_in_parts, 2)
    approx_out = jnp.concatenate(approx_out_parts, 1)
    w_in_error_new = matrix_in - approx_in[None]
    w_out_error_new = matrix_out - approx_out[None]
    w_in_mom_new = MOMENTUM_DECAY * w_in_mom + approx_in
    w_out_mom_new = MOMENTUM_DECAY * w_out_mom + approx_out
    w_in_new = w_in_master - LEARN_RATE * w_in_mom_new
    w_out_new = w_out_master - LEARN_RATE * w_out_mom_new
    vec_mom_new = MOMENTUM_DECAY * vec_mom + lax.optimization_barrier(jnp.mean(grad_vec, 0))
    vec_new = vec_master - VECTOR_RATE * vec_mom_new
    bias_in_mom_new = MOMENTUM_DECAY * bias_in_mom + lax.optimization_barrier(jnp.mean(grad_bias, 0))
    bias_in_new = bias_in_master - VECTOR_RATE * bias_in_mom_new
    q_in_new = jnp.concatenate(right_in_parts, 1)
    q_out_new = jnp.concatenate(right_out_parts, 1)
    block_out = outputs.reshape(TOKENS, D).astype(jnp.bfloat16)
    input_grad = input_grads.reshape(TOKENS, D)
    return (block_out, input_grad, w_in_new, w_out_new, vec_new, bias_in_new, w_in_mom_new, w_out_mom_new, vec_mom_new, bias_in_mom_new, w_in_error_new, w_out_error_new, q_in_new, q_out_new)
```

```python
import functools

import jax
import jax.numpy as jnp
from jax import lax
from jax.experimental import pallas as pl
from jax.experimental.pallas import tpu as pltpu
from jax.sharding import PartitionSpec as P

HEAD_DIM = 64
ROT = 16
EPSILON = 1e-05
MOMENTUM_DECAY = 0.9
LEARN_RATE = 0.05
VECTOR_RATE = 0.05
LN2 = 0.6931471805599453
LOG2E = 1.4426950408889634
QUERY_SCALE = 0.125 * LOG2E
FAR = 2.0**30
BLOCK = 256
LANES = 128
MOST_BLOCKS = 5

f32 = jnp.float32
bf16 = jnp.bfloat16
ROWS = (((0,), (0,)), ((), ()))
COLS = (((1,), (1,)), ((), ()))


def dot(a, b, dims=(((1,), (0,)), ((), ()))):
    return lax.dot_general(a, b, dims, preferred_element_type=f32)


def params(**more):
    return pltpu.CompilerParams(vmem_limit_bytes=56 * 1024 * 1024, **more)


def pieces(value):
    high = value.astype(bf16)
    rest = value - high.astype(f32)
    middle = rest.astype(bf16)
    low = (rest - middle.astype(f32)).astype(bf16)
    return high, middle, low


def stacked(value):
    return jnp.concatenate([part.astype(f32) for part in pieces(value)], 0).astype(bf16)


def folded(total, rows=8):
    return total[:rows] + total[rows : 2 * rows] + total[2 * rows : 3 * rows]


def full(shape):
    return pl.BlockSpec(shape, lambda i: (0,) * len(shape))


def norm_kernel(x_ref, vec_ref, one_ref, two_ref, one_t_ref, two_t_ref, mean_ref, rstd_ref):
    x = x_ref[...].astype(f32)
    mean = jnp.mean(x, 1, keepdims=True)
    shifted = x - mean
    rstd = lax.rsqrt(jnp.mean(shifted * shifted, 1, keepdims=True) + EPSILON)
    normed = shifted * rstd
    one = (normed * vec_ref[0:1, :] + vec_ref[1:2, :]).astype(bf16)
    two = (normed * vec_ref[2:3, :] + vec_ref[3:4, :]).astype(bf16)
    one_ref[...] = one
    two_ref[...] = two
    one_t_ref[...] = one.T
    two_t_ref[...] = two.T
    mean_ref[...] = mean
    rstd_ref[...] = rstd


def norms(tokens, vec):
    rows, width = tokens.shape
    block = pl.BlockSpec((BLOCK, width), lambda i: (i, 0))
    block_t = pl.BlockSpec((width, BLOCK), lambda i: (0, i))
    one = pl.BlockSpec((BLOCK, 1), lambda i: (i, 0))
    return pl.pallas_call(
        norm_kernel,
        grid=(rows // BLOCK,),
        in_specs=[block, full(vec.shape)],
        out_specs=[block, block, block_t, block_t, one, one],
        out_shape=[
            jax.ShapeDtypeStruct((rows, width), bf16),
            jax.ShapeDtypeStruct((rows, width), bf16),
            jax.ShapeDtypeStruct((width, rows), bf16),
            jax.ShapeDtypeStruct((width, rows), bf16),
            jax.ShapeDtypeStruct((rows, 1), f32),
            jax.ShapeDtypeStruct((rows, 1), f32),
        ],
        compiler_params=params(),
        cost_estimate=pl.CostEstimate(flops=0, bytes_accessed=20 * rows * width, transcendentals=0),
        name="norms",
    )(tokens, vec)


def error_in_kernel(q_ref, e_ref, out_ref):
    @pl.when(pl.program_id(0) == 0)
    def _():
        out_ref[...] = jnp.zeros_like(out_ref)

    high, middle, _ = pieces(e_ref[0])
    q = stacked(q_ref[0])
    out_ref[...] += folded(dot(q, high, COLS)) + folded(dot(q, middle, COLS))


def error_out_kernel(q_ref, e_ref, out_ref):
    @pl.when(pl.program_id(0) == 0)
    def _():
        out_ref[...] = jnp.zeros_like(out_ref)

    high, middle, _ = pieces(e_ref[0])
    q = stacked(q_ref[0])
    out_ref[...] += folded(dot(q, high)) + folded(dot(q, middle))


def error_left(kernel, q, error, width):
    slots = q.shape[0]
    return pl.pallas_call(
        kernel,
        grid=(slots,),
        in_specs=[
            pl.BlockSpec((1,) + q.shape[1:], lambda i: (i, 0, 0)),
            pl.BlockSpec((1,) + error.shape[1:], lambda i: (i, 0, 0)),
        ],
        out_specs=full((8, width)),
        out_shape=jax.ShapeDtypeStruct((8, width), f32),
        compiler_params=params(),
        cost_estimate=pl.CostEstimate(flops=0, bytes_accessed=error.size * 4, transcendentals=0),
        name="error_left",
    )(q, error)


def lane_of(rows):
    return lax.broadcasted_iota(jnp.int32, (rows, LANES), 1)


def turned(value, cosine, sine_a, sine_b):
    return (
        value * cosine
        + pltpu.roll(value, LANES - ROT // 2, 1) * sine_a
        + pltpu.roll(value, ROT // 2, 1) * sine_b
    )


def forward_kernel(
    count_ref, x_ref, w_ref, bias_ref, cos_ref, sa_ref, sb_ref, seg_ref,
    q_ref, k_ref, v_ref, o_ref, log_ref, keys, vals,
):
    step = pl.program_id(0)
    row = pl.multiple_of(step * BLOCK, BLOCK)
    x = x_ref[...]
    cosine, sine_a, sine_b = cos_ref[...], sa_ref[...], sb_ref[...]
    lane = lane_of(BLOCK)
    spot = lane & (HEAD_DIM - 1)
    same = spot == seg_ref[...]
    key_aug = jnp.where(spot < 4, jnp.where(same, 1.0, 0.0), 1.0)
    query_aug = jnp.where(spot < 4, jnp.where(same, 0.0, -FAR), 0.0)
    heads = 2 * (o_ref.shape[1] // LANES)
    queries = []
    proj = [dot(x, w_ref[s]) + bias_ref[s : s + 1, :] for s in range(3)]
    for tile in range(heads // 2):
        cols = slice(tile * LANES, (tile + 1) * LANES)
        q = (turned(proj[0][:, cols], cosine, sine_a, sine_b) * QUERY_SCALE).astype(bf16)
        k = turned(proj[1][:, cols], cosine, sine_a, sine_b).astype(bf16)
        v = proj[2][:, cols].astype(bf16)
        q_ref[:, cols], k_ref[:, cols], v_ref[:, cols] = q, k, v
        q, k, v = q.astype(f32), k.astype(f32), v.astype(f32)
        for odd in range(2):
            own = (lane >= HEAD_DIM) if odd else (lane < HEAD_DIM)
            head = 2 * tile + odd
            queries.append(jnp.where(own, q, query_aug).astype(bf16))
            keys[head, pl.ds(row, BLOCK), :] = jnp.where(own, k, key_aug).astype(bf16)
            vals[head, pl.ds(row, BLOCK), :] = jnp.where(own, v, 1.0).astype(bf16)
    below = lax.broadcasted_iota(jnp.int32, (BLOCK, BLOCK), 0) >= lax.broadcasted_iota(
        jnp.int32, (BLOCK, BLOCK), 1
    )

    def attend(blocks):
        first = pl.multiple_of(row - (blocks - 1) * BLOCK, BLOCK)
        for tile in range(heads // 2):
            cols = slice(tile * LANES, (tile + 1) * LANES)
            results = []
            for odd in range(2):
                head = 2 * tile + odd
                q = queries[head]
                near = dot(q, keys[head, pl.ds(row, BLOCK), :], COLS)
                near = jnp.where(below, near, -FAR)
                top = jnp.max(near, 1, keepdims=True)
                if blocks > 1:
                    span = pl.ds(first, (blocks - 1) * BLOCK)
                    far = dot(q, keys[head, span, :], COLS)
                    top = jnp.maximum(top, jnp.max(far, 1, keepdims=True))
                    far_p = jnp.exp2(far - top).astype(bf16)
                near_p = jnp.exp2(near - top).astype(bf16)
                out = dot(near_p, vals[head, pl.ds(row, BLOCK), :])
                if blocks > 1:
                    out = out + dot(far_p, vals[head, span, :])
                total = pltpu.roll(out, HEAD_DIM, 1)
                results.append((out / total, top + jnp.log2(out)))
            low = lane < HEAD_DIM
            o_ref[:, cols] = jnp.where(low, results[0][0], results[1][0])
            log_ref[:, cols] = jnp.where(low, results[1][1], results[0][1])

    for blocks in range(1, MOST_BLOCKS + 1):
        pl.when(count_ref[step] == blocks)(functools.partial(attend, blocks))


def attention_forward(counts, norm_one, w_attn, bias, tables, seg_col):
    rows, width = norm_one.shape
    local = w_attn.shape[2]
    heads = local // HEAD_DIM
    block = lambda cols: pl.BlockSpec((BLOCK, cols), lambda i, *_: (i, 0))
    whole = lambda shape: pl.BlockSpec(shape, lambda i, *_: (0,) * len(shape))
    return pl.pallas_call(
        forward_kernel,
        grid_spec=pltpu.PrefetchScalarGridSpec(
            num_scalar_prefetch=1,
            grid=(rows // BLOCK,),
            in_specs=[
                block(width), whole(w_attn.shape), whole(bias.shape),
                block(LANES), block(LANES), block(LANES), block(1),
            ],
            out_specs=[block(local)] * 5,
            scratch_shapes=[
                pltpu.VMEM((heads, rows, LANES), bf16),
                pltpu.VMEM((heads, rows, LANES), bf16),
            ],
        ),
        out_shape=[jax.ShapeDtypeStruct((rows, local), bf16)] * 3
        + [jax.ShapeDtypeStruct((rows, local), f32)] * 2,
        compiler_params=params(),
        cost_estimate=pl.CostEstimate(
            flops=2 * rows * width * 3 * local + 8 * rows * 1024 * 128 * heads // 4,
            bytes_accessed=16 * rows * local, transcendentals=rows * 1024 * heads,
        ),
        name="attention_forward",
    )(counts, norm_one, w_attn, bias, *tables, seg_col)


def backward_kernel(
    count_ref, g_ref, w_ref, q_ref, k_ref, v_ref, o_ref, log_ref, cos_ref, sa_ref, sb_ref, seg_ref,
    x_ref, factor_ref, gq_ref, left_ref, bias_ref, queries, grads, turn,
):
    step = pl.program_id(0)
    steps = pl.num_programs(0)
    block_id = steps - 1 - step
    row = pl.multiple_of(block_id * BLOCK, BLOCK)
    lane = lane_of(BLOCK)
    spot = lane & (HEAD_DIM - 1)
    same = spot == seg_ref[pl.ds(row, BLOCK), :]
    local = gq_ref.shape[2]
    heads = local // HEAD_DIM
    key_aug = jnp.where(spot < 4, jnp.where(same, 1.0, 0.0), 1.0)
    query_aug = jnp.where(same, 0.0, -FAR)

    @pl.when(step == 0)
    def _():
        turn[...] = jnp.zeros_like(turn)
        bias_ref[...] = jnp.zeros_like(bias_ref)

    grad_out = dot(g_ref[...], w_ref[...], COLS).astype(bf16)
    keys, vals = [], []
    for tile in range(heads // 2):
        cols = slice(tile * LANES, (tile + 1) * LANES)
        q, k, v = (ref[:, cols].astype(f32) for ref in (q_ref, k_ref, v_ref))
        do = grad_out[:, cols].astype(f32)
        both = do * o_ref[:, cols]
        logs = log_ref[:, cols]
        log_h = logs.astype(bf16).astype(f32)
        log_m = (logs - log_h).astype(bf16).astype(f32)
        log_l = logs - log_h - log_m
        aug = jnp.where(
            spot < 4, query_aug,
            jnp.where(spot == 4, -log_h, jnp.where(spot == 5, -log_m, jnp.where(spot == 6, -log_l, 0.0))),
        )
        for odd in range(2):
            own = (lane >= HEAD_DIM) if odd else (lane < HEAD_DIM)
            head = 2 * tile + odd
            delta = jnp.sum(jnp.where(own, both, 0.0), 1, keepdims=True)
            delta_h = delta.astype(bf16).astype(f32)
            delta_m = (delta - delta_h).astype(bf16).astype(f32)
            delta_l = delta - delta_h - delta_m
            delta_aug = jnp.where(
                spot == 0, -delta_h, jnp.where(spot == 1, -delta_m, jnp.where(spot == 2, -delta_l, 0.0))
            )
            queries[head, pl.ds(row, BLOCK), :] = jnp.where(own, q, aug).astype(bf16)
            grads[head, pl.ds(row, BLOCK), :] = jnp.where(own, do, delta_aug).astype(bf16)
            keys.append(jnp.where(own, k, key_aug).astype(bf16))
            vals.append(jnp.where(own, v, 1.0).astype(bf16))
    above = lax.broadcasted_iota(jnp.int32, (BLOCK, BLOCK), 0) <= lax.broadcasted_iota(
        jnp.int32, (BLOCK, BLOCK), 1
    )
    cosine, sine_a, sine_b = (ref[pl.ds(row, BLOCK), :] for ref in (cos_ref, sa_ref, sb_ref))

    def attend(blocks):
        for tile in range(heads // 2):
            cols = slice(tile * LANES, (tile + 1) * LANES)
            key_t = k_ref[:, cols].astype(f32).T.astype(bf16)
            results = []
            for odd in range(2):
                head = 2 * tile + odd
                key_rows = key_t[odd * HEAD_DIM : (odd + 1) * HEAD_DIM, :]
                turn_rows = slice(head * HEAD_DIM, (head + 1) * HEAD_DIM)
                grad_key = grad_val = None
                for first, size in ((0, 1), (1, blocks - 1)):
                    if size == 0:
                        continue
                    span = pl.ds(pl.multiple_of(row + first * BLOCK, BLOCK), size * BLOCK)
                    q = queries[head, span, :]
                    do = grads[head, span, :]
                    p = jnp.exp2(dot(keys[head], q, COLS))
                    if first == 0:
                        p = jnp.where(above, p, 0.0)
                    ds = (p * dot(vals[head], do, COLS)).astype(bf16)
                    dv = dot(p.astype(bf16), do)
                    dk = dot(ds, q)
                    grad_val = dv if grad_val is None else grad_val + dv
                    grad_key = dk if grad_key is None else grad_key + dk
                    turn[turn_rows, span] += dot(key_rows, ds)
                results.append((grad_key, grad_val))
            low = lane < HEAD_DIM
            dk = jnp.where(low, results[0][0], results[1][0]) * LN2
            dv = jnp.where(low, results[0][1], results[1][1])
            gq_ref[1, pl.ds(row, BLOCK), cols] = turned(dk, cosine, -sine_a, -sine_b).astype(bf16)
            gq_ref[2, pl.ds(row, BLOCK), cols] = dv.astype(bf16)

    for blocks in range(1, MOST_BLOCKS + 1):
        pl.when(count_ref[block_id] == blocks)(functools.partial(attend, blocks))

    @pl.when(step == steps - 1)
    def _():
        for part in range(turn.shape[1] // BLOCK):
            rows = slice(part * BLOCK, (part + 1) * BLOCK)
            for tile in range(heads // 2):
                cols = slice(tile * LANES, (tile + 1) * LANES)
                dq = turn[cols, rows].T * 0.125
                gq_ref[0, rows, cols] = turned(
                    dq, cos_ref[rows, :], -sa_ref[rows, :], -sb_ref[rows, :]
                ).astype(bf16)
        mixed = sum(dot(stacked(factor_ref[s]), gq_ref[s], COLS) for s in range(3))
        left_ref[...] = folded(dot(stacked(folded(mixed)), x_ref[...]))
        for s in range(3):
            bias_ref[s : s + 1, :] = jnp.sum(gq_ref[s].astype(f32), 0, keepdims=True)


def attention_backward(counts, cot, w_first, q, k, v, out, logs, tables, seg_col, norm_one, factors):
    rows, width = cot.shape
    local = q.shape[1]
    heads = local // HEAD_DIM
    steps = rows // BLOCK
    block = lambda cols: pl.BlockSpec((BLOCK, cols), lambda i, *_: (steps - 1 - i, 0))
    whole = lambda shape: pl.BlockSpec(shape, lambda i, *_: (0,) * len(shape))
    return pl.pallas_call(
        backward_kernel,
        grid_spec=pltpu.PrefetchScalarGridSpec(
            num_scalar_prefetch=1,
            grid=(steps,),
            in_specs=[
                block(width), whole(w_first.shape), block(local), block(local), block(local),
                block(local), block(local), whole((rows, LANES)), whole((rows, LANES)),
                whole((rows, LANES)), whole((rows, 1)), whole((rows, width)), whole(factors.shape),
            ],
            out_specs=[whole((3, rows, local)), whole((8, width)), whole((8, local))],
            scratch_shapes=[
                pltpu.VMEM((heads, rows, LANES), bf16),
                pltpu.VMEM((heads, rows, LANES), bf16),
                pltpu.VMEM((local, rows), f32),
            ],
        ),
        out_shape=[
            jax.ShapeDtypeStruct((3, rows, local), bf16),
            jax.ShapeDtypeStruct((8, width), f32),
            jax.ShapeDtypeStruct((8, local), f32),
        ],
        compiler_params=params(),
        cost_estimate=pl.CostEstimate(
            flops=2 * rows * width * local + 20 * rows * 1024 * 128 * heads // 4,
            bytes_accessed=16 * rows * local, transcendentals=rows * 1024 * heads,
        ),
        name="attention_backward",
    )(counts, cot, w_first, q, k, v, out, logs, *tables, seg_col, norm_one, factors)


def normal_cdf(value):
    bell = jnp.exp2(value * value * (-0.5 * LOG2E))
    t = 1.0 / (1.0 + (0.3275911 / 1.4142135623730951) * jnp.abs(value))
    poly = 0.5 * 1.061405429
    for coefficient in (-1.453152027, 1.421413741, -0.284496736, 0.254829592):
        poly = poly * t + 0.5 * coefficient
    tail = poly * t * bell
    return jnp.where(value >= 0.0, 1.0 - tail, tail), bell


def feed_kernel(
    x_ref, g_ref, o_ref, wu_ref, wo_ref, bias_ref, qi_ref, qo_ref,
    part_ref, gup_ref, mixed_t_ref, left_in_ref, left_out_ref, sums_ref,
):
    @pl.when(pl.program_id(0) == 0)
    def _():
        left_in_ref[...] = jnp.zeros_like(left_in_ref)
        left_out_ref[...] = jnp.zeros_like(left_out_ref)
        sums_ref[...] = jnp.zeros_like(sums_ref)

    x, g = x_ref[...], g_ref[...]
    slots, _, local = wu_ref.shape
    att = o_ref[...].astype(bf16)
    branch = dot(att, wo_ref[0:local, :])
    mixed_t = att.T
    mixed_t_ref[0] = mixed_t
    into_out = dot(stacked(qo_ref[0]), mixed_t)
    into_in = jnp.zeros_like(into_out)
    for s in range(slots):
        w_rows = slice((s + 1) * local, (s + 2) * local)
        up = dot(x, wu_ref[s]) + bias_ref[3 + s : 4 + s, :]
        grad_hidden = dot(g, wo_ref[w_rows, :], COLS)
        cdf, bell = normal_cdf(up)
        hidden = (up * cdf).astype(bf16)
        grad_up = (grad_hidden * (cdf + up * bell * 0.3989422804014327)).astype(bf16)
        gup_ref[s] = grad_up
        branch = branch + dot(hidden, wo_ref[w_rows, :])
        mixed_t = hidden.T
        mixed_t_ref[s + 1] = mixed_t
        into_out = into_out + dot(stacked(qo_ref[s + 1]), mixed_t)
        into_in = into_in + dot(stacked(qi_ref[3 + s]), grad_up, COLS)
        sums_ref[s : s + 1, :] += jnp.sum(grad_up.astype(f32), 0, keepdims=True)
    for c in range(part_ref.shape[0]):
        part_ref[c] = branch[:, c * local : (c + 1) * local].astype(bf16)
    left_in_ref[...] += folded(dot(stacked(folded(into_in)), x))
    left_out_ref[...] += folded(dot(stacked(folded(into_out)), g))


def feed(norm_two, cot, out, w_up, w_out, bias, q_in, q_out):
    rows, width = cot.shape
    slots, _, local = w_up.shape
    share = width // local
    block = lambda cols: pl.BlockSpec((BLOCK, cols), lambda i: (i, 0))
    return pl.pallas_call(
        feed_kernel,
        grid=(rows // BLOCK,),
        in_specs=[
            block(width), block(width), block(local), full(w_up.shape), full(w_out.shape),
            full(bias.shape), full(q_in.shape), full(q_out.shape),
        ],
        out_specs=[
            pl.BlockSpec((share, BLOCK, local), lambda i: (0, i, 0)),
            pl.BlockSpec((slots, BLOCK, local), lambda i: (0, i, 0)),
            pl.BlockSpec((slots + 1, local, BLOCK), lambda i: (0, 0, i)),
            full((8, width)), full((8, width)), full((8, local)),
        ],
        out_shape=[
            jax.ShapeDtypeStruct((share, rows, local), bf16),
            jax.ShapeDtypeStruct((slots, rows, local), bf16),
            jax.ShapeDtypeStruct((slots + 1, local, rows), bf16),
            jax.ShapeDtypeStruct((8, width), f32),
            jax.ShapeDtypeStruct((8, width), f32),
            jax.ShapeDtypeStruct((8, local), f32),
        ],
        compiler_params=params(),
        cost_estimate=pl.CostEstimate(
            flops=2 * rows * width * local * 13, bytes_accessed=16 * rows * width,
            transcendentals=rows * width * 2,
        ),
        name="feed",
    )(norm_two, cot, out, w_up, w_out, bias, q_in, q_out)


def norm_grad_kernel(
    gq_ref, gu_ref, wa_ref, wu_ref, x_ref, mean_ref, rstd_ref, vec_ref,
    part_ref, sum_ref, dot_ref, vec_grad_ref,
):
    @pl.when(pl.program_id(0) == 0)
    def _():
        vec_grad_ref[...] = jnp.zeros_like(vec_grad_ref)

    normed = (x_ref[...].astype(f32) - mean_ref[...]) * rstd_ref[...]
    local = gq_ref.shape[2]
    sums = dots = 0.0
    for c in range(part_ref.shape[0]):
        cols = slice(c * local, (c + 1) * local)
        one = sum(dot(gq_ref[s], wa_ref[s, cols, :], COLS) for s in range(gq_ref.shape[0]))
        two = sum(dot(gu_ref[s], wu_ref[s, cols, :], COLS) for s in range(gu_ref.shape[0]))
        scaled = one * vec_ref[0:1, cols] + two * vec_ref[2:3, cols]
        part_ref[c] = scaled.astype(bf16)
        sums = sums + jnp.sum(scaled, 1, keepdims=True)
        dots = dots + jnp.sum(scaled * normed[:, cols], 1, keepdims=True)
        vec_grad_ref[0:1, cols] += jnp.sum(one * normed[:, cols], 0, keepdims=True)
        vec_grad_ref[1:2, cols] += jnp.sum(one, 0, keepdims=True)
        vec_grad_ref[2:3, cols] += jnp.sum(two * normed[:, cols], 0, keepdims=True)
        vec_grad_ref[3:4, cols] += jnp.sum(two, 0, keepdims=True)
    sum_ref[...] = sums
    dot_ref[...] = dots


def norm_grad(grad_qkv, grad_up, w_attn, w_up, tokens, mean, rstd, vec):
    rows, width = tokens.shape
    local = w_up.shape[2]
    share = width // local
    block = lambda cols: pl.BlockSpec((BLOCK, cols), lambda i: (i, 0))
    slotted = lambda slots: pl.BlockSpec((slots, BLOCK, local), lambda i: (0, i, 0))
    return pl.pallas_call(
        norm_grad_kernel,
        grid=(rows // BLOCK,),
        in_specs=[
            slotted(3), slotted(w_up.shape[0]), full(w_attn.shape), full(w_up.shape),
            block(width), block(1), block(1), full(vec.shape),
        ],
        out_specs=[slotted(share), block(1), block(1), full((8, width))],
        out_shape=[
            jax.ShapeDtypeStruct((share, rows, local), bf16),
            jax.ShapeDtypeStruct((rows, 1), f32),
            jax.ShapeDtypeStruct((rows, 1), f32),
            jax.ShapeDtypeStruct((8, width), f32),
        ],
        compiler_params=params(),
        cost_estimate=pl.CostEstimate(
            flops=2 * rows * width * local * 7, bytes_accessed=8 * rows * width, transcendentals=0
        ),
        name="norm_grad",
    )(grad_qkv, grad_up, w_attn, w_up, tokens, mean, rstd, vec)


def matrix_kernel(a_ref, b_ref, e_ref, m_ref):
    m_ref[0] = dot(a_ref[...] if len(a_ref.shape) == 2 else a_ref[0],
                   b_ref[...] if len(b_ref.shape) == 2 else b_ref[0]) + e_ref[0]


def matrix_grad(left, right, error, first):
    slots = right.shape[0] if right.ndim == 3 else left.shape[0]
    spec = lambda a: full(a.shape) if a.ndim == 2 else pl.BlockSpec((1,) + a.shape[1:], lambda i: (i, 0, 0))
    shape = error.shape[1:]
    depth = left.shape[-1]
    return pl.pallas_call(
        matrix_kernel,
        grid=(slots,),
        in_specs=[spec(left), spec(right), pl.BlockSpec((1,) + shape, lambda i: (first + i, 0, 0))],
        out_specs=pl.BlockSpec((1,) + shape, lambda i: (i, 0, 0)),
        out_shape=jax.ShapeDtypeStruct((slots,) + shape, f32),
        compiler_params=params(),
        cost_estimate=pl.CostEstimate(
            flops=2 * slots * depth * shape[0] * shape[1],
            bytes_accessed=8 * slots * shape[0] * shape[1], transcendentals=0,
        ),
        name="matrix_grad",
    )(left, right, error)


def orthonormal_rows(matrix):
    index = lax.broadcasted_iota(jnp.int32, (matrix.shape[0], 1), 0)
    for r in range(matrix.shape[0]):
        row = matrix[r : r + 1, :]
        row = row * lax.rsqrt(jnp.sum(row * row, 1, keepdims=True) + 1e-06)
        along = jnp.sum(matrix * row, 1, keepdims=True)
        matrix = jnp.where(index == r, row, jnp.where(index > r, matrix - along * row, matrix))
    return matrix


def basis_kernel(left_in_ref, left_out_ref, basis_in_ref, basis_out_ref):
    basis_in_ref[...] = orthonormal_rows(left_in_ref[...])
    basis_out_ref[...] = orthonormal_rows(left_out_ref[...])


def bases(left_in, left_out):
    shape = jax.ShapeDtypeStruct(left_in.shape, f32)
    return pl.pallas_call(
        basis_kernel, out_shape=[shape, shape], compiler_params=params(), name="bases"
    )(left_in, left_out)


def right_kernel(dims, basis_ref, m_ref, out_ref):
    high, middle, _ = pieces(m_ref[0])
    basis = stacked(basis_ref[...])
    out_ref[0] = folded(dot(basis, high, dims)) + folded(dot(basis, middle, dims))


def right_factor(basis, matrix, dims, columns):
    slots = matrix.shape[0]
    return pl.pallas_call(
        functools.partial(right_kernel, dims),
        grid=(slots,),
        in_specs=[full(basis.shape), pl.BlockSpec((1,) + matrix.shape[1:], lambda i: (i, 0, 0))],
        out_specs=pl.BlockSpec((1, 8, columns), lambda i: (i, 0, 0)),
        out_shape=jax.ShapeDtypeStruct((slots, 8, columns), f32),
        compiler_params=params(),
        cost_estimate=pl.CostEstimate(flops=0, bytes_accessed=matrix.size * 4, transcendentals=0),
        name="right_factor",
    )(basis, matrix)


def outer(a, b):
    ah, am, al = (part.astype(f32) for part in pieces(a))
    bh, bm, bl = (part.astype(f32) for part in pieces(b))
    left = jnp.concatenate([ah, ah, am, ah, am, al], 0).astype(bf16)
    right = jnp.concatenate([bh, bm, bh, bl, bm, bh], 0).astype(bf16)
    return dot(left, right, ROWS)


def finish_kernel(swap, basis_ref, own_ref, right_ref, m_ref, mom_ref, w_ref, error_ref, new_mom_ref, new_w_ref):
    pair = lambda a, b: outer(b, a) if swap else outer(a, b)
    error_ref[0] = m_ref[0] - pair(basis_ref[...], right_ref[0])
    mom = MOMENTUM_DECAY * mom_ref[0] + pair(own_ref[...], right_ref[0])
    new_mom_ref[0] = mom
    new_w_ref[0] = w_ref[0] - LEARN_RATE * mom


def finish(swap, basis, own, right, matrix, mom, master):
    slots = right.shape[0]
    spec = lambda a: pl.BlockSpec((1,) + a.shape[1:], lambda i: (i, 0, 0))
    return pl.pallas_call(
        functools.partial(finish_kernel, swap),
        grid=(slots,),
        in_specs=[full(basis.shape), full(own.shape), spec(right), spec(matrix), spec(mom), spec(master)],
        out_specs=[spec(matrix), spec(mom), spec(master)],
        out_shape=[jax.ShapeDtypeStruct(a.shape, f32) for a in (matrix, mom, master)],
        compiler_params=params(),
        cost_estimate=pl.CostEstimate(flops=0, bytes_accessed=matrix.size * 10, transcendentals=0),
        name="finish",
    )(basis, own, right, matrix, mom, master)


def swapped(value, axis, bits):
    size = lax.axis_size(axis)
    return lax.ppermute(value, axis, [(i, i ^ bits) for i in range(size)])


def gathered(shard, dim):
    workers = lax.axis_size("dp")
    if workers != 8:
        return lax.all_gather(shard, "dp", axis=dim, tiled=True)
    me = lax.axis_index("dp")
    size = shard.shape[dim]
    shape = list(shard.shape)
    shape[dim] = size * workers
    line = [(0, shard)] + [(bits, swapped(shard, "dp", bits)) for bits in (2, 4, 6)]
    line = line + [(bits ^ 1, swapped(part, "dp", 1)) for bits, part in line]
    whole = jnp.zeros(shape, shard.dtype)
    for bits, part in line:
        whole = lax.dynamic_update_slice_in_dim(whole, part, (me ^ bits) * size, dim)
    return whole


def summed(value):
    if lax.axis_size("dp") != 8:
        return lax.psum(value, "dp")
    value = value + swapped(value, "dp", 1)
    near, far, last = (swapped(value, "dp", bits) for bits in (2, 4, 6))
    return (value + near) + (far + last)


def scattered(parts):
    count = lax.axis_size("tensor")
    me = lax.axis_index("tensor")
    if count != 4:
        return lax.psum_scatter(parts, "tensor", scatter_dimension=0, tiled=False).astype(f32)
    core = me % 2
    pairs = parts.reshape(2, 2, *parts.shape[1:])
    away = lax.dynamic_index_in_dim(pairs, 1 - core, 1, keepdims=False)
    here = lax.dynamic_index_in_dim(pairs, core, 1, keepdims=False)
    near = here.astype(f32) + swapped(away, "tensor", 1).astype(f32)
    chip = me // 2
    send = lax.dynamic_index_in_dim(near, 1 - chip, 0, keepdims=False).astype(bf16)
    keep = lax.dynamic_index_in_dim(near, chip, 0, keepdims=False)
    return keep + swapped(send, "tensor", 2).astype(f32)


def rotary(positions):
    half = ROT // 2
    inverse = 10000.0 ** (-jnp.arange(half, dtype=f32) * 2.0 / ROT)
    angles = positions.astype(f32)[:, None] * inverse[None, :]
    cosine, sine = jnp.cos(angles), jnp.sin(angles)
    none = jnp.zeros_like(cosine)
    rest = jnp.zeros((positions.shape[0], HEAD_DIM - ROT), f32)
    heads = LANES // HEAD_DIM
    return (
        jnp.concatenate([cosine, cosine, rest + 1.0] * heads, 1),
        jnp.concatenate([-sine, none, rest] * heads, 1),
        jnp.concatenate([none, sine, rest] * heads, 1),
    )


def on_device(
    tokens, cotangent, segments, w_in_master, w_out_master, vec_master, bias_in_master,
    w_in_mom, w_out_mom, vec_mom, bias_in_mom, w_in_error, w_out_error, q_in, q_out,
):
    workers = lax.axis_size("dp")
    tensor_index = lax.axis_index("tensor")
    worker_index = lax.axis_index("dp")
    rows, width = tokens.shape
    local = bias_in_master.shape[1]
    start_col = tensor_index * local
    cut = lambda a: lax.dynamic_slice_in_dim(a, start_col, local, 1)

    w_in = w_in_master.transpose(1, 0, 2)
    w_in_low, w_out_low = w_in.astype(bf16), w_out_master.astype(bf16)
    w_attn = gathered(w_in_low[:3], 1)
    w_first = gathered(w_out_low[0], 1)
    w_up = gathered(w_in_low[3:], 1)
    w_rest = gathered(w_out_low[1:].reshape(-1, w_out_low.shape[2]), 1)
    w_out = jnp.concatenate([w_first, w_rest], 0)

    segs = segments[0]
    index = jnp.arange(rows, dtype=jnp.int32)
    counts = [jnp.sum(segs == c, dtype=jnp.int32) for c in range(4)]
    before = sum(jnp.where(segs > c, counts[c], 0) for c in range(3))
    after = sum(jnp.where(segs >= c, counts[c], 0) for c in range(4))
    tables = rotary(index - before)
    blocks = jnp.arange(rows // BLOCK, dtype=jnp.int32)
    span_forward = blocks - before[::BLOCK] // BLOCK + 1
    span_backward = (after[BLOCK - 1 :: BLOCK] - 1) // BLOCK - blocks + 1
    seg_col = segs[:, None]

    factors_in, factors_out = q_in.transpose(0, 2, 1), q_out.transpose(0, 2, 1)
    error_in = w_in_error[0].transpose(1, 0, 2)
    error_out = w_out_error[0]
    norm_one, norm_two, one_t, two_t, mean, rstd = norms(tokens, vec_master)
    left_in = error_left(error_in_kernel, factors_in, error_in, width)
    left_out = error_left(error_out_kernel, factors_out, error_out, width)

    q, k, v, out, logs = attention_forward(
        span_forward, norm_one, w_attn, bias_in_master, tables, seg_col
    )
    grad_qkv, left_attn, bias_attn = attention_backward(
        span_backward, cotangent, w_first, q, k, v, out, logs, tables, seg_col, norm_one, factors_in
    )
    branch_parts, grad_up, mixed_t, left_up, left_mixed, bias_up = feed(
        norm_two, cotangent, out, w_up, w_out, bias_in_master, factors_in, factors_out
    )
    left_in = left_in + left_attn + left_up
    left_out = left_out + left_mixed
    left = summed(jnp.concatenate([left_in, left_out], 0)) / workers

    grad_parts, row_sum, row_dot, vec_local = norm_grad(
        grad_qkv, grad_up, w_attn, w_up, tokens, mean, rstd, vec_master
    )
    matrix_attn = matrix_grad(one_t, grad_qkv, error_in, 0)
    matrix_up = matrix_grad(two_t, grad_up, error_in, 3)
    matrix_out = matrix_grad(mixed_t, cotangent, error_out, 0)

    basis_in, basis_out = bases(left[:8], left[8:])
    plain = (((1,), (0,)), ((), ()))
    right_attn = right_factor(basis_in, matrix_attn, plain, local)
    right_up = right_factor(basis_in, matrix_up, plain, local)
    right_out = right_factor(basis_out, matrix_out, COLS, local)

    cot_cols = cut(cotangent).astype(f32)
    bias_local = jnp.concatenate([bias_attn[:3], bias_up[:4]], 0)
    vec_rows = lax.psum_scatter(
        vec_local[:4].reshape(4, -1, local), "tensor", scatter_dimension=1, tiled=False
    )
    vec_rows = jnp.concatenate([vec_rows, jnp.sum(cot_cols, 0)[None]], 0)
    sizes = [7 * 8, 5 * 8, 5, 7]
    bundle = summed(
        jnp.concatenate(
            [
                right_attn.reshape(-1, local), right_up.reshape(-1, local),
                right_out.reshape(-1, local), vec_rows, bias_local,
            ],
            0,
        )
    ) / workers
    cuts = [0]
    for size in sizes:
        cuts.append(cuts[-1] + size)
    right_in = bundle[cuts[0] : cuts[1]].reshape(7, 8, local)
    right_out = bundle[cuts[1] : cuts[2]].reshape(5, 8, local)
    vec_grad, bias_grad = bundle[cuts[2] : cuts[3]], bundle[cuts[3] : cuts[4]]

    owned = w_in_master.shape[0]
    own_in = lax.dynamic_slice_in_dim(basis_in, worker_index * owned, owned, 1)
    own_out = lax.dynamic_slice_in_dim(basis_out, worker_index * owned, owned, 1)
    w_in_mom = w_in_mom.transpose(1, 0, 2)
    matrix_in = jnp.concatenate([matrix_attn, matrix_up], 0)
    new_error_in, new_mom_in, new_w_in = finish(
        False, basis_in, own_in, right_in, matrix_in, w_in_mom, w_in
    )
    new_error_out, new_mom_out, new_w_out = finish(
        True, basis_out, own_out, right_out, matrix_out, w_out_mom, w_out_master
    )

    vec_mom_new = MOMENTUM_DECAY * vec_mom + vec_grad
    vec_new = cut(vec_master) - VECTOR_RATE * vec_mom_new
    bias_in_mom_new = MOMENTUM_DECAY * bias_in_mom + bias_grad
    bias_in_new = bias_in_master - VECTOR_RATE * bias_in_mom_new

    token_cols = cut(tokens).astype(f32)
    block_out = (token_cols + scattered(branch_parts) + cut(vec_master)[4:5]).astype(bf16)
    row_means = lax.psum(jnp.concatenate([row_sum, row_dot], 1), "tensor") / width
    normed_cols = (token_cols - mean) * rstd
    input_grad = cot_cols + rstd * (
        scattered(grad_parts) - row_means[:, 0:1] - normed_cols * row_means[:, 1:2]
    )
    return (
        block_out,
        input_grad,
        new_w_in.transpose(1, 0, 2),
        new_w_out,
        vec_new,
        bias_in_new,
        new_mom_in.transpose(1, 0, 2),
        new_mom_out,
        vec_mom_new,
        bias_in_mom_new,
        new_error_in.transpose(1, 0, 2)[None],
        new_error_out[None],
        right_in.transpose(0, 2, 1),
        right_out.transpose(0, 2, 1),
    )


def solution(mesh):
    return jax.shard_map(
        on_device,
        mesh=mesh,
        in_specs=(
            P("dp", None), P("dp", None), P("dp", None), P("dp", None, "tensor"),
            P(None, "tensor", "dp"), P(), P(None, "tensor"), P("dp", None, "tensor"),
            P(None, "tensor", "dp"), P(None, "tensor"), P(None, "tensor"),
            P("dp", None, None, "tensor"), P("dp", None, "tensor", None),
            P(None, "tensor", None), P(None, "tensor", None),
        ),
        out_specs=(
            P("dp", "tensor"), P("dp", "tensor"), P("dp", None, "tensor"), P(None, "tensor", "dp"),
            P(None, "tensor"), P(None, "tensor"), P("dp", None, "tensor"), P(None, "tensor", "dp"),
            P(None, "tensor"), P(None, "tensor"), P("dp", None, None, "tensor"),
            P("dp", None, "tensor", None), P(None, "tensor", None), P(None, "tensor", None),
        ),
        check_vma=False,
    )
```

```python
import functools

import jax
import jax.numpy as jnp
from jax import lax
from jax.experimental import pallas as pl
from jax.experimental.pallas import tpu as pltpu
from jax.sharding import PartitionSpec as P

HEAD_DIM = 64
ROT = 16
EPSILON = 1e-05
MOMENTUM_DECAY = 0.9
LEARN_RATE = 0.05
VECTOR_RATE = 0.05
LN2 = 0.6931471805599453
LOG2E = 1.4426950408889634
QUERY_SCALE = 0.125 * LOG2E
FAR = 2.0**30
BLOCK = 256
LANES = 128
MOST_BLOCKS = 5

f32 = jnp.float32
bf16 = jnp.bfloat16
ROWS = (((0,), (0,)), ((), ()))
COLS = (((1,), (1,)), ((), ()))
PLAIN = (((1,), (0,)), ((), ()))
MESH = pl.DeviceIdType.MESH


def dot(a, b, dims=PLAIN):
    return lax.dot_general(a, b, dims, preferred_element_type=f32)


def params(**more):
    return pltpu.CompilerParams(vmem_limit_bytes=56 * 1024 * 1024, **more)


def pieces(value):
    high = value.astype(bf16)
    rest = value - high.astype(f32)
    middle = rest.astype(bf16)
    low = (rest - middle.astype(f32)).astype(bf16)
    return high, middle, low


def stacked(value):
    return jnp.concatenate([part.astype(f32) for part in pieces(value)], 0).astype(bf16)


def folded(total, rows=8):
    return total[:rows] + total[rows : 2 * rows] + total[2 * rows : 3 * rows]


def full(shape):
    return pl.BlockSpec(shape, lambda i: (0,) * len(shape))


class Relay:
    LANES = ("up", "down", "x")

    def __init__(self, own, place, sems):
        self.own, self.place, self.sems = own, place, sems
        me = lax.axis_index("dp")
        self.z, self.x = lax.div(me, 2), lax.rem(me, 2)
        self.last = lax.axis_size("dp") // 2 - 1

    def copy(self, distance, lane):
        index = self.LANES.index(lane)
        step = (1, -1, 0)[index]
        worker = (self.z + distance) * 2 + self.x
        to = (self.z + step) * 2 + (1 - self.x if lane == "x" else self.x)
        return pltpu.make_async_remote_copy(
            src_ref=self.own if distance == 0 else self.place(worker),
            dst_ref=self.place(worker),
            send_sem=self.sems.at[0, index, distance + 3],
            recv_sem=self.sems.at[1, index, distance - step + 3],
            device_id={"dp": to},
            device_id_type=MESH,
        )

    def arrival(self, distance, lane):
        index = self.LANES.index(lane)
        ref = self.place((self.z + distance) * 2 + (1 - self.x if lane == "x" else self.x))
        return pltpu.make_async_remote_copy(
            src_ref=ref,
            dst_ref=ref,
            send_sem=self.sems.at[0, index, 3],
            recv_sem=self.sems.at[1, index, distance + 3],
            device_id={"dp": self.z * 2 + 1 - self.x},
            device_id_type=MESH,
        )

    def each(self, distance, lanes, act):
        for lane in lanes:
            run = functools.partial(act, self.copy(distance, lane))
            if lane == "up":
                pl.when(self.z < self.last)(run)
            elif lane == "down":
                pl.when(self.z > 0)(run)
            else:
                run()

    def start(self):
        self.each(0, self.LANES, lambda copy: copy.start())

    def hop(self, k):
        @pl.when(self.z >= k)
        def _():
            self.arrival(-k, "up").wait_recv()
            self.each(-k, ("up", "x"), lambda copy: copy.start())

        @pl.when(self.z + k <= self.last)
        def _():
            self.arrival(k, "down").wait_recv()
            self.each(k, ("down", "x"), lambda copy: copy.start())

    def finish(self):
        def close(distance, lanes):
            self.arrival(distance, "x").wait_recv()
            self.each(distance, lanes, lambda copy: copy.wait_send())

        close(0, self.LANES)
        for k in range(1, self.last + 1):
            pl.when(self.z >= k)(functools.partial(close, -k, ("up", "x")))
            pl.when(self.z + k <= self.last)(functools.partial(close, k, ("down", "x")))


def greet():
    me = lax.axis_index("dp")
    z, x = lax.div(me, 2), lax.rem(me, 2)
    last = lax.axis_size("dp") // 2 - 1
    barrier = pltpu.get_barrier_semaphore()

    def signal(to):
        pl.semaphore_signal(barrier, inc=1, device_id={"dp": to}, device_id_type=MESH)

    signal(z * 2 + 1 - x)
    pl.when(z > 0)(lambda: signal((z - 1) * 2 + x))
    pl.when(z < last)(lambda: signal((z + 1) * 2 + x))
    pl.semaphore_wait(barrier, 1 + jnp.minimum(z, 1) + jnp.minimum(last - z, 1))


def lane_of(rows):
    return lax.broadcasted_iota(jnp.int32, (rows, LANES), 1)


def turned(value, cosine, sine_a, sine_b):
    return (
        value * cosine
        + pltpu.roll(value, LANES - ROT // 2, 1) * sine_a
        + pltpu.roll(value, ROT // 2, 1) * sine_b
    )


def norm_step(x, vec):
    mean = jnp.mean(x, 1, keepdims=True)
    shifted = x - mean
    normed = shifted * lax.rsqrt(jnp.mean(shifted * shifted, 1, keepdims=True) + EPSILON)
    return (
        (normed * vec[0:1, :] + vec[1:2, :]).astype(bf16),
        (normed * vec[2:3, :] + vec[3:4, :]).astype(bf16),
    )


def token_tables(seg_ref, cos_ref, sa_ref, sb_ref, key_aug, query_aug):
    segs = seg_ref[...]
    rows = segs.shape[1]
    half = ROT // 2
    position = lax.broadcasted_iota(jnp.int32, (1, rows), 1)
    for c in range(3):
        amount = jnp.sum(jnp.where(segs == c, 1, 0), 1, keepdims=True)
        position = position - jnp.where(segs > c, amount, 0)
    which = lax.broadcasted_iota(jnp.int32, (half, 1), 0)
    rate = jnp.zeros((half, 1), f32)
    for i in range(half):
        rate = jnp.where(which == i, 10000.0 ** (-2.0 * i / ROT), rate)
    angle = rate * position.astype(f32)
    values = jnp.concatenate([jnp.cos(angle), jnp.sin(angle)], 0)
    values = jnp.concatenate([part.astype(f32) for part in pieces(values)], 0).astype(bf16)
    source = lax.broadcasted_iota(jnp.int32, (3 * ROT, LANES), 0) & (ROT - 1)
    spot = lax.broadcasted_iota(jnp.int32, (3 * ROT, LANES), 1) & (HEAD_DIM - 1)
    hit = (spot & (half - 1)) == (source & (half - 1))
    pick = lambda low, high, sine, sign: jnp.where(
        hit & (spot >= low) & (spot < high) & ((source >= half) == sine), sign, 0.0
    ).astype(bf16)
    lane = lane_of(BLOCK) & (HEAD_DIM - 1)
    rest = jnp.where(lane < ROT, 0.0, 1.0)
    kinds = lax.broadcasted_iota(jnp.int32, (8, rows), 0)
    member = jnp.where(kinds == segs, 1.0, 0.0).astype(bf16)
    kind = lax.broadcasted_iota(jnp.int32, (8, LANES), 0)
    where = lax.broadcasted_iota(jnp.int32, (8, LANES), 1) & (HEAD_DIM - 1)
    key_pick = jnp.where((where >= 4) | (where == kind), 1.0, 0.0).astype(bf16)
    query_pick = jnp.where((where < 4) & (where != kind), -FAR, 0.0).astype(bf16)
    cos_pick = pick(0, ROT, False, 1.0)
    sa_pick, sb_pick = pick(0, half, True, -1.0), pick(half, ROT, True, 1.0)
    for part in range(rows // BLOCK):
        span = slice(part * BLOCK, (part + 1) * BLOCK)
        cos_ref[span, :] = dot(values[:, span], cos_pick, ROWS) + rest
        sa_ref[span, :] = dot(values[:, span], sa_pick, ROWS)
        sb_ref[span, :] = dot(values[:, span], sb_pick, ROWS)
        key_aug[span, :] = dot(member[:, span], key_pick, ROWS)
        query_aug[span, :] = dot(member[:, span], query_pick, ROWS)


def front_kernel(linked, *refs):
    (w_in_ref, w_out_ref, x_ref, g_ref, vec_ref, bias_ref, seg_ref,
     w_up_out, w_rest_out, w_attn_out, w_first_out, one_out, two_out, att_out, gq_out,
     master_in, master_out, own_in, own_out, w_attn, w_first, tokens, cot, one, two, gq, att,
     cos_ref, sa_ref, sb_ref, key_aug, query_aug, queries, keys, vals, grads, keys_t, turn,
     load_sem, chunk_sem, store_sem, last_sem, relay_sem) = refs
    rows, width = tokens.shape
    steps = rows // BLOCK
    local = w_attn.shape[2]
    heads = local // HEAD_DIM
    copy = pltpu.make_async_copy
    at = lambda step: pl.ds(pl.multiple_of(step * BLOCK, BLOCK), BLOCK)

    into = (master_in, master_out) if linked else (w_attn, w_first)
    loads = [copy(w_in_ref, into[0], load_sem.at[0]), copy(w_out_ref, into[1], load_sem.at[1])]
    for load in loads:
        load.start()
    load_x = lambda step: copy(x_ref.at[at(step)], tokens.at[at(step)], chunk_sem.at[0, step])
    load_g = lambda step: copy(g_ref.at[at(step)], cot.at[at(step)], chunk_sem.at[1, step])
    for step in range(steps):
        load_x(step).start()
    if linked:
        me = lax.axis_index("dp")
        greet()
        for load in loads:
            load.wait()
        for s in range(own_in.shape[0]):
            own_in[s] = master_in[s].astype(bf16)
        own_out[...] = master_out[...].astype(bf16)
        depth, cols = own_in.shape[1], own_out.shape[1]
        rest = own_out.shape[0] - local
        in_rows = lambda w: pl.ds(pl.multiple_of(w * depth, depth), depth)
        out_cols = lambda w: pl.ds(pl.multiple_of(w * cols, cols), cols)
        relays = [
            Relay(own_in.at[0:3], lambda w: w_attn.at[:, in_rows(w), :], relay_sem.at[0]),
            Relay(own_out.at[0:local], lambda w: w_first.at[:, out_cols(w)], relay_sem.at[1]),
            Relay(own_in.at[3:], lambda w: w_up_out.at[:, in_rows(w), :], relay_sem.at[2]),
            Relay(own_out.at[local:], lambda w: w_rest_out.at[:, out_cols(w)], relay_sem.at[3]),
        ]
        for relay in relays:
            relay.start()
        mine = [
            copy(own_in.at[0:3], w_attn.at[:, in_rows(me), :], load_sem.at[2]),
            copy(own_out.at[0:local], w_first.at[:, out_cols(me)], load_sem.at[3]),
            copy(own_in.at[3:], w_up_out.at[:, in_rows(me), :], load_sem.at[4]),
            copy(own_out.at[local:], w_rest_out.at[:, out_cols(me)], load_sem.at[5]),
        ]
        for part in mine:
            part.start()
    for step in range(steps):
        load_g(step).start()
    token_tables(seg_ref, cos_ref, sa_ref, sb_ref, key_aug, query_aug)

    store_one = lambda step: copy(one.at[at(step)], one_out.at[at(step)], store_sem.at[0, step])
    store_two = lambda step: copy(two.at[at(step)], two_out.at[at(step)], store_sem.at[1, step])

    @pl.loop(0, steps)
    def _(step):
        load_x(step).wait()
        one[at(step), :], two[at(step), :] = norm_step(tokens[at(step), :].astype(f32), vec_ref[...])
        store_one(step).start()
        store_two(step).start()
        if linked:
            for k in (1, 2, 3):
                @pl.when(step == 2 * k)
                def _(k=k):
                    relays[0].hop(k)
                    relays[1].hop(k)

    if linked:
        for part in (0, 1):
            relays[part].finish()
            mine[part].wait()
        away = [copy(w_attn, w_attn_out, last_sem.at[0]), copy(w_first, w_first_out, last_sem.at[1])]
        for part in away:
            part.start()
    else:
        for load in loads:
            load.wait()

    lane = lane_of(BLOCK)
    spot = lane & (HEAD_DIM - 1)
    low = lane < HEAD_DIM
    own_of = (low, lane >= HEAD_DIM)
    line = lambda dim: lax.broadcasted_iota(jnp.int32, (BLOCK, BLOCK), dim)
    load_att = lambda step: copy(att.at[at(step)], att_out.at[at(step)], store_sem.at[2, step])
    load_gq = lambda step: copy(gq.at[1:3, at(step), :], gq_out.at[1:3, at(step), :], store_sem.at[3, step])

    @pl.loop(0, steps)
    def _(step):
        if linked:
            for index, (which, k) in enumerate(((2, 1), (3, 1), (2, 2), (3, 2), (2, 3), (3, 3))):
                pl.when(step == index + 2)(functools.partial(relays[which].hop, k))
        load_g(step).wait()
        row = pl.multiple_of(step * BLOCK, BLOCK)
        mine_rows = pl.ds(row, BLOCK)
        x = one[mine_rows, :]
        proj = [dot(x, w_attn[s]) + bias_ref[s : s + 1, :] for s in range(3)]
        grad_out = dot(cot[mine_rows, :], w_first[...], COLS).astype(bf16).astype(f32)
        tables = cos_ref[mine_rows, :], sa_ref[mine_rows, :], sb_ref[mine_rows, :]
        for tile in range(heads // 2):
            cols = slice(tile * LANES, (tile + 1) * LANES)
            q = turned(proj[0][:, cols], *tables) * QUERY_SCALE
            k = turned(proj[1][:, cols], *tables)
            v = proj[2][:, cols]
            keys_t[cols, mine_rows] = k.astype(bf16).T
            for odd in range(2):
                own = own_of[odd]
                head = 2 * tile + odd
                queries[head, mine_rows, :] = jnp.where(own, q, query_aug[mine_rows, :]).astype(bf16)
                keys[head, mine_rows, :] = jnp.where(own, k, key_aug[mine_rows, :]).astype(bf16)
                vals[head, mine_rows, :] = jnp.where(own, v, 1.0).astype(bf16)

        def attend(blocks):
            for tile in range(heads // 2):
                cols = slice(tile * LANES, (tile + 1) * LANES)
                outs, logs = [], []
                for odd in range(2):
                    head = 2 * tile + odd
                    q = queries[head, mine_rows, :]
                    near = jnp.where(line(0) >= line(1), dot(q, keys[head, mine_rows, :], COLS), -FAR)
                    top = jnp.max(near, 1, keepdims=True)
                    if blocks > 1:
                        span = pl.ds(pl.multiple_of(row - (blocks - 1) * BLOCK, BLOCK), (blocks - 1) * BLOCK)
                        far = dot(q, keys[head, span, :], COLS)
                        top = jnp.maximum(top, jnp.max(far, 1, keepdims=True))
                    out = dot(jnp.exp2(near - top).astype(bf16), vals[head, mine_rows, :])
                    if blocks > 1:
                        out = out + dot(jnp.exp2(far - top).astype(bf16), vals[head, span, :])
                    outs.append(out / pltpu.roll(out, HEAD_DIM, 1))
                    logs.append(top + jnp.log2(out))
                out = jnp.where(low, outs[0], outs[1])
                att[mine_rows, cols] = out.astype(bf16)
                do = grad_out[:, cols]
                both = do * out
                for odd in range(2):
                    own = own_of[odd]
                    head = 2 * tile + odd
                    log_h = logs[odd].astype(bf16).astype(f32)
                    log_m = (logs[odd] - log_h).astype(bf16).astype(f32)
                    log_l = logs[odd] - log_h - log_m
                    parts = jnp.where(spot == 4, log_h, jnp.where(spot == 5, log_m, log_l))
                    taken = (~own) & (spot >= 4) & (spot < 7)
                    queries[head, mine_rows, :] = jnp.where(
                        taken, -parts, queries[head, mine_rows, :].astype(f32)
                    ).astype(bf16)
                    delta = jnp.sum(jnp.where(own, both, 0.0), 1, keepdims=True)
                    delta_h = delta.astype(bf16).astype(f32)
                    delta_m = (delta - delta_h).astype(bf16).astype(f32)
                    delta_l = delta - delta_h - delta_m
                    parts = jnp.where(
                        spot == 0, -delta_h, jnp.where(spot == 1, -delta_m, jnp.where(spot == 2, -delta_l, 0.0))
                    )
                    grads[head, mine_rows, :] = jnp.where(own, do, parts).astype(bf16)

        for blocks in range(1, MOST_BLOCKS + 1):
            pl.when(jnp.minimum(step + 1, MOST_BLOCKS) == blocks)(functools.partial(attend, blocks))
        load_att(step).start()

    turn[...] = jnp.zeros_like(turn)

    @pl.loop(0, steps)
    def _(back):
        step = steps - 1 - back
        row = pl.multiple_of(step * BLOCK, BLOCK)
        mine_rows = pl.ds(row, BLOCK)
        tables = cos_ref[mine_rows, :], -sa_ref[mine_rows, :], -sb_ref[mine_rows, :]

        def attend(blocks):
            for tile in range(heads // 2):
                cols = slice(tile * LANES, (tile + 1) * LANES)
                results = []
                for odd in range(2):
                    head = 2 * tile + odd
                    turn_rows = slice(head * HEAD_DIM, (head + 1) * HEAD_DIM)
                    total = None
                    for first, size in ((0, 1), (1, blocks - 1)):
                        if size == 0:
                            continue
                        span = pl.ds(pl.multiple_of(row + first * BLOCK, BLOCK), size * BLOCK)
                        q, do = queries[head, span, :], grads[head, span, :]
                        p = jnp.exp2(dot(keys[head, mine_rows, :], q, COLS))
                        if first == 0:
                            p = jnp.where(line(0) <= line(1), p, 0.0)
                        ds = (p * dot(vals[head, mine_rows, :], do, COLS)).astype(bf16)
                        part = dot(ds, q), dot(p.astype(bf16), do)
                        total = part if total is None else (total[0] + part[0], total[1] + part[1])
                        turn[turn_rows, span] += dot(keys_t[turn_rows, mine_rows], ds)
                    results.append(total)
                dk = jnp.where(low, results[0][0], results[1][0]) * LN2
                gq[1, mine_rows, cols] = turned(dk, *tables).astype(bf16)
                gq[2, mine_rows, cols] = jnp.where(low, results[0][1], results[1][1]).astype(bf16)

        for blocks in range(1, MOST_BLOCKS + 1):
            pl.when(jnp.minimum(back + 1, MOST_BLOCKS) == blocks)(functools.partial(attend, blocks))
        load_gq(step).start()

    @pl.loop(0, steps)
    def _(step):
        mine_rows = at(step)
        for tile in range(heads // 2):
            cols = slice(tile * LANES, (tile + 1) * LANES)
            dq = turn[cols, mine_rows].T * 0.125
            gq[0, mine_rows, cols] = turned(
                dq, cos_ref[mine_rows, :], -sa_ref[mine_rows, :], -sb_ref[mine_rows, :]
            ).astype(bf16)

    final = copy(gq.at[0], gq_out.at[0], last_sem.at[2])
    final.start()
    if linked:
        for part in (2, 3):
            relays[part].finish()
            mine[part].wait()
        for part in away:
            part.wait()

    @pl.loop(0, steps)
    def _(step):
        for store in (store_one, store_two, load_att, load_gq):
            store(step).wait()

    final.wait()


def front(linked, w_in, w_out, tokens, cot, vec, bias, segments):
    rows, width = tokens.shape
    local = bias.shape[1]
    heads = local // HEAD_DIM
    steps = rows // BLOCK
    anywhere = pl.BlockSpec(memory_space=pl.ANY)
    vmem = pl.BlockSpec(memory_space=pltpu.VMEM)
    shape = jax.ShapeDtypeStruct
    tiny = (16, LANES)
    gathered_shapes = [
        shape((4, width, local) if linked else tiny, bf16),
        shape((4 * local, width) if linked else tiny, bf16),
        shape((3, width, local) if linked else tiny, bf16),
        shape((local, width) if linked else tiny, bf16),
    ]
    masters = [w_in.shape, w_out.shape] if linked else [tiny, tiny]
    owns = [w_in.shape, w_out.shape] if linked else [tiny, tiny]
    return pl.pallas_call(
        functools.partial(front_kernel, linked),
        in_specs=[anywhere] * 4 + [vmem] * 3,
        out_specs=[anywhere] * 8,
        out_shape=gathered_shapes + [
            shape((rows, width), bf16), shape((rows, width), bf16),
            shape((rows, local), bf16), shape((3, rows, local), bf16),
        ],
        scratch_shapes=[
            pltpu.VMEM(masters[0], f32), pltpu.VMEM(masters[1], f32),
            pltpu.VMEM(owns[0], bf16), pltpu.VMEM(owns[1], bf16),
            pltpu.VMEM((3, width, local), bf16), pltpu.VMEM((local, width), bf16),
            pltpu.VMEM((rows, width), bf16), pltpu.VMEM((rows, width), bf16),
            pltpu.VMEM((rows, width), bf16), pltpu.VMEM((rows, width), bf16),
            pltpu.VMEM((3, rows, local), bf16), pltpu.VMEM((rows, local), bf16),
            pltpu.VMEM((rows, LANES), f32), pltpu.VMEM((rows, LANES), f32), pltpu.VMEM((rows, LANES), f32),
            pltpu.VMEM((rows, LANES), f32), pltpu.VMEM((rows, LANES), f32),
            pltpu.VMEM((heads, rows, LANES), bf16), pltpu.VMEM((heads, rows, LANES), bf16),
            pltpu.VMEM((heads, rows, LANES), bf16), pltpu.VMEM((heads, rows, LANES), bf16),
            pltpu.VMEM((local, rows), bf16), pltpu.VMEM((local, rows), f32),
            pltpu.SemaphoreType.DMA((6,)), pltpu.SemaphoreType.DMA((2, steps)),
            pltpu.SemaphoreType.DMA((4, steps)), pltpu.SemaphoreType.DMA((3,)),
            pltpu.SemaphoreType.DMA((4, 2, 3, 7)),
        ],
        compiler_params=params(collective_id=0, has_side_effects=True) if linked else params(),
        name="front",
    )(w_in, w_out, tokens, cot, vec, bias, segments)


def normal_cdf(value):
    bell = jnp.exp2(value * value * (-0.5 * LOG2E))
    t = 1.0 / (1.0 + (0.3275911 / 1.4142135623730951) * jnp.abs(value))
    poly = 0.5 * 1.061405429
    for coefficient in (-1.453152027, 1.421413741, -0.284496736, 0.254829592):
        poly = poly * t + 0.5 * coefficient
    tail = poly * t * bell
    return jnp.where(value >= 0.0, 1.0 - tail, tail), bell


def feed_kernel(x_ref, g_ref, att_ref, wu_ref, wf_ref, wr_ref, bias_ref, part_ref, gup_ref, hidden_ref):
    x, g = x_ref[...], g_ref[...]
    slots, _, local = wu_ref.shape
    branch = dot(att_ref[...], wf_ref[...])
    for s in range(slots):
        w_rows = slice(s * local, (s + 1) * local)
        up = dot(x, wu_ref[s]) + bias_ref[3 + s : 4 + s, :]
        grad_hidden = dot(g, wr_ref[w_rows, :], COLS)
        cdf, bell = normal_cdf(up)
        hidden = (up * cdf).astype(bf16)
        gup_ref[s] = (grad_hidden * (cdf + up * bell * 0.3989422804014327)).astype(bf16)
        hidden_ref[s] = hidden
        branch = branch + dot(hidden, wr_ref[w_rows, :])
    for c in range(part_ref.shape[0]):
        part_ref[c] = branch[:, c * local : (c + 1) * local].astype(bf16)


def feed(norm_two, cot, att, w_up, w_first, w_rest, bias):
    rows, width = cot.shape
    slots, _, local = w_up.shape
    share = width // local
    size = 2 * BLOCK
    block = lambda cols: pl.BlockSpec((size, cols), lambda i: (i, 0))
    slotted = lambda count: pl.BlockSpec((count, size, local), lambda i: (0, i, 0))
    return pl.pallas_call(
        feed_kernel,
        grid=(rows // size,),
        in_specs=[
            block(width), block(width), block(local), full(w_up.shape), full(w_first.shape),
            full(w_rest.shape), full(bias.shape),
        ],
        out_specs=[slotted(share), slotted(slots), slotted(slots)],
        out_shape=[
            jax.ShapeDtypeStruct((share, rows, local), bf16),
            jax.ShapeDtypeStruct((slots, rows, local), bf16),
            jax.ShapeDtypeStruct((slots, rows, local), bf16),
        ],
        compiler_params=params(),
        cost_estimate=pl.CostEstimate(
            flops=2 * rows * width * local * 13, bytes_accessed=16 * rows * width,
            transcendentals=rows * width * 2,
        ),
        name="feed",
    )(norm_two, cot, att, w_up, w_first, w_rest, bias)


def norm_grad_kernel(
    gq_ref, gu_ref, wa_ref, wu_ref, x_ref, vec_ref,
    part_ref, sum_ref, dot_ref, mean_ref, rstd_ref, vec_grad_ref,
):
    @pl.when(pl.program_id(0) == 0)
    def _():
        vec_grad_ref[...] = jnp.zeros_like(vec_grad_ref)

    x = x_ref[...].astype(f32)
    mean = jnp.mean(x, 1, keepdims=True)
    shifted = x - mean
    rstd = lax.rsqrt(jnp.mean(shifted * shifted, 1, keepdims=True) + EPSILON)
    normed = shifted * rstd
    mean_ref[...], rstd_ref[...] = mean, rstd
    local = gq_ref.shape[2]
    sums = dots = 0.0
    for c in range(part_ref.shape[0]):
        cols = slice(c * local, (c + 1) * local)
        one = sum(dot(gq_ref[s], wa_ref[s, cols, :], COLS) for s in range(gq_ref.shape[0]))
        two = sum(dot(gu_ref[s], wu_ref[s, cols, :], COLS) for s in range(gu_ref.shape[0]))
        scaled = one * vec_ref[0:1, cols] + two * vec_ref[2:3, cols]
        part_ref[c] = scaled.astype(bf16)
        sums = sums + jnp.sum(scaled, 1, keepdims=True)
        dots = dots + jnp.sum(scaled * normed[:, cols], 1, keepdims=True)
        vec_grad_ref[0:1, cols] += jnp.sum(one * normed[:, cols], 0, keepdims=True)
        vec_grad_ref[1:2, cols] += jnp.sum(one, 0, keepdims=True)
        vec_grad_ref[2:3, cols] += jnp.sum(two * normed[:, cols], 0, keepdims=True)
        vec_grad_ref[3:4, cols] += jnp.sum(two, 0, keepdims=True)
    sum_ref[...] = sums
    dot_ref[...] = dots


def norm_grad(grad_qkv, grad_up, w_attn, w_up, tokens, vec):
    rows, width = tokens.shape
    local = w_up.shape[2]
    share = width // local
    size = 2 * BLOCK
    block = lambda cols: pl.BlockSpec((size, cols), lambda i: (i, 0))
    slotted = lambda slots: pl.BlockSpec((slots, size, local), lambda i: (0, i, 0))
    return pl.pallas_call(
        norm_grad_kernel,
        grid=(rows // size,),
        in_specs=[
            slotted(3), slotted(w_up.shape[0]), full(w_attn.shape), full(w_up.shape),
            block(width), full(vec.shape),
        ],
        out_specs=[slotted(share)] + [block(1)] * 4 + [full((8, width))],
        out_shape=[jax.ShapeDtypeStruct((share, rows, local), bf16)]
        + [jax.ShapeDtypeStruct((rows, 1), f32)] * 4
        + [
            jax.ShapeDtypeStruct((8, width), f32),
        ],
        compiler_params=params(),
        cost_estimate=pl.CostEstimate(
            flops=2 * rows * width * local * 7, bytes_accessed=8 * rows * width, transcendentals=0
        ),
        name="norm_grad",
    )(grad_qkv, grad_up, w_attn, w_up, tokens, vec)


def two_parts(value, high_ref, low_ref):
    high = value.astype(bf16)
    low = (value - high.astype(f32)).astype(bf16)
    high_ref[0], low_ref[0] = high, low
    return high, low


def clear_first(*refs):
    @pl.when(pl.program_id(0) == 0)
    def _():
        for ref in refs:
            ref[...] = jnp.zeros_like(ref)


def matrix_in_kernel(one_ref, two_ref, gq_ref, gu_ref, e_ref, q_ref, high_ref, low_ref, left_ref, bias_ref):
    clear_first(left_ref)
    slot = pl.program_id(0)

    def run(x_ref, grad_ref):
        grad = grad_ref[0]
        high, low = two_parts(dot(x_ref[...], grad, ROWS) + e_ref[0], high_ref, low_ref)
        q = stacked(q_ref[0])
        left_ref[...] += folded(dot(q, high, COLS)) + folded(dot(q, low, COLS))
        bias_ref[0] = jnp.sum(grad.astype(f32), 0, keepdims=True)

    pl.when(slot < 3)(lambda: run(one_ref, gq_ref))
    pl.when(slot >= 3)(lambda: run(two_ref, gu_ref))


def matrix_out_kernel(att_ref, hid_ref, g_ref, e_ref, q_ref, high_ref, low_ref, left_ref):
    clear_first(left_ref)
    slot = pl.program_id(0)

    def run(mixed):
        high, low = two_parts(dot(mixed, g_ref[...], ROWS) + e_ref[0], high_ref, low_ref)
        q = stacked(q_ref[0])
        left_ref[...] += folded(dot(q, high)) + folded(dot(q, low))

    pl.when(slot < 1)(lambda: run(att_ref[...]))
    pl.when(slot >= 1)(lambda: run(hid_ref[0]))


def slot_spec(shape, index=lambda i: i):
    return pl.BlockSpec((1,) + tuple(shape[1:]), lambda i: (index(i), 0, 0))


def matrix_in(norm_one, norm_two, grad_qkv, grad_up, error, q):
    slots, width, local = error.shape
    rows = norm_one.shape[0]
    big = jax.ShapeDtypeStruct(error.shape, bf16)
    return pl.pallas_call(
        matrix_in_kernel,
        grid=(slots,),
        in_specs=[
            full(norm_one.shape), full(norm_two.shape),
            slot_spec(grad_qkv.shape, lambda i: jnp.minimum(i, 2)),
            slot_spec(grad_up.shape, lambda i: jnp.maximum(i - 3, 0)),
            slot_spec(error.shape), slot_spec(q.shape),
        ],
        out_specs=[slot_spec(error.shape), slot_spec(error.shape), full((8, width)), slot_spec((slots, 1, local))],
        out_shape=[big, big, jax.ShapeDtypeStruct((8, width), f32), jax.ShapeDtypeStruct((slots, 1, local), f32)],
        compiler_params=params(),
        cost_estimate=pl.CostEstimate(
            flops=2 * slots * rows * width * local, bytes_accessed=10 * error.size, transcendentals=0
        ),
        name="matrix_in",
    )(norm_one, norm_two, grad_qkv, grad_up, error, q)


def matrix_out(att, hidden, cot, error, q):
    slots, local, width = error.shape
    rows = cot.shape[0]
    big = jax.ShapeDtypeStruct(error.shape, bf16)
    return pl.pallas_call(
        matrix_out_kernel,
        grid=(slots,),
        in_specs=[
            full(att.shape), slot_spec(hidden.shape, lambda i: jnp.maximum(i - 1, 0)), full(cot.shape),
            slot_spec(error.shape), slot_spec(q.shape),
        ],
        out_specs=[slot_spec(error.shape), slot_spec(error.shape), full((8, width))],
        out_shape=[big, big, jax.ShapeDtypeStruct((8, width), f32)],
        compiler_params=params(),
        cost_estimate=pl.CostEstimate(
            flops=2 * slots * rows * width * local, bytes_accessed=10 * error.size, transcendentals=0
        ),
        name="matrix_out",
    )(att, hidden, cot, error, q)


def orthonormal_rows(matrix):
    index = lax.broadcasted_iota(jnp.int32, (matrix.shape[0], 1), 0)
    for r in range(matrix.shape[0]):
        row = matrix[r : r + 1, :]
        row = row * lax.rsqrt(jnp.sum(row * row, 1, keepdims=True) + 1e-06)
        along = jnp.sum(matrix * row, 1, keepdims=True)
        matrix = jnp.where(index == r, row, jnp.where(index > r, matrix - along * row, matrix))
    return matrix


def basis_kernel(left_in_ref, left_out_ref, basis_in_ref, basis_out_ref):
    basis_in_ref[...] = orthonormal_rows(left_in_ref[...])
    basis_out_ref[...] = orthonormal_rows(left_out_ref[...])


def bases(left_in, left_out):
    shape = jax.ShapeDtypeStruct(left_in.shape, f32)
    return pl.pallas_call(
        basis_kernel, out_shape=[shape, shape], compiler_params=params(), name="bases"
    )(left_in, left_out)


def right_kernel(dims, basis_ref, high_ref, low_ref, out_ref):
    basis = stacked(basis_ref[...])
    out_ref[0] = folded(dot(basis, high_ref[0], dims)) + folded(dot(basis, low_ref[0], dims))


def right_factor(basis, matrix, dims, columns):
    slots = matrix[0].shape[0]
    return pl.pallas_call(
        functools.partial(right_kernel, dims),
        grid=(slots,),
        in_specs=[full(basis.shape), slot_spec(matrix[0].shape), slot_spec(matrix[1].shape)],
        out_specs=pl.BlockSpec((1, 8, columns), lambda i: (i, 0, 0)),
        out_shape=jax.ShapeDtypeStruct((slots, 8, columns), f32),
        compiler_params=params(),
        cost_estimate=pl.CostEstimate(flops=0, bytes_accessed=matrix[0].size * 4, transcendentals=0),
        name="right_factor",
    )(basis, *matrix)


def outer(a, b):
    ah, am, al = (part.astype(f32) for part in pieces(a))
    bh, bm, bl = (part.astype(f32) for part in pieces(b))
    left = jnp.concatenate([ah, ah, am, ah, am, al], 0).astype(bf16)
    right = jnp.concatenate([bh, bm, bh, bl, bm, bh], 0).astype(bf16)
    return dot(left, right, ROWS)


def finish_kernel(swap, basis_ref, own_ref, right_ref, high_ref, low_ref, mom_ref, w_ref, error_ref, new_mom_ref, new_w_ref):
    pair = lambda a, b: outer(b, a) if swap else outer(a, b)
    error_ref[0] = high_ref[0].astype(f32) + low_ref[0].astype(f32) - pair(basis_ref[...], right_ref[0])
    mom = MOMENTUM_DECAY * mom_ref[0] + pair(own_ref[...], right_ref[0])
    new_mom_ref[0] = mom
    new_w_ref[0] = w_ref[0] - LEARN_RATE * mom


def finish(swap, basis, own, right, matrix, mom, master):
    slots = right.shape[0]
    spec = lambda a: pl.BlockSpec((1,) + a.shape[1:], lambda i: (i, 0, 0))
    return pl.pallas_call(
        functools.partial(finish_kernel, swap),
        grid=(slots,),
        in_specs=[full(basis.shape), full(own.shape), spec(right), spec(matrix[0]), spec(matrix[1]), spec(mom), spec(master)],
        out_specs=[spec(matrix[0]), spec(mom), spec(master)],
        out_shape=[jax.ShapeDtypeStruct(a.shape, f32) for a in (matrix[0], mom, master)],
        compiler_params=params(),
        cost_estimate=pl.CostEstimate(flops=0, bytes_accessed=matrix[0].size * 10, transcendentals=0),
        name="finish",
    )(basis, own, right, *matrix, mom, master)


def swapped(value, axis, bits):
    size = lax.axis_size(axis)
    return lax.ppermute(value, axis, [(i, i ^ bits) for i in range(size)])


def summed(value):
    if lax.axis_size("dp") != 8:
        return lax.psum(value, "dp")
    value = value + swapped(value, "dp", 1)
    near, far, last = (swapped(value, "dp", bits) for bits in (2, 4, 6))
    return (value + near) + (far + last)


def scattered(parts):
    count = lax.axis_size("tensor")
    me = lax.axis_index("tensor")
    if count != 4:
        return lax.psum_scatter(parts, "tensor", scatter_dimension=0, tiled=False).astype(f32)
    core = me % 2
    pairs = parts.reshape(2, 2, *parts.shape[1:])
    away = lax.dynamic_index_in_dim(pairs, 1 - core, 1, keepdims=False)
    here = lax.dynamic_index_in_dim(pairs, core, 1, keepdims=False)
    near = here.astype(f32) + swapped(away, "tensor", 1).astype(f32)
    chip = me // 2
    send = lax.dynamic_index_in_dim(near, 1 - chip, 0, keepdims=False).astype(bf16)
    keep = lax.dynamic_index_in_dim(near, chip, 0, keepdims=False)
    return keep + swapped(send, "tensor", 2).astype(f32)


def on_device(
    tokens, cotangent, segments, w_in_master, w_out_master, vec_master, bias_in_master,
    w_in_mom, w_out_mom, vec_mom, bias_in_mom, w_in_error, w_out_error, q_in, q_out,
):
    workers = lax.axis_size("dp")
    tensor_index = lax.axis_index("tensor")
    worker_index = lax.axis_index("dp")
    rows, width = tokens.shape
    local = bias_in_master.shape[1]
    start_col = tensor_index * local
    cut = lambda a: lax.dynamic_slice_in_dim(a, start_col, local, 1)

    w_in = w_in_master.transpose(1, 0, 2)
    linked = workers == 8
    if linked:
        shards = w_in, w_out_master.reshape(5 * local, -1)
    else:
        w_in_low = lax.all_gather(w_in.astype(bf16), "dp", axis=1, tiled=True)
        w_out_low = lax.all_gather(w_out_master.astype(bf16), "dp", axis=2, tiled=True)
        shards = w_in_low[:3], w_out_low[0]
    w_up, w_rest, w_attn, w_first, norm_one, norm_two, att, grad_qkv = front(
        linked, *shards, tokens, cotangent, vec_master, bias_in_master, segments
    )
    if not linked:
        w_attn, w_first = shards
        w_up, w_rest = w_in_low[3:], w_out_low[1:].reshape(4 * local, width)

    factors_in, factors_out = q_in.transpose(0, 2, 1), q_out.transpose(0, 2, 1)
    error_in = w_in_error[0].transpose(1, 0, 2)
    error_out = w_out_error[0]
    branch_parts, grad_up, hidden = feed(norm_two, cotangent, att, w_up, w_first, w_rest, bias_in_master)
    *matrix_out_parts, left_out = matrix_out(att, hidden, cotangent, error_out, factors_out)
    *matrix_in_parts, left_in, bias_local = matrix_in(
        norm_one, norm_two, grad_qkv, grad_up, error_in, factors_in
    )
    left = summed(jnp.concatenate([left_in, left_out], 0)) / workers
    grad_parts, row_sum, row_dot, mean, rstd, vec_local = norm_grad(
        grad_qkv, grad_up, w_attn, w_up, tokens, vec_master
    )
    basis_in, basis_out = bases(left[:8], left[8:])
    right_in = right_factor(basis_in, matrix_in_parts, PLAIN, local)
    right_out = right_factor(basis_out, matrix_out_parts, COLS, local)

    cot_cols = cut(cotangent).astype(f32)
    bias_local = bias_local[:, 0, :]
    vec_rows = lax.psum_scatter(
        vec_local[:4].reshape(4, -1, local), "tensor", scatter_dimension=1, tiled=False
    )
    vec_rows = jnp.concatenate([vec_rows, jnp.sum(cot_cols, 0)[None]], 0)
    sizes = [7 * 8, 5 * 8, 5, 7]
    bundle = summed(
        jnp.concatenate(
            [
                right_in.reshape(-1, local), right_out.reshape(-1, local), vec_rows, bias_local,
            ],
            0,
        )
    ) / workers
    cuts = [0]
    for size in sizes:
        cuts.append(cuts[-1] + size)
    right_in = bundle[cuts[0] : cuts[1]].reshape(7, 8, local)
    right_out = bundle[cuts[1] : cuts[2]].reshape(5, 8, local)
    vec_grad, bias_grad = bundle[cuts[2] : cuts[3]], bundle[cuts[3] : cuts[4]]

    owned = w_in_master.shape[0]
    own_in = lax.dynamic_slice_in_dim(basis_in, worker_index * owned, owned, 1)
    own_out = lax.dynamic_slice_in_dim(basis_out, worker_index * owned, owned, 1)
    w_in_mom = w_in_mom.transpose(1, 0, 2)
    new_error_in, new_mom_in, new_w_in = finish(
        False, basis_in, own_in, right_in, matrix_in_parts, w_in_mom, w_in
    )
    new_error_out, new_mom_out, new_w_out = finish(
        True, basis_out, own_out, right_out, matrix_out_parts, w_out_mom, w_out_master
    )

    vec_mom_new = MOMENTUM_DECAY * vec_mom + vec_grad
    vec_new = cut(vec_master) - VECTOR_RATE * vec_mom_new
    bias_in_mom_new = MOMENTUM_DECAY * bias_in_mom + bias_grad
    bias_in_new = bias_in_master - VECTOR_RATE * bias_in_mom_new

    token_cols = cut(tokens).astype(f32)
    block_out = (token_cols + scattered(branch_parts) + cut(vec_master)[4:5]).astype(bf16)
    row_means = lax.psum(jnp.concatenate([row_sum, row_dot], 1), "tensor") / width
    normed_cols = (token_cols - mean) * rstd
    input_grad = cot_cols + rstd * (
        scattered(grad_parts) - row_means[:, 0:1] - normed_cols * row_means[:, 1:2]
    )
    return (
        block_out,
        input_grad,
        new_w_in.transpose(1, 0, 2),
        new_w_out,
        vec_new,
        bias_in_new,
        new_mom_in.transpose(1, 0, 2),
        new_mom_out,
        vec_mom_new,
        bias_in_mom_new,
        new_error_in.transpose(1, 0, 2)[None],
        new_error_out[None],
        right_in.transpose(0, 2, 1),
        right_out.transpose(0, 2, 1),
    )


def solution(mesh):
    return jax.shard_map(
        on_device,
        mesh=mesh,
        in_specs=(
            P("dp", None), P("dp", None), P("dp", None), P("dp", None, "tensor"),
            P(None, "tensor", "dp"), P(), P(None, "tensor"), P("dp", None, "tensor"),
            P(None, "tensor", "dp"), P(None, "tensor"), P(None, "tensor"),
            P("dp", None, None, "tensor"), P("dp", None, "tensor", None),
            P(None, "tensor", None), P(None, "tensor", None),
        ),
        out_specs=(
            P("dp", "tensor"), P("dp", "tensor"), P("dp", None, "tensor"), P(None, "tensor", "dp"),
            P(None, "tensor"), P(None, "tensor"), P("dp", None, "tensor"), P(None, "tensor", "dp"),
            P(None, "tensor"), P(None, "tensor"), P("dp", None, None, "tensor"),
            P("dp", None, "tensor", None), P(None, "tensor", None), P(None, "tensor", None),
        ),
        check_vma=False,
    )
```

```python
import functools

import jax
import jax.numpy as jnp
from jax import lax
from jax.experimental import pallas as pl
from jax.experimental.pallas import tpu as pltpu
from jax.sharding import PartitionSpec as P

HEAD_DIM = 64
ROT = 16
EPSILON = 1e-05
MOMENTUM_DECAY = 0.9
LEARN_RATE = 0.05
VECTOR_RATE = 0.05
LN2 = 0.6931471805599453
LOG2E = 1.4426950408889634
QUERY_SCALE = 0.125 * LOG2E
FAR = 2.0**30
BLOCK = 256
LANES = 128
MOST_BLOCKS = 5

f32 = jnp.float32
bf16 = jnp.bfloat16
ROWS = (((0,), (0,)), ((), ()))
COLS = (((1,), (1,)), ((), ()))
PLAIN = (((1,), (0,)), ((), ()))
MESH = pl.DeviceIdType.MESH


def dot(a, b, dims=PLAIN):
    return lax.dot_general(a, b, dims, preferred_element_type=f32)


def params(**more):
    return pltpu.CompilerParams(vmem_limit_bytes=56 * 1024 * 1024, **more)


def pieces(value):
    high = value.astype(bf16)
    rest = value - high.astype(f32)
    middle = rest.astype(bf16)
    low = (rest - middle.astype(f32)).astype(bf16)
    return high, middle, low


def stacked(value):
    return jnp.concatenate([part.astype(f32) for part in pieces(value)], 0).astype(bf16)


def folded(total, rows=8):
    return total[:rows] + total[rows : 2 * rows] + total[2 * rows : 3 * rows]


def full(shape):
    return pl.BlockSpec(shape, lambda i: (0,) * len(shape))


class Relay:
    LANES = ("up", "down", "x")

    def __init__(self, own, place, sems):
        self.own, self.place, self.sems = own, place, sems
        me = lax.axis_index("dp")
        self.z, self.x = lax.div(me, 2), lax.rem(me, 2)
        self.last = lax.axis_size("dp") // 2 - 1

    def copy(self, distance, lane):
        index = self.LANES.index(lane)
        step = (1, -1, 0)[index]
        worker = (self.z + distance) * 2 + self.x
        to = (self.z + step) * 2 + (1 - self.x if lane == "x" else self.x)
        return pltpu.make_async_remote_copy(
            src_ref=self.own if distance == 0 else self.place(worker),
            dst_ref=self.place(worker),
            send_sem=self.sems.at[0, index, distance + 3],
            recv_sem=self.sems.at[1, index, distance - step + 3],
            device_id={"dp": to},
            device_id_type=MESH,
        )

    def arrival(self, distance, lane):
        index = self.LANES.index(lane)
        ref = self.place((self.z + distance) * 2 + (1 - self.x if lane == "x" else self.x))
        return pltpu.make_async_remote_copy(
            src_ref=ref,
            dst_ref=ref,
            send_sem=self.sems.at[0, index, 3],
            recv_sem=self.sems.at[1, index, distance + 3],
            device_id={"dp": self.z * 2 + 1 - self.x},
            device_id_type=MESH,
        )

    def each(self, distance, lanes, act):
        for lane in lanes:
            run = functools.partial(act, self.copy(distance, lane))
            if lane == "up":
                pl.when(self.z < self.last)(run)
            elif lane == "down":
                pl.when(self.z > 0)(run)
            else:
                run()

    def start(self):
        self.each(0, self.LANES, lambda copy: copy.start())

    def hop(self, k):
        @pl.when(self.z >= k)
        def _():
            self.arrival(-k, "up").wait_recv()
            self.each(-k, ("up", "x"), lambda copy: copy.start())

        @pl.when(self.z + k <= self.last)
        def _():
            self.arrival(k, "down").wait_recv()
            self.each(k, ("down", "x"), lambda copy: copy.start())

    def finish(self):
        def close(distance, lanes):
            self.arrival(distance, "x").wait_recv()
            self.each(distance, lanes, lambda copy: copy.wait_send())

        close(0, self.LANES)
        for k in range(1, self.last + 1):
            pl.when(self.z >= k)(functools.partial(close, -k, ("up", "x")))
            pl.when(self.z + k <= self.last)(functools.partial(close, k, ("down", "x")))


def greet():
    me = lax.axis_index("dp")
    z, x = lax.div(me, 2), lax.rem(me, 2)
    last = lax.axis_size("dp") // 2 - 1
    barrier = pltpu.get_barrier_semaphore()

    def signal(to):
        pl.semaphore_signal(barrier, inc=1, device_id={"dp": to}, device_id_type=MESH)

    signal(z * 2 + 1 - x)
    pl.when(z > 0)(lambda: signal((z - 1) * 2 + x))
    pl.when(z < last)(lambda: signal((z + 1) * 2 + x))
    pl.semaphore_wait(barrier, 1 + jnp.minimum(z, 1) + jnp.minimum(last - z, 1))


def lane_of(rows):
    return lax.broadcasted_iota(jnp.int32, (rows, LANES), 1)


def turned(value, cosine, sine_a, sine_b):
    return (
        value * cosine
        + pltpu.roll(value, LANES - ROT // 2, 1) * sine_a
        + pltpu.roll(value, ROT // 2, 1) * sine_b
    )


def norm_step(x, vec):
    mean = jnp.mean(x, 1, keepdims=True)
    shifted = x - mean
    normed = shifted * lax.rsqrt(jnp.mean(shifted * shifted, 1, keepdims=True) + EPSILON)
    return (
        (normed * vec[0:1, :] + vec[1:2, :]).astype(bf16),
        (normed * vec[2:3, :] + vec[3:4, :]).astype(bf16),
    )


def token_tables(seg_ref, cos_ref, sa_ref, sb_ref, key_aug, query_aug):
    segs = seg_ref[...]
    rows = segs.shape[1]
    half = ROT // 2
    position = lax.broadcasted_iota(jnp.int32, (1, rows), 1)
    for c in range(3):
        amount = jnp.sum(jnp.where(segs == c, 1, 0), 1, keepdims=True)
        position = position - jnp.where(segs > c, amount, 0)
    which = lax.broadcasted_iota(jnp.int32, (half, 1), 0)
    rate = jnp.zeros((half, 1), f32)
    for i in range(half):
        rate = jnp.where(which == i, 10000.0 ** (-2.0 * i / ROT), rate)
    angle = rate * position.astype(f32)
    values = jnp.concatenate([jnp.cos(angle), jnp.sin(angle)], 0)
    values = jnp.concatenate([part.astype(f32) for part in pieces(values)], 0).astype(bf16)
    source = lax.broadcasted_iota(jnp.int32, (3 * ROT, LANES), 0) & (ROT - 1)
    spot = lax.broadcasted_iota(jnp.int32, (3 * ROT, LANES), 1) & (HEAD_DIM - 1)
    hit = (spot & (half - 1)) == (source & (half - 1))
    pick = lambda low, high, sine, sign: jnp.where(
        hit & (spot >= low) & (spot < high) & ((source >= half) == sine), sign, 0.0
    ).astype(bf16)
    lane = lane_of(BLOCK) & (HEAD_DIM - 1)
    rest = jnp.where(lane < ROT, 0.0, 1.0)
    kinds = lax.broadcasted_iota(jnp.int32, (8, rows), 0)
    member = jnp.where(kinds == segs, 1.0, 0.0).astype(bf16)
    kind = lax.broadcasted_iota(jnp.int32, (8, LANES), 0)
    where = lax.broadcasted_iota(jnp.int32, (8, LANES), 1) & (HEAD_DIM - 1)
    key_pick = jnp.where((where >= 4) | (where == kind), 1.0, 0.0).astype(bf16)
    query_pick = jnp.where((where < 4) & (where != kind), -FAR, 0.0).astype(bf16)
    cos_pick = pick(0, ROT, False, 1.0)
    sa_pick, sb_pick = pick(0, half, True, -1.0), pick(half, ROT, True, 1.0)
    for part in range(rows // BLOCK):
        span = slice(part * BLOCK, (part + 1) * BLOCK)
        cos_ref[span, :] = dot(values[:, span], cos_pick, ROWS) + rest
        sa_ref[span, :] = dot(values[:, span], sa_pick, ROWS)
        sb_ref[span, :] = dot(values[:, span], sb_pick, ROWS)
        key_aug[span, :] = dot(member[:, span], key_pick, ROWS)
        query_aug[span, :] = dot(member[:, span], query_pick, ROWS)


def front_kernel(linked, *refs):
    (w_in_ref, w_out_ref, x_ref, g_ref, vec_ref, bias_ref, seg_ref,
     w_up_out, w_rest_out, w_attn_out, w_first_out, one_out, two_out, att_out, gq_out,
     master_in, master_out, own_in, own_out, w_attn, w_first, tokens, cot, one, two, gq, att,
     cos_ref, sa_ref, sb_ref, key_aug, query_aug, queries, keys, vals, grads, keys_t, turn,
     load_sem, chunk_sem, store_sem, last_sem, relay_sem) = refs
    rows, width = tokens.shape
    steps = rows // BLOCK
    local = w_attn.shape[2]
    heads = local // HEAD_DIM
    copy = pltpu.make_async_copy
    at = lambda step: pl.ds(pl.multiple_of(step * BLOCK, BLOCK), BLOCK)

    into = (master_in, master_out) if linked else (w_attn, w_first)
    loads = [copy(w_in_ref, into[0], load_sem.at[0]), copy(w_out_ref, into[1], load_sem.at[1])]
    for load in loads:
        load.start()
    load_x = lambda step: copy(x_ref.at[at(step)], tokens.at[at(step)], chunk_sem.at[0, step])
    load_g = lambda step: copy(g_ref.at[at(step)], cot.at[at(step)], chunk_sem.at[1, step])
    for step in range(steps):
        load_x(step).start()
    if linked:
        me = lax.axis_index("dp")
        greet()
        for load in loads:
            load.wait()
        for s in range(own_in.shape[0]):
            own_in[s] = master_in[s].astype(bf16)
        own_out[...] = master_out[...].astype(bf16)
        depth, cols = own_in.shape[1], own_out.shape[1]
        rest = own_out.shape[0] - local
        in_rows = lambda w: pl.ds(pl.multiple_of(w * depth, depth), depth)
        out_cols = lambda w: pl.ds(pl.multiple_of(w * cols, cols), cols)
        relays = [
            Relay(own_in.at[0:3], lambda w: w_attn.at[:, in_rows(w), :], relay_sem.at[0]),
            Relay(own_out.at[0:local], lambda w: w_first.at[:, out_cols(w)], relay_sem.at[1]),
            Relay(own_in.at[3:], lambda w: w_up_out.at[:, in_rows(w), :], relay_sem.at[2]),
            Relay(own_out.at[local:], lambda w: w_rest_out.at[:, out_cols(w)], relay_sem.at[3]),
        ]
        for relay in relays:
            relay.start()
        mine = [
            copy(own_in.at[0:3], w_attn.at[:, in_rows(me), :], load_sem.at[2]),
            copy(own_out.at[0:local], w_first.at[:, out_cols(me)], load_sem.at[3]),
            copy(own_in.at[3:], w_up_out.at[:, in_rows(me), :], load_sem.at[4]),
            copy(own_out.at[local:], w_rest_out.at[:, out_cols(me)], load_sem.at[5]),
        ]
        for part in mine:
            part.start()
    for step in range(steps):
        load_g(step).start()
    token_tables(seg_ref, cos_ref, sa_ref, sb_ref, key_aug, query_aug)

    store_one = lambda step: copy(one.at[at(step)], one_out.at[at(step)], store_sem.at[0, step])
    store_two = lambda step: copy(two.at[at(step)], two_out.at[at(step)], store_sem.at[1, step])

    @pl.loop(0, steps)
    def _(step):
        load_x(step).wait()
        one[at(step), :], two[at(step), :] = norm_step(tokens[at(step), :].astype(f32), vec_ref[...])
        store_one(step).start()
        store_two(step).start()
        if linked:
            for k in (1, 2, 3):
                @pl.when(step == 2 * k)
                def _(k=k):
                    relays[0].hop(k)
                    relays[1].hop(k)

    if linked:
        for part in (0, 1):
            relays[part].finish()
            mine[part].wait()
        away = [copy(w_attn, w_attn_out, last_sem.at[0]), copy(w_first, w_first_out, last_sem.at[1])]
        for part in away:
            part.start()
    else:
        for load in loads:
            load.wait()

    lane = lane_of(BLOCK)
    spot = lane & (HEAD_DIM - 1)
    low = lane < HEAD_DIM
    own_of = (low, lane >= HEAD_DIM)
    line = lambda dim: lax.broadcasted_iota(jnp.int32, (BLOCK, BLOCK), dim)
    load_att = lambda step: copy(att.at[at(step)], att_out.at[at(step)], store_sem.at[2, step])
    load_gq = lambda step: copy(gq.at[1:3, at(step), :], gq_out.at[1:3, at(step), :], store_sem.at[3, step])

    @pl.loop(0, steps)
    def _(step):
        if linked:
            for index, (which, k) in enumerate(((2, 1), (3, 1), (2, 2), (3, 2), (2, 3), (3, 3))):
                pl.when(step == index + 2)(functools.partial(relays[which].hop, k))
        load_g(step).wait()
        row = pl.multiple_of(step * BLOCK, BLOCK)
        mine_rows = pl.ds(row, BLOCK)
        x = one[mine_rows, :]
        proj = [dot(x, w_attn[s]) + bias_ref[s : s + 1, :] for s in range(3)]
        grad_out = dot(cot[mine_rows, :], w_first[...], COLS).astype(bf16).astype(f32)
        tables = cos_ref[mine_rows, :], sa_ref[mine_rows, :], sb_ref[mine_rows, :]
        for tile in range(heads // 2):
            cols = slice(tile * LANES, (tile + 1) * LANES)
            q = turned(proj[0][:, cols], *tables) * QUERY_SCALE
            k = turned(proj[1][:, cols], *tables)
            v = proj[2][:, cols]
            keys_t[cols, mine_rows] = k.astype(bf16).T
            for odd in range(2):
                own = own_of[odd]
                head = 2 * tile + odd
                queries[head, mine_rows, :] = jnp.where(own, q, query_aug[mine_rows, :]).astype(bf16)
                keys[head, mine_rows, :] = jnp.where(own, k, key_aug[mine_rows, :]).astype(bf16)
                vals[head, mine_rows, :] = jnp.where(own, v, 1.0).astype(bf16)

        def attend(blocks):
            for tile in range(heads // 2):
                cols = slice(tile * LANES, (tile + 1) * LANES)
                outs, logs = [], []
                for odd in range(2):
                    head = 2 * tile + odd
                    q = queries[head, mine_rows, :]
                    near = jnp.where(line(0) >= line(1), dot(q, keys[head, mine_rows, :], COLS), -FAR)
                    top = jnp.max(near, 1, keepdims=True)
                    if blocks > 1:
                        span = pl.ds(pl.multiple_of(row - (blocks - 1) * BLOCK, BLOCK), (blocks - 1) * BLOCK)
                        far = dot(q, keys[head, span, :], COLS)
                        top = jnp.maximum(top, jnp.max(far, 1, keepdims=True))
                    out = dot(jnp.exp2(near - top).astype(bf16), vals[head, mine_rows, :])
                    if blocks > 1:
                        out = out + dot(jnp.exp2(far - top).astype(bf16), vals[head, span, :])
                    outs.append(out / pltpu.roll(out, HEAD_DIM, 1))
                    logs.append(top + jnp.log2(out))
                out = jnp.where(low, outs[0], outs[1])
                att[mine_rows, cols] = out.astype(bf16)
                do = grad_out[:, cols]
                both = do * out
                for odd in range(2):
                    own = own_of[odd]
                    head = 2 * tile + odd
                    log_h = logs[odd].astype(bf16).astype(f32)
                    log_m = (logs[odd] - log_h).astype(bf16).astype(f32)
                    log_l = logs[odd] - log_h - log_m
                    parts = jnp.where(spot == 4, log_h, jnp.where(spot == 5, log_m, log_l))
                    taken = (~own) & (spot >= 4) & (spot < 7)
                    queries[head, mine_rows, :] = jnp.where(
                        taken, -parts, queries[head, mine_rows, :].astype(f32)
                    ).astype(bf16)
                    delta = jnp.sum(jnp.where(own, both, 0.0), 1, keepdims=True)
                    delta_h = delta.astype(bf16).astype(f32)
                    delta_m = (delta - delta_h).astype(bf16).astype(f32)
                    delta_l = delta - delta_h - delta_m
                    parts = jnp.where(
                        spot == 0, -delta_h, jnp.where(spot == 1, -delta_m, jnp.where(spot == 2, -delta_l, 0.0))
                    )
                    grads[head, mine_rows, :] = jnp.where(own, do, parts).astype(bf16)

        for blocks in range(1, MOST_BLOCKS + 1):
            pl.when(jnp.minimum(step + 1, MOST_BLOCKS) == blocks)(functools.partial(attend, blocks))
        load_att(step).start()

    turn[...] = jnp.zeros_like(turn)

    @pl.loop(0, steps)
    def _(back):
        step = steps - 1 - back
        row = pl.multiple_of(step * BLOCK, BLOCK)
        mine_rows = pl.ds(row, BLOCK)
        tables = cos_ref[mine_rows, :], -sa_ref[mine_rows, :], -sb_ref[mine_rows, :]

        def attend(blocks):
            for tile in range(heads // 2):
                cols = slice(tile * LANES, (tile + 1) * LANES)
                results = []
                for odd in range(2):
                    head = 2 * tile + odd
                    turn_rows = slice(head * HEAD_DIM, (head + 1) * HEAD_DIM)
                    total = None
                    for first, size in ((0, 1), (1, blocks - 1)):
                        if size == 0:
                            continue
                        span = pl.ds(pl.multiple_of(row + first * BLOCK, BLOCK), size * BLOCK)
                        q, do = queries[head, span, :], grads[head, span, :]
                        p = jnp.exp2(dot(keys[head, mine_rows, :], q, COLS))
                        if first == 0:
                            p = jnp.where(line(0) <= line(1), p, 0.0)
                        ds = (p * dot(vals[head, mine_rows, :], do, COLS)).astype(bf16)
                        part = dot(ds, q), dot(p.astype(bf16), do)
                        total = part if total is None else (total[0] + part[0], total[1] + part[1])
                        turn[turn_rows, span] += dot(keys_t[turn_rows, mine_rows], ds)
                    results.append(total)
                dk = jnp.where(low, results[0][0], results[1][0]) * LN2
                gq[1, mine_rows, cols] = turned(dk, *tables).astype(bf16)
                gq[2, mine_rows, cols] = jnp.where(low, results[0][1], results[1][1]).astype(bf16)

        for blocks in range(1, MOST_BLOCKS + 1):
            pl.when(jnp.minimum(back + 1, MOST_BLOCKS) == blocks)(functools.partial(attend, blocks))
        load_gq(step).start()

    @pl.loop(0, steps)
    def _(step):
        mine_rows = at(step)
        for tile in range(heads // 2):
            cols = slice(tile * LANES, (tile + 1) * LANES)
            dq = turn[cols, mine_rows].T * 0.125
            gq[0, mine_rows, cols] = turned(
                dq, cos_ref[mine_rows, :], -sa_ref[mine_rows, :], -sb_ref[mine_rows, :]
            ).astype(bf16)

    final = copy(gq.at[0], gq_out.at[0], last_sem.at[2])
    final.start()
    if linked:
        for part in (2, 3):
            relays[part].finish()
            mine[part].wait()
        for part in away:
            part.wait()

    @pl.loop(0, steps)
    def _(step):
        for store in (store_one, store_two, load_att, load_gq):
            store(step).wait()

    final.wait()


def front(linked, w_in, w_out, tokens, cot, vec, bias, segments):
    rows, width = tokens.shape
    local = bias.shape[1]
    heads = local // HEAD_DIM
    steps = rows // BLOCK
    anywhere = pl.BlockSpec(memory_space=pl.ANY)
    vmem = pl.BlockSpec(memory_space=pltpu.VMEM)
    shape = jax.ShapeDtypeStruct
    tiny = (16, LANES)
    gathered_shapes = [
        shape((4, width, local) if linked else tiny, bf16),
        shape((4 * local, width) if linked else tiny, bf16),
        shape((3, width, local) if linked else tiny, bf16),
        shape((local, width) if linked else tiny, bf16),
    ]
    masters = [w_in.shape, w_out.shape] if linked else [tiny, tiny]
    owns = [w_in.shape, w_out.shape] if linked else [tiny, tiny]
    return pl.pallas_call(
        functools.partial(front_kernel, linked),
        in_specs=[anywhere] * 4 + [vmem] * 3,
        out_specs=[anywhere] * 8,
        out_shape=gathered_shapes + [
            shape((rows, width), bf16), shape((rows, width), bf16),
            shape((rows, local), bf16), shape((3, rows, local), bf16),
        ],
        scratch_shapes=[
            pltpu.VMEM(masters[0], f32), pltpu.VMEM(masters[1], f32),
            pltpu.VMEM(owns[0], bf16), pltpu.VMEM(owns[1], bf16),
            pltpu.VMEM((3, width, local), bf16), pltpu.VMEM((local, width), bf16),
            pltpu.VMEM((rows, width), bf16), pltpu.VMEM((rows, width), bf16),
            pltpu.VMEM((rows, width), bf16), pltpu.VMEM((rows, width), bf16),
            pltpu.VMEM((3, rows, local), bf16), pltpu.VMEM((rows, local), bf16),
            pltpu.VMEM((rows, LANES), f32), pltpu.VMEM((rows, LANES), f32), pltpu.VMEM((rows, LANES), f32),
            pltpu.VMEM((rows, LANES), f32), pltpu.VMEM((rows, LANES), f32),
            pltpu.VMEM((heads, rows, LANES), bf16), pltpu.VMEM((heads, rows, LANES), bf16),
            pltpu.VMEM((heads, rows, LANES), bf16), pltpu.VMEM((heads, rows, LANES), bf16),
            pltpu.VMEM((local, rows), bf16), pltpu.VMEM((local, rows), f32),
            pltpu.SemaphoreType.DMA((6,)), pltpu.SemaphoreType.DMA((2, steps)),
            pltpu.SemaphoreType.DMA((4, steps)), pltpu.SemaphoreType.DMA((3,)),
            pltpu.SemaphoreType.DMA((4, 2, 3, 7)),
        ],
        compiler_params=params(collective_id=0, has_side_effects=True) if linked else params(),
        name="front",
    )(w_in, w_out, tokens, cot, vec, bias, segments)


def normal_cdf(value):
    bell = jnp.exp2(value * value * (-0.5 * LOG2E))
    t = 1.0 / (1.0 + (0.3275911 / 1.4142135623730951) * jnp.abs(value))
    poly = 0.5 * 1.061405429
    for coefficient in (-1.453152027, 1.421413741, -0.284496736, 0.254829592):
        poly = poly * t + 0.5 * coefficient
    tail = poly * t * bell
    return jnp.where(value >= 0.0, 1.0 - tail, tail), bell


def by_device(value, held, outs):
    me, local = lax.axis_index("tensor"), value.shape[1] // len(outs)
    for c in range(len(outs)):
        held[lax.bitwise_xor(me, c)] = value[:, c * local : (c + 1) * local].astype(bf16)
    for k, out in enumerate(outs):
        out[...] = held[k]


def feed_kernel(x_ref, g_ref, att_ref, wu_ref, wf_ref, wr_ref, bias_ref, *refs):
    *part_refs, gup_ref, hidden_ref, gsum_ref, held = refs
    clear_first(gsum_ref)
    x, g = x_ref[...], g_ref[...]
    gsum_ref[0:1, :] += jnp.sum(g.astype(f32), 0, keepdims=True)
    slots, _, local = wu_ref.shape
    branch = dot(att_ref[...], wf_ref[...])
    for s in range(slots):
        w_rows = slice(s * local, (s + 1) * local)
        up = dot(x, wu_ref[s]) + bias_ref[3 + s : 4 + s, :]
        grad_hidden = dot(g, wr_ref[w_rows, :], COLS)
        cdf, bell = normal_cdf(up)
        hidden = (up * cdf).astype(bf16)
        gup_ref[s] = (grad_hidden * (cdf + up * bell * 0.3989422804014327)).astype(bf16)
        hidden_ref[s] = hidden
        branch = branch + dot(hidden, wr_ref[w_rows, :])
    by_device(branch, held, part_refs)


def feed(norm_two, cot, att, w_up, w_first, w_rest, bias):
    rows, width = cot.shape
    slots, _, local = w_up.shape
    share = width // local
    size = 2 * BLOCK
    block = lambda cols: pl.BlockSpec((size, cols), lambda i: (i, 0))
    slotted = lambda count: pl.BlockSpec((count, size, local), lambda i: (0, i, 0))
    return pl.pallas_call(
        feed_kernel,
        grid=(rows // size,),
        in_specs=[
            block(width), block(width), block(local), full(w_up.shape), full(w_first.shape),
            full(w_rest.shape), full(bias.shape),
        ],
        out_specs=[block(local)] * share + [slotted(slots), slotted(slots), full((8, width))],
        scratch_shapes=[pltpu.VMEM((share, size, local), bf16)],
        out_shape=[jax.ShapeDtypeStruct((rows, local), bf16)] * share
        + [
            jax.ShapeDtypeStruct((slots, rows, local), bf16),
            jax.ShapeDtypeStruct((slots, rows, local), bf16),
            jax.ShapeDtypeStruct((8, width), f32),
        ],
        compiler_params=params(),
        cost_estimate=pl.CostEstimate(
            flops=2 * rows * width * local * 13, bytes_accessed=16 * rows * width,
            transcendentals=rows * width * 2,
        ),
        name="feed",
    )(norm_two, cot, att, w_up, w_first, w_rest, bias)


def norm_grad_kernel(
    gq_ref, gu_ref, wa_ref, wu_ref, x_ref, vec_ref, *refs
):
    *part_refs, stat_ref, vec_grad_ref, held = refs
    me = lax.axis_index("tensor")
    @pl.when(pl.program_id(0) == 0)
    def _():
        vec_grad_ref[...] = jnp.zeros_like(vec_grad_ref)

    x = x_ref[...].astype(f32)
    mean = jnp.mean(x, 1, keepdims=True)
    shifted = x - mean
    rstd = lax.rsqrt(jnp.mean(shifted * shifted, 1, keepdims=True) + EPSILON)
    normed = shifted * rstd
    local = gq_ref.shape[2]
    sums = dots = 0.0
    for c in range(len(part_refs)):
        cols = slice(c * local, (c + 1) * local)
        one = sum(dot(gq_ref[s], wa_ref[s, cols, :], COLS) for s in range(gq_ref.shape[0]))
        two = sum(dot(gu_ref[s], wu_ref[s, cols, :], COLS) for s in range(gu_ref.shape[0]))
        scaled = one * vec_ref[0:1, cols] + two * vec_ref[2:3, cols]
        held[lax.bitwise_xor(me, c)] = scaled.astype(bf16)
        sums = sums + jnp.sum(scaled, 1, keepdims=True)
        dots = dots + jnp.sum(scaled * normed[:, cols], 1, keepdims=True)
        vec_grad_ref[0:1, cols] += jnp.sum(one * normed[:, cols], 0, keepdims=True)
        vec_grad_ref[1:2, cols] += jnp.sum(one, 0, keepdims=True)
        vec_grad_ref[2:3, cols] += jnp.sum(two * normed[:, cols], 0, keepdims=True)
        vec_grad_ref[3:4, cols] += jnp.sum(two, 0, keepdims=True)
    for k, out in enumerate(part_refs):
        out[...] = held[k]
    lane = lane_of(x.shape[0])
    stats = jnp.where(lane == 0, sums, jnp.where(lane == 1, dots, jnp.where(lane == 2, mean, rstd)))
    stat_ref[...] = stats.T[0:8, :]


def norm_grad(grad_qkv, grad_up, w_attn, w_up, tokens, vec):
    rows, width = tokens.shape
    local = w_up.shape[2]
    share = width // local
    size = 2 * BLOCK
    block = lambda cols: pl.BlockSpec((size, cols), lambda i: (i, 0))
    slotted = lambda slots: pl.BlockSpec((slots, size, local), lambda i: (0, i, 0))
    return pl.pallas_call(
        norm_grad_kernel,
        grid=(rows // size,),
        in_specs=[
            slotted(3), slotted(w_up.shape[0]), full(w_attn.shape), full(w_up.shape),
            block(width), full(vec.shape),
        ],
        out_specs=[block(local)] * share + [pl.BlockSpec((8, size), lambda i: (0, i)), full((8, width))],
        scratch_shapes=[pltpu.VMEM((share, size, local), bf16)],
        out_shape=[jax.ShapeDtypeStruct((rows, local), bf16)] * share
        + [
            jax.ShapeDtypeStruct((8, rows), f32),
            jax.ShapeDtypeStruct((8, width), f32),
        ],
        compiler_params=params(),
        cost_estimate=pl.CostEstimate(
            flops=2 * rows * width * local * 7, bytes_accessed=8 * rows * width, transcendentals=0
        ),
        name="norm_grad",
    )(grad_qkv, grad_up, w_attn, w_up, tokens, vec)


def two_parts(value, high_ref, low_ref):
    high = value.astype(bf16)
    low = (value - high.astype(f32)).astype(bf16)
    high_ref[0], low_ref[0] = high, low
    return high, low


def clear_first(*refs):
    @pl.when(pl.program_id(0) == 0)
    def _():
        for ref in refs:
            ref[...] = jnp.zeros_like(ref)


def matrix_in_kernel(one_ref, two_ref, gq_ref, gu_ref, e_ref, q_ref, high_ref, low_ref, left_ref, bias_ref):
    clear_first(left_ref)
    slot = pl.program_id(0)

    def run(x_ref, grad_ref):
        grad = grad_ref[0]
        high, low = two_parts(dot(x_ref[...], grad, ROWS) + e_ref[0], high_ref, low_ref)
        q = stacked(q_ref[0])
        left_ref[...] += folded(dot(q, high, COLS)) + folded(dot(q, low, COLS))
        bias_ref[0] = jnp.sum(grad.astype(f32), 0, keepdims=True)

    pl.when(slot < 3)(lambda: run(one_ref, gq_ref))
    pl.when(slot >= 3)(lambda: run(two_ref, gu_ref))


def matrix_out_kernel(att_ref, hid_ref, g_ref, e_ref, q_ref, high_ref, low_ref, left_ref):
    clear_first(left_ref)
    slot = pl.program_id(0)

    def run(mixed):
        high, low = two_parts(dot(mixed, g_ref[...], ROWS) + e_ref[0], high_ref, low_ref)
        q = stacked(q_ref[0])
        left_ref[...] += folded(dot(q, high)) + folded(dot(q, low))

    pl.when(slot < 1)(lambda: run(att_ref[...]))
    pl.when(slot >= 1)(lambda: run(hid_ref[0]))


def slot_spec(shape, index=lambda i: i):
    return pl.BlockSpec((1,) + tuple(shape[1:]), lambda i: (index(i), 0, 0))


def matrix_in(norm_one, norm_two, grad_qkv, grad_up, error, q):
    slots, width, local = error.shape
    rows = norm_one.shape[0]
    big = jax.ShapeDtypeStruct(error.shape, bf16)
    return pl.pallas_call(
        matrix_in_kernel,
        grid=(slots,),
        in_specs=[
            full(norm_one.shape), full(norm_two.shape),
            slot_spec(grad_qkv.shape, lambda i: jnp.minimum(i, 2)),
            slot_spec(grad_up.shape, lambda i: jnp.maximum(i - 3, 0)),
            slot_spec(error.shape), slot_spec(q.shape),
        ],
        out_specs=[slot_spec(error.shape), slot_spec(error.shape), full((8, width)), slot_spec((slots, 1, local))],
        out_shape=[big, big, jax.ShapeDtypeStruct((8, width), f32), jax.ShapeDtypeStruct((slots, 1, local), f32)],
        compiler_params=params(),
        cost_estimate=pl.CostEstimate(
            flops=2 * slots * rows * width * local, bytes_accessed=10 * error.size, transcendentals=0
        ),
        name="matrix_in",
    )(norm_one, norm_two, grad_qkv, grad_up, error, q)


def matrix_out(att, hidden, cot, error, q):
    slots, local, width = error.shape
    rows = cot.shape[0]
    big = jax.ShapeDtypeStruct(error.shape, bf16)
    return pl.pallas_call(
        matrix_out_kernel,
        grid=(slots,),
        in_specs=[
            full(att.shape), slot_spec(hidden.shape, lambda i: jnp.maximum(i - 1, 0)), full(cot.shape),
            slot_spec(error.shape), slot_spec(q.shape),
        ],
        out_specs=[slot_spec(error.shape), slot_spec(error.shape), full((8, width))],
        out_shape=[big, big, jax.ShapeDtypeStruct((8, width), f32)],
        compiler_params=params(),
        cost_estimate=pl.CostEstimate(
            flops=2 * slots * rows * width * local, bytes_accessed=10 * error.size, transcendentals=0
        ),
        name="matrix_out",
    )(att, hidden, cot, error, q)


def orthonormal_rows(matrix):
    index = lax.broadcasted_iota(jnp.int32, (matrix.shape[0], 1), 0)
    for r in range(matrix.shape[0]):
        row = matrix[r : r + 1, :]
        row = row * lax.rsqrt(jnp.sum(row * row, 1, keepdims=True) + 1e-06)
        along = jnp.sum(matrix * row, 1, keepdims=True)
        matrix = jnp.where(index == r, row, jnp.where(index > r, matrix - along * row, matrix))
    return matrix


def basis_kernel(left_in_ref, left_out_ref, basis_in_ref, basis_out_ref):
    basis_in_ref[...] = orthonormal_rows(left_in_ref[...])
    basis_out_ref[...] = orthonormal_rows(left_out_ref[...])


def bases(left_in, left_out):
    shape = jax.ShapeDtypeStruct(left_in.shape, f32)
    return pl.pallas_call(
        basis_kernel, out_shape=[shape, shape], compiler_params=params(), name="bases"
    )(left_in, left_out)


def right_kernel(dims, basis_ref, high_ref, low_ref, out_ref):
    basis = stacked(basis_ref[...])
    out_ref[0] = folded(dot(basis, high_ref[0], dims)) + folded(dot(basis, low_ref[0], dims))


def right_factor(basis, matrix, dims, columns):
    slots = matrix[0].shape[0]
    return pl.pallas_call(
        functools.partial(right_kernel, dims),
        grid=(slots,),
        in_specs=[full(basis.shape), slot_spec(matrix[0].shape), slot_spec(matrix[1].shape)],
        out_specs=pl.BlockSpec((1, 8, columns), lambda i: (i, 0, 0)),
        out_shape=jax.ShapeDtypeStruct((slots, 8, columns), f32),
        compiler_params=params(),
        cost_estimate=pl.CostEstimate(flops=0, bytes_accessed=matrix[0].size * 4, transcendentals=0),
        name="right_factor",
    )(basis, *matrix)


def outer(a, b):
    ah, am, al = (part.astype(f32) for part in pieces(a))
    bh, bm, bl = (part.astype(f32) for part in pieces(b))
    left = jnp.concatenate([ah, ah, am, ah, am, al], 0).astype(bf16)
    right = jnp.concatenate([bh, bm, bh, bl, bm, bh], 0).astype(bf16)
    return dot(left, right, ROWS)


def finish_kernel(
    basis_in_ref, basis_out_ref, own_ref, bundle_ref, vec_ref, vec_mom_ref, bias_ref, bias_mom_ref,
    mi_ref, mo_ref, momi_ref, momo_ref, wi_ref, wo_ref,
    ei_out, eo_out, momi_out, momo_out, wi_out, wo_out,
    vec_out, vec_mom_out, bias_out, bias_mom_out, right_in_out, right_out_out,
    mi, mo, momi, momo, wi, wo, load_sem, store_sem,
):
    copy = pltpu.make_async_copy
    slots_in, slots_out = mi.shape[0], mo.shape[0]
    local = vec_mom_ref.shape[1]
    work = []
    for s in range(slots_in + slots_out):
        wide = s < slots_in
        slot = s if wide else s - slots_in
        group = ((mi_ref, mi, ei_out), (momi_ref, momi, momi_out), (wi_ref, wi, wi_out)) if wide else (
            (mo_ref, mo, eo_out), (momo_ref, momo, momo_out), (wo_ref, wo, wo_out))
        work.append(
            (wide, slot,
             [copy(src.at[slot], held.at[slot], load_sem.at[s, n]) for n, (src, held, _) in enumerate(group)],
             [copy(held.at[slot], out.at[slot], store_sem.at[s, n]) for n, (_, held, out) in enumerate(group)])
        )
    for _, _, loads, _ in work:
        for load in loads:
            load.start()
    basis_in, basis_out = basis_in_ref[...], basis_out_ref[...]
    own_in, own_out = own_ref[0:8, :], own_ref[8:16, :]
    row = (slots_in + slots_out) * 8
    start = pl.ds(pl.multiple_of(lax.axis_index("tensor") * local, local), local)
    mom = MOMENTUM_DECAY * vec_mom_ref[...] + bundle_ref[row : row + vec_mom_ref.shape[0], :]
    vec_mom_out[...] = mom
    vec_out[...] = vec_ref[:, start] - VECTOR_RATE * mom
    mom = MOMENTUM_DECAY * bias_mom_ref[...] + bundle_ref[row + 8 : row + 8 + slots_in, :]
    bias_mom_out[...] = mom
    bias_out[...] = bias_ref[...] - VECTOR_RATE * mom
    for wide, slot, loads, stores in work:
        right = bundle_ref[8 * slot : 8 * slot + 8, :] if wide else bundle_ref[
            8 * (slots_in + slot) : 8 * (slots_in + slot) + 8, :]
        if wide:
            right_in_out[slot] = right
        else:
            right_out_out[slot] = right
        matrix, momentum, master = (mi, momi, wi) if wide else (mo, momo, wo)
        pair = (lambda b: outer(b, right)) if wide else (lambda b: outer(right, b))
        for load in loads:
            load.wait()
        matrix[slot] = matrix[slot] - pair(basis_in if wide else basis_out)
        stores[0].start()
        mom = MOMENTUM_DECAY * momentum[slot] + pair(own_in if wide else own_out)
        momentum[slot] = mom
        master[slot] = master[slot] - LEARN_RATE * mom
        stores[1].start()
        stores[2].start()
    for _, _, _, stores in work:
        for store in stores:
            store.wait()


def finish(basis_in, basis_out, own, bundle, vec, vec_mom, bias, bias_mom, *matrices):
    anywhere = pl.BlockSpec(memory_space=pl.ANY)
    vmem = pl.BlockSpec(memory_space=pltpu.VMEM)
    like = lambda a: jax.ShapeDtypeStruct(a.shape, f32)
    slots_in, slots_out = matrices[0].shape[0], matrices[1].shape[0]
    local = vec_mom.shape[1]
    return pl.pallas_call(
        finish_kernel,
        in_specs=[vmem] * 8 + [anywhere] * 6,
        out_specs=[anywhere] * 6 + [vmem] * 6,
        out_shape=[like(a) for a in matrices]
        + [like(vec_mom), like(vec_mom), like(bias_mom), like(bias_mom)]
        + [jax.ShapeDtypeStruct((slots, 8, local), f32) for slots in (slots_in, slots_out)],
        scratch_shapes=[pltpu.VMEM(a.shape, f32) for a in matrices]
        + [pltpu.SemaphoreType.DMA((slots_in + slots_out, 3)), pltpu.SemaphoreType.DMA((slots_in + slots_out, 3))],
        compiler_params=params(),
        name="finish",
    )(basis_in, basis_out, own, bundle, vec, vec_mom, bias, bias_mom, *matrices)


def trade(axis, send, take, sems):
    me, size = lax.axis_index(axis), lax.axis_size(axis)
    copies = []
    for k in range(1, size):
        peer = lax.bitwise_xor(me, k)
        copies.append(
            pltpu.make_async_remote_copy(
                src_ref=send(peer, k), dst_ref=take(peer, k),
                send_sem=sems.at[0, k], recv_sem=sems.at[1, k],
                device_id={axis: peer}, device_id_type=MESH,
            )
        )
    for copy in copies:
        copy.start()
    return copies


def back_kernel(
    one_ref, two_ref, g_ref, gq_ref, gu_ref, att_ref, hid_ref, ei_ref, eo_ref,
    branch_pair, branch_far, branch_both, grad_pair, grad_far, grad_both, stat_ref,
    qi_ref, qo_ref, vec_ref, gsum_ref,
    branch_near_out, branch_far_out, grad_near_out, grad_far_out, stats_out, mi_out, mo_out, basis_in_ref, basis_out_ref, own_ref, bundle_ref,
    one, two, cot, gq, gu, att, hid, mi, mo, left, left_take, left_sum, vec_take, bundle, bundle_take, bundle_sum,
    sums, sum_take,
    load_sem, slot_sem, store_sem, link_sem, tensor_sem, stat_sem, pair_sem, pair_load_sem,
):
    copy = pltpu.make_async_copy
    me, column = lax.axis_index("dp"), lax.axis_index("tensor")
    workers, parts = lax.axis_size("dp"), lax.axis_size("tensor")
    slots_in, width, local = mi.shape
    slots_out = mo.shape[0]
    lanes = width // workers
    group = bundle.shape[0] // workers
    loads = {
        name: copy(src, dst, load_sem.at[index])
        for index, (name, src, dst) in enumerate(
            (("g", g_ref, cot), ("att", att_ref, att), ("one", one_ref, one), ("gq", gq_ref, gq), ("two", two_ref, two))
        )
    }
    load_hid = [copy(hid_ref.at[s], hid.at[s], slot_sem.at[0, s]) for s in range(slots_out - 1)]
    load_gu = [copy(gu_ref.at[s], gu.at[s], slot_sem.at[1, s]) for s in range(slots_in - 3)]
    load_mo = [copy(eo_ref.at[s], mo.at[s], slot_sem.at[2, s]) for s in range(slots_out)]
    load_mi = [copy(ei_ref.at[s], mi.at[s], slot_sem.at[3, s]) for s in range(slots_in)]
    store_mo = [copy(mo.at[s], mo_out.at[s], store_sem.at[0, s]) for s in range(slots_out)]
    store_mi = [copy(mi.at[s], mi_out.at[s], store_sem.at[1, s]) for s in range(slots_in)]
    loads["g"].start()
    loads["att"].start()
    load_mo[0].start()
    for s in range(1, slots_out):
        load_hid[s - 1].start()
        load_mo[s].start()
    loads["one"].start()
    loads["gq"].start()
    for s in range(3):
        load_mi[s].start()
    loads["two"].start()
    for s in range(3, slots_in):
        load_gu[s - 3].start()
        load_mi[s].start()

    barrier = pltpu.get_barrier_semaphore()
    for axis, size in (("dp", workers), ("tensor", parts)):
        for k in range(1, size):
            peer = lax.bitwise_xor(lax.axis_index(axis), k)
            pl.semaphore_signal(barrier, inc=1, device_id={axis: peer}, device_id_type=MESH)
    pl.semaphore_wait(barrier, workers + parts - 2)

    block = lambda index: pl.ds(pl.multiple_of(index * local, local), local)
    vec_copies = trade(
        "tensor", lambda peer, k: vec_ref.at[:, block(peer)], lambda peer, k: vec_take.at[k], tensor_sem
    )
    stat_copies = trade("tensor", lambda peer, k: stat_ref, lambda peer, k: stats_out.at[k - 1], stat_sem)
    sibling, opposite = lax.bitwise_xor(column, 1), lax.bitwise_xor(column, 2)

    def pass_to(peer, src, dst, index):
        return pltpu.make_async_remote_copy(
            src_ref=src, dst_ref=dst, send_sem=pair_sem.at[0, index], recv_sem=pair_sem.at[1, index],
            device_id={"tensor": peer}, device_id_type=MESH,
        )

    exchanges = []
    for n, (pair, far, both, near_out, far_out) in enumerate(
        ((branch_pair, branch_far, branch_both, branch_near_out, branch_far_out),
         (grad_pair, grad_far, grad_both, grad_near_out, grad_far_out))
    ):
        exchanges.append(
            (copy(far, sums.at[n], pair_load_sem.at[n]),
             pass_to(sibling, both, sum_take.at[n], 3 * n),
             pass_to(sibling, pair, near_out, 3 * n + 1),
             pass_to(opposite, sums.at[n], far_out, 3 * n + 2))
        )
    for load, first, second, _ in exchanges:
        load.start()
        first.start()
        second.start()

    def send_sums(n):
        load, first, _, last = exchanges[n]
        load.wait()
        first.wait()
        sums[n] = (sums[n].astype(f32) + sum_take[n].astype(f32)).astype(bf16)
        last.start()

    bundle[...] = jnp.zeros_like(bundle)
    first_vec = (slots_in + slots_out) * 8
    first_bias = first_vec + 8

    total = jnp.zeros((8, width), f32)
    loads["g"].wait()
    loads["att"].wait()
    for s in range(slots_out):
        if s:
            load_hid[s - 1].wait()
        if s == 1:
            send_sums(0)
        if s == 2:
            send_sums(1)
        load_mo[s].wait()
        value = dot(hid[s - 1] if s else att[...], cot[...], ROWS) + mo[s]
        mo[s] = value
        store_mo[s].start()
        high, low, _ = pieces(value)
        q = stacked(qo_ref[s])
        total = total + folded(dot(q, high)) + folded(dot(q, low))
    left[8:16, :] = total
    total = jnp.zeros((8, width), f32)
    loads["one"].wait()
    loads["gq"].wait()
    for s in range(slots_in):
        if s == 3:
            loads["two"].wait()
        if s >= 3:
            load_gu[s - 3].wait()
        load_mi[s].wait()
        grad = gq[s] if s < 3 else gu[s - 3]
        value = dot(one[...] if s < 3 else two[...], grad, ROWS) + mi[s]
        mi[s] = value
        store_mi[s].start()
        high, low, _ = pieces(value)
        q = stacked(qi_ref[s])
        total = total + folded(dot(q, high, COLS)) + folded(dot(q, low, COLS))
    left[0:8, :] = total

    part = lambda index: pl.ds(pl.multiple_of(index * lanes, lanes), lanes)
    copies = trade("dp", lambda peer, k: left.at[:, part(peer)], lambda peer, k: left_take.at[k], link_sem.at[0])
    for s in range(slots_in):
        grad = gq[s] if s < 3 else gu[s - 3]
        bundle[first_bias + s : first_bias + s + 1, :] = jnp.sum(grad.astype(f32), 0, keepdims=True)
    for c in vec_copies:
        c.wait()
    vec = vec_ref[:, block(column)]
    for k in range(1, parts):
        vec = vec + vec_take[k]
    rows8 = lax.broadcasted_iota(jnp.int32, (8, local), 0)
    bundle[first_vec : first_vec + 8, :] = jnp.where(
        rows8 < 4, vec, jnp.where(rows8 == 4, gsum_ref[0:1, block(column)], 0.0)
    )
    for c in copies:
        c.wait()
    value = left[:, part(me)]
    for k in range(1, workers):
        value = value + left_take[k]
    left_sum[:, part(me)] = value / workers
    copies = trade(
        "dp", lambda peer, k: left_sum.at[:, part(me)], lambda peer, k: left_sum.at[:, part(me)], link_sem.at[1]
    )
    for c in copies:
        c.wait()
    basis_in, basis_out = orthonormal_rows(left_sum[0:8, :]), orthonormal_rows(left_sum[8:16, :])
    basis_in_ref[...], basis_out_ref[...] = basis_in, basis_out
    left_sum[0:8, :], left_sum[8:16, :] = basis_in, basis_out
    own_ref[...] = left_sum[:, part(me)]
    sides = stacked(basis_in), stacked(basis_out)
    for s in range(slots_in):
        high, low, _ = pieces(mi[s])
        bundle[8 * s : 8 * s + 8, :] = folded(dot(sides[0], high)) + folded(dot(sides[0], low))
    for s in range(slots_out):
        high, low, _ = pieces(mo[s])
        row = 8 * (slots_in + s)
        bundle[row : row + 8, :] = folded(dot(sides[1], high, COLS)) + folded(dot(sides[1], low, COLS))

    lot = lambda index: pl.ds(pl.multiple_of(index * group, group), group)
    copies = trade("dp", lambda peer, k: bundle.at[lot(peer), :], lambda peer, k: bundle_take.at[k], link_sem.at[2])
    for c in copies:
        c.wait()
    value = bundle[lot(me), :]
    for k in range(1, workers):
        value = value + bundle_take[k]
    bundle_sum[lot(me), :] = value / workers
    copies = trade(
        "dp", lambda peer, k: bundle_sum.at[lot(me), :], lambda peer, k: bundle_sum.at[lot(me), :], link_sem.at[3]
    )
    for c in copies:
        c.wait()
    bundle_ref[...] = bundle_sum[...]
    for store in store_mo + store_mi:
        store.wait()
    for c in stat_copies:
        c.wait()
    for _, _, second, last in exchanges:
        second.wait()
        last.wait()


def back(norm_one, norm_two, cot, grad_qkv, grad_up, att, hidden, error_in, error_out, branch, grad, stats,
    q_in, q_out, vec, gsum):
    slots_in, width, local = error_in.shape
    slots_out = error_out.shape[0]
    workers, parts = lax.axis_size("dp"), lax.axis_size("tensor")
    anywhere = pl.BlockSpec(memory_space=pl.ANY)
    vmem = pl.BlockSpec(memory_space=pltpu.VMEM)
    shape = jax.ShapeDtypeStruct
    rows = 8 * workers * pl.cdiv((slots_in + slots_out) * 8 + 8 + slots_in, 8 * workers)
    group = rows // workers
    like = lambda a: pltpu.VMEM(a.shape, a.dtype)
    return pl.pallas_call(
        back_kernel,
        in_specs=[anywhere] * 16 + [vmem] * 4,
        out_specs=[anywhere] * 7 + [vmem] * 4,
        out_shape=[shape(branch[0].shape, bf16)] * 4 + [
            shape((parts - 1,) + stats.shape, f32),
            shape(error_in.shape, f32), shape(error_out.shape, f32),
            shape((8, width), f32), shape((8, width), f32), shape((16, width // workers), f32),
            shape((rows, local), f32),
        ],
        scratch_shapes=[
            like(a) for a in (norm_one, norm_two, cot, grad_qkv, grad_up, att, hidden, error_in, error_out)
        ] + [
            pltpu.VMEM((16, width), f32), pltpu.VMEM((workers, 16, width // workers), f32),
            pltpu.VMEM((16, width), f32), pltpu.VMEM((parts, 8, local), f32),
            pltpu.VMEM((rows, local), f32), pltpu.VMEM((workers, group, local), f32), pltpu.VMEM((rows, local), f32),
            pltpu.VMEM((2,) + branch[0].shape, bf16), pltpu.VMEM((2,) + branch[0].shape, bf16),
            pltpu.SemaphoreType.DMA((5,)), pltpu.SemaphoreType.DMA((4, slots_in)),
            pltpu.SemaphoreType.DMA((2, slots_in)), pltpu.SemaphoreType.DMA((4, 2, workers)),
            pltpu.SemaphoreType.DMA((2, parts)), pltpu.SemaphoreType.DMA((2, parts)),
            pltpu.SemaphoreType.DMA((2, 6)), pltpu.SemaphoreType.DMA((2,)),
        ],
        compiler_params=params(collective_id=1, has_side_effects=True),
        name="back",
    )(norm_one, norm_two, cot, grad_qkv, grad_up, att, hidden, error_in, error_out,
      *branch[1:], *grad[1:], stats, q_in, q_out, vec, gsum)


def ends_kernel(column_ref, x_ref, g_ref, bias_ref, *refs):
    *refs, out_ref, in_grad_ref = refs
    branch, grad, stats = refs[:3], refs[3:6], refs[6:]
    total = lambda parts: sum(part[...].astype(f32) for part in parts)
    x = x_ref[...].astype(f32)
    out_ref[...] = (x + total(branch) + bias_ref[...]).astype(bf16)
    own = stats[0][...].T
    means = total(stats).T / (len(stats) * x.shape[1])
    normed = (x - own[:, 2:3]) * own[:, 3:4]
    in_grad_ref[...] = g_ref[...].astype(f32) + own[:, 3:4] * (total(grad) - means[:, 0:1] - normed * means[:, 1:2])


def ends(column, tokens, cot, bias, branch, grad, stats):
    rows, local = branch[0].shape
    size = 4 * BLOCK
    block = pl.BlockSpec((size, local), lambda i, column: (i, 0))
    mine = pl.BlockSpec((size, local), lambda i, column: (i, column[0]))
    stat = pl.BlockSpec((8, size), lambda i, column: (0, i))
    return pl.pallas_call(
        ends_kernel,
        grid_spec=pltpu.PrefetchScalarGridSpec(
            num_scalar_prefetch=1,
            grid=(rows // size,),
            in_specs=[mine, mine, pl.BlockSpec((1, local), lambda i, column: (0, column[0]))]
            + [block] * (len(branch) + len(grad)) + [stat] * len(stats),
            out_specs=[block, block],
        ),
        out_shape=[jax.ShapeDtypeStruct((rows, local), bf16), jax.ShapeDtypeStruct((rows, local), f32)],
        compiler_params=params(),
        name="ends",
    )(column[None], tokens, cot, bias, *branch, *grad, *stats)


def swapped(value, axis, bits):
    size = lax.axis_size(axis)
    return lax.ppermute(value, axis, [(i, i ^ bits) for i in range(size)])


def spread(parts):
    return [parts[0]] + [swapped(part, "tensor", k) for k, part in enumerate(parts) if k]


def on_device(
    tokens, cotangent, segments, w_in_master, w_out_master, vec_master, bias_in_master,
    w_in_mom, w_out_mom, vec_mom, bias_in_mom, w_in_error, w_out_error, q_in, q_out,
):
    workers = lax.axis_size("dp")
    tensor_index = lax.axis_index("tensor")
    worker_index = lax.axis_index("dp")
    rows, width = tokens.shape
    local = bias_in_master.shape[1]
    start_col = tensor_index * local
    cut = lambda a: lax.dynamic_slice_in_dim(a, start_col, local, 1)

    w_in = w_in_master.transpose(1, 0, 2)
    linked = workers == 8
    if linked:
        shards = w_in, w_out_master.reshape(5 * local, -1)
    else:
        w_in_low = lax.all_gather(w_in.astype(bf16), "dp", axis=1, tiled=True)
        w_out_low = lax.all_gather(w_out_master.astype(bf16), "dp", axis=2, tiled=True)
        shards = w_in_low[:3], w_out_low[0]
    w_up, w_rest, w_attn, w_first, norm_one, norm_two, att, grad_qkv = front(
        linked, *shards, tokens, cotangent, vec_master, bias_in_master, segments
    )
    if not linked:
        w_attn, w_first = shards
        w_up, w_rest = w_in_low[3:], w_out_low[1:].reshape(4 * local, width)

    factors_in, factors_out = q_in.transpose(0, 2, 1), q_out.transpose(0, 2, 1)
    error_in = w_in_error[0].transpose(1, 0, 2)
    error_out = w_out_error[0]
    *branch_parts, grad_up, hidden, cot_sum = feed(
        norm_two, cotangent, att, w_up, w_first, w_rest, bias_in_master
    )
    *grad_parts, stats, vec_local = norm_grad(grad_qkv, grad_up, w_attn, w_up, tokens, vec_master)

    if linked:
        (
            branch_near, branch_far, grad_near, grad_far, far_stats,
            matrix_in_f32, matrix_out_f32, basis_in, basis_out, own, bundle,
        ) = back(
            norm_one, norm_two, cotangent, grad_qkv, grad_up, att, hidden, error_in, error_out,
            branch_parts, grad_parts, stats, factors_in, factors_out, vec_local, cot_sum,
        )
        branch = branch_parts[0], branch_near, branch_far
        grad = grad_parts[0], grad_near, grad_far
        stats = [stats] + [far_stats[k] for k in range(3)]
    else:
        branch, grad = (
            (parts[0], swapped(parts[1], "tensor", 1), swapped(parts[2], "tensor", 2) + swapped(parts[3], "tensor", 3))
            for parts in (branch_parts, grad_parts)
        )
        stats = spread([stats] * 4)
        *parts_out, left_out = matrix_out(att, hidden, cotangent, error_out, factors_out)
        *parts_in, left_in, bias_local = matrix_in(norm_one, norm_two, grad_qkv, grad_up, error_in, factors_in)
        left = lax.psum(jnp.concatenate([left_in, left_out], 0), "dp") / workers
        basis_in, basis_out = bases(left[:8], left[8:])
        vec_rows = cut(jnp.concatenate([lax.psum(vec_local[:4], "tensor"), cot_sum[:1]], 0))
        bundle = jnp.concatenate(
            [
                right_factor(basis_in, parts_in, PLAIN, local).reshape(-1, local),
                right_factor(basis_out, parts_out, COLS, local).reshape(-1, local),
                vec_rows, jnp.zeros((3, local), f32), bias_local[:, 0, :],
            ],
            0,
        )
        bundle = lax.psum(bundle, "dp") / workers
        matrix_in_f32, matrix_out_f32 = (
            high.astype(f32) + low.astype(f32) for high, low in (parts_in, parts_out)
        )
        owned = w_in.shape[1]
        own = jnp.concatenate([basis_in, basis_out], 0)
        own = lax.dynamic_slice_in_dim(own, worker_index * owned, owned, 1)
    (
        new_error_in, new_error_out, new_mom_in, new_mom_out, new_w_in, new_w_out,
        vec_new, vec_mom_new, bias_in_new, bias_in_mom_new, right_in, right_out,
    ) = finish(
        basis_in, basis_out, own, bundle, vec_master, vec_mom, bias_in_master, bias_in_mom,
        matrix_in_f32, matrix_out_f32, w_in_mom.transpose(1, 0, 2), w_out_mom, w_in, w_out_master,
    )
    block_out, input_grad = ends(
        tensor_index, tokens, cotangent, vec_master[4:5], branch, grad, stats
    )
    return (
        block_out,
        input_grad,
        new_w_in.transpose(1, 0, 2),
        new_w_out,
        vec_new,
        bias_in_new,
        new_mom_in.transpose(1, 0, 2),
        new_mom_out,
        vec_mom_new,
        bias_in_mom_new,
        new_error_in.transpose(1, 0, 2)[None],
        new_error_out[None],
        right_in.transpose(0, 2, 1),
        right_out.transpose(0, 2, 1),
    )


def solution(mesh):
    return jax.shard_map(
        on_device,
        mesh=mesh,
        in_specs=(
            P("dp", None), P("dp", None), P("dp", None), P("dp", None, "tensor"),
            P(None, "tensor", "dp"), P(), P(None, "tensor"), P("dp", None, "tensor"),
            P(None, "tensor", "dp"), P(None, "tensor"), P(None, "tensor"),
            P("dp", None, None, "tensor"), P("dp", None, "tensor", None),
            P(None, "tensor", None), P(None, "tensor", None),
        ),
        out_specs=(
            P("dp", "tensor"), P("dp", "tensor"), P("dp", None, "tensor"), P(None, "tensor", "dp"),
            P(None, "tensor"), P(None, "tensor"), P("dp", None, "tensor"), P(None, "tensor", "dp"),
            P(None, "tensor"), P(None, "tensor"), P("dp", None, None, "tensor"),
            P("dp", None, "tensor", None), P(None, "tensor", None), P(None, "tensor", None),
        ),
        check_vma=False,
    )
```

```python
import functools

import jax
import jax.numpy as jnp
from jax import lax
from jax.experimental import pallas as pl
from jax.experimental.pallas import tpu as pltpu
from jax.sharding import PartitionSpec as P

HEAD_DIM = 64
ROT = 16
EPSILON = 1e-05
MOMENTUM_DECAY = 0.9
LEARN_RATE = 0.05
VECTOR_RATE = 0.05
LN2 = 0.6931471805599453
LOG2E = 1.4426950408889634
QUERY_SCALE = 0.125 * LOG2E
FAR = 2.0**30
BLOCK = 256
LANES = 128
MOST_BLOCKS = 5

f32 = jnp.float32
bf16 = jnp.bfloat16
ROWS = (((0,), (0,)), ((), ()))
COLS = (((1,), (1,)), ((), ()))
PLAIN = (((1,), (0,)), ((), ()))
MESH = pl.DeviceIdType.MESH


def dot(a, b, dims=PLAIN):
    return lax.dot_general(a, b, dims, preferred_element_type=f32)


def params(megabytes=56, **more):
    return pltpu.CompilerParams(vmem_limit_bytes=megabytes * 1024 * 1024, **more)


def pieces(value):
    high = value.astype(bf16)
    rest = value - high.astype(f32)
    middle = rest.astype(bf16)
    low = (rest - middle.astype(f32)).astype(bf16)
    return high, middle, low


def stacked(value):
    return jnp.concatenate([part.astype(f32) for part in pieces(value)], 0).astype(bf16)


def folded(total, rows=8):
    return total[:rows] + total[rows : 2 * rows] + total[2 * rows : 3 * rows]


def full(shape):
    return pl.BlockSpec(shape, lambda i: (0,) * len(shape))


class Relay:
    LANES = ("up", "down", "x")

    def __init__(self, place, sems):
        self.place, self.sems = place, sems
        me = lax.axis_index("dp")
        self.z, self.x = lax.div(me, 2), lax.rem(me, 2)
        self.last = lax.axis_size("dp") // 2 - 1

    def copy(self, distance, lane):
        index = self.LANES.index(lane)
        step = (1, -1, 0)[index]
        worker = (self.z + distance) * 2 + self.x
        to = (self.z + step) * 2 + (1 - self.x if lane == "x" else self.x)
        return pltpu.make_async_remote_copy(
            src_ref=self.place(worker),
            dst_ref=self.place(worker),
            send_sem=self.sems.at[0, index, distance + 3],
            recv_sem=self.sems.at[1, index, distance - step + 3],
            device_id={"dp": to},
            device_id_type=MESH,
        )

    def arrival(self, distance, lane):
        index = self.LANES.index(lane)
        ref = self.place((self.z + distance) * 2 + (1 - self.x if lane == "x" else self.x))
        return pltpu.make_async_remote_copy(
            src_ref=ref,
            dst_ref=ref,
            send_sem=self.sems.at[0, index, 3],
            recv_sem=self.sems.at[1, index, distance + 3],
            device_id={"dp": self.z * 2 + 1 - self.x},
            device_id_type=MESH,
        )

    def each(self, distance, lanes, act):
        for lane in lanes:
            run = functools.partial(act, self.copy(distance, lane))
            if lane == "up":
                pl.when(self.z < self.last)(run)
            elif lane == "down":
                pl.when(self.z > 0)(run)
            else:
                run()

    def start(self):
        self.each(0, self.LANES, lambda copy: copy.start())

    def hop(self, k):
        @pl.when(self.z >= k)
        def _():
            self.arrival(-k, "up").wait_recv()
            self.each(-k, ("up", "x"), lambda copy: copy.start())

        @pl.when(self.z + k <= self.last)
        def _():
            self.arrival(k, "down").wait_recv()
            self.each(k, ("down", "x"), lambda copy: copy.start())

    def finish(self):
        def close(distance, lanes):
            self.arrival(distance, "x").wait_recv()
            self.each(distance, lanes, lambda copy: copy.wait_send())

        close(0, self.LANES)
        for k in range(1, self.last + 1):
            pl.when(self.z >= k)(functools.partial(close, -k, ("up", "x")))
            pl.when(self.z + k <= self.last)(functools.partial(close, k, ("down", "x")))


class Direct(Relay):
    def along(self, distance):
        return pltpu.make_async_remote_copy(
            src_ref=self.place(self.z * 2 + self.x),
            dst_ref=self.place(self.z * 2 + self.x),
            send_sem=self.sems.at[0, 0, distance + 3],
            recv_sem=self.sems.at[1, 0, 3 - distance],
            device_id={"dp": (self.z + distance) * 2 + self.x},
            device_id_type=MESH,
        )

    def reach(self, k, act):
        pl.when(self.z >= k)(functools.partial(act, -k))
        pl.when(self.z + k <= self.last)(functools.partial(act, k))

    def start(self):
        for k in range(1, self.last + 1):
            self.reach(k, lambda distance: self.along(distance).start())
        self.copy(0, "x").start()

    def hop(self, k):
        def pass_on(distance):
            self.arrival(distance, "up").wait_recv()
            self.copy(distance, "x").start()

        self.reach(k, pass_on)

    def finish(self):
        def close(distance):
            self.arrival(distance, "x").wait_recv()
            self.copy(distance, "x").wait_send()
            if isinstance(distance, int) and distance:
                self.along(distance).wait_send()

        close(0)
        for k in range(1, self.last + 1):
            self.reach(k, close)


def greet():
    me, workers = lax.axis_index("dp"), lax.axis_size("dp")
    barrier = pltpu.get_barrier_semaphore()
    peers = [1] + list(range(2, workers, 2))
    for bits in peers:
        pl.semaphore_signal(
            barrier, inc=1, device_id={"dp": lax.bitwise_xor(me, bits)}, device_id_type=MESH
        )
    pl.semaphore_wait(barrier, len(peers))


def lane_of(rows):
    return lax.broadcasted_iota(jnp.int32, (rows, LANES), 1)


def turned(value, cosine, sine_a, sine_b):
    return (
        value * cosine
        + pltpu.roll(value, LANES - ROT // 2, 1) * sine_a
        + pltpu.roll(value, ROT // 2, 1) * sine_b
    )


def norm_step(x, vec):
    mean = jnp.mean(x, 1, keepdims=True)
    shifted = x - mean
    normed = shifted * lax.rsqrt(jnp.mean(shifted * shifted, 1, keepdims=True) + EPSILON)
    return (
        (normed * vec[0:1, :] + vec[1:2, :]).astype(bf16),
        (normed * vec[2:3, :] + vec[3:4, :]).astype(bf16),
    )


def token_tables(seg_ref, cos_ref, sa_ref, sb_ref, key_aug, query_aug):
    segs = seg_ref[...]
    rows = segs.shape[1]
    half = ROT // 2
    position = lax.broadcasted_iota(jnp.int32, (1, rows), 1)
    for c in range(3):
        amount = jnp.sum(jnp.where(segs == c, 1, 0), 1, keepdims=True)
        position = position - jnp.where(segs > c, amount, 0)
    which = lax.broadcasted_iota(jnp.int32, (half, 1), 0)
    rate = jnp.zeros((half, 1), f32)
    for i in range(half):
        rate = jnp.where(which == i, 10000.0 ** (-2.0 * i / ROT), rate)
    angle = rate * position.astype(f32)
    values = jnp.concatenate([jnp.cos(angle), jnp.sin(angle)], 0)
    values = jnp.concatenate([part.astype(f32) for part in pieces(values)], 0).astype(bf16)
    source = lax.broadcasted_iota(jnp.int32, (3 * ROT, LANES), 0) & (ROT - 1)
    spot = lax.broadcasted_iota(jnp.int32, (3 * ROT, LANES), 1) & (HEAD_DIM - 1)
    hit = (spot & (half - 1)) == (source & (half - 1))
    pick = lambda low, high, sine, sign: jnp.where(
        hit & (spot >= low) & (spot < high) & ((source >= half) == sine), sign, 0.0
    ).astype(bf16)
    lane = lane_of(BLOCK) & (HEAD_DIM - 1)
    rest = jnp.where(lane < ROT, 0.0, 1.0)
    kinds = lax.broadcasted_iota(jnp.int32, (8, rows), 0)
    member = jnp.where(kinds == segs, 1.0, 0.0).astype(bf16)
    kind = lax.broadcasted_iota(jnp.int32, (8, LANES), 0)
    where = lax.broadcasted_iota(jnp.int32, (8, LANES), 1) & (HEAD_DIM - 1)
    key_pick = jnp.where((where >= 4) | (where == kind), 1.0, 0.0).astype(bf16)
    query_pick = jnp.where((where < 4) & (where != kind), -FAR, 0.0).astype(bf16)
    cos_pick = pick(0, ROT, False, 1.0)
    sa_pick, sb_pick = pick(0, half, True, -1.0), pick(half, ROT, True, 1.0)
    for part in range(rows // BLOCK):
        span = slice(part * BLOCK, (part + 1) * BLOCK)
        cos_ref[span, :] = dot(values[:, span], cos_pick, ROWS) + rest
        sa_ref[span, :] = dot(values[:, span], sa_pick, ROWS)
        sb_ref[span, :] = dot(values[:, span], sb_pick, ROWS)
        key_aug[span, :] = dot(member[:, span], key_pick, ROWS)
        query_aug[span, :] = dot(member[:, span], query_pick, ROWS)


FIRST = 3
UP = 4


def front_kernel(linked, *refs):
    (w_in_ref, w_out_ref, x_ref, g_ref, vec_ref, bias_ref, seg_ref, *refs) = refs
    (w_up_out, w_attn_out, one_out, two_out, att_out, gq_out, *refs) = refs
    part_outs, refs = refs[:4], refs[4:]
    (gup_out, hidden_out, gsum_ref,
     master_in, master_out, weights, tokens, cot, one, two, gq, att, gup, hidden,
     cos_ref, sa_ref, sb_ref, key_aug, query_aug, *attention_refs,
     load_sem, chunk_sem, store_sem, last_sem, slot_sem, part_sem, relay_sem) = refs
    rows, width = tokens.shape
    steps = rows // BLOCK
    local = weights.shape[2]
    quarters = gup.shape[0]
    copy = pltpu.make_async_copy
    at = lambda step: pl.ds(pl.multiple_of(step * BLOCK, BLOCK), BLOCK)

    loads = [copy(w_in_ref, master_in, load_sem.at[0]), copy(w_out_ref, master_out, load_sem.at[1])]
    if not linked:
        loads = [copy(w_in_ref, weights, load_sem.at[0])]
    for load in loads:
        load.start()
    load_x = lambda step: copy(x_ref.at[at(step)], tokens.at[at(step)], chunk_sem.at[0, step])
    load_g = lambda step: copy(g_ref.at[at(step)], cot.at[at(step)], chunk_sem.at[1, step])
    for step in range(steps):
        load_x(step).start()
    relays = []
    if linked:
        me = lax.axis_index("dp")
        depth = master_in.shape[1]
        shard = lambda w: pl.ds(pl.multiple_of(w * depth, depth), depth)
        for load in loads:
            load.wait()
        turned_out = lambda s: master_out[s * local : (s + 1) * local, :].T.astype(bf16)
        for s in range(FIRST):
            weights[s, shard(me), :] = master_in[s].astype(bf16)
        weights[FIRST, shard(me), :] = turned_out(0)
        greet()
        for index in range(1 + quarters):
            first, last = (0, UP) if index == 0 else (UP + 2 * (index - 1), UP + 2 * index)
            relays.append(
                (Direct if index else Relay)(lambda w, first=first, last=last: weights.at[first:last, shard(w), :], relay_sem.at[index])
            )
        relays[0].start()
        for s in range(quarters):
            weights[UP + 2 * s, shard(me), :] = master_in[FIRST + s].astype(bf16)
            weights[UP + 2 * s + 1, shard(me), :] = turned_out(1 + s)
    for step in range(steps):
        load_g(step).start()
    token_tables(seg_ref, cos_ref, sa_ref, sb_ref, key_aug, query_aug)

    store_one = lambda step: copy(one.at[at(step)], one_out.at[at(step)], store_sem.at[0, step])
    store_two = lambda step: copy(two.at[at(step)], two_out.at[at(step)], store_sem.at[1, step])

    @pl.loop(0, steps)
    def _(step):
        load_x(step).wait()
        one[at(step), :], two[at(step), :] = norm_step(tokens[at(step), :].astype(f32), vec_ref[...])
        store_one(step).start()
        store_two(step).start()
        if linked:
            for k in (1, 2, 3):
                @pl.when(step == 2 * k)
                def _(k=k):
                    relays[0].hop(k)
                    if k == 3:
                        for relay in relays[1:]:
                            relay.start()

    if linked:
        relays[0].finish()
    else:
        for load in loads:
            load.wait()
    store_attn = copy(weights.at[0:FIRST], w_attn_out, last_sem.at[0])
    store_attn.start()
    attention_stage(
        relays, weights, bias_ref, cot, one, gq, att, att_out, gq_out,
        (cos_ref, sa_ref, sb_ref), key_aug, query_aug, load_g, store_sem, *attention_refs,
    )
    final = copy(gq.at[0], gq_out.at[0], last_sem.at[1])
    final.start()

    gsum_ref[...] = jnp.zeros_like(gsum_ref)
    store_gup = [copy(gup.at[s], gup_out.at[s], slot_sem.at[0, s]) for s in range(quarters)]
    store_hidden = [copy(hidden.at[s], hidden_out.at[s], slot_sem.at[1, s]) for s in range(quarters)]
    store_up = [copy(weights.at[UP + 2 * s], w_up_out.at[s], slot_sem.at[2, s]) for s in range(quarters)]
    size = 2 * BLOCK
    span_of = lambda step: pl.ds(pl.multiple_of(step * size, size), size)
    for s in range(quarters):
        if linked:
            relays[1 + s].finish()
        store_up[s].start()

        @pl.loop(0, rows // size)
        def _(step, s=s):
            span = span_of(step)
            g = cot[span, :]
            up = dot(two[span, :], weights[UP + 2 * s]) + bias_ref[FIRST + s : FIRST + s + 1, :]
            grad_hidden = dot(g, weights[UP + 2 * s + 1])
            cdf, bell = normal_cdf(up)
            hidden[s, span, :] = (up * cdf).astype(bf16)
            gup[s, span, :] = (grad_hidden * (cdf + up * bell * 0.3989422804014327)).astype(bf16)
            if s == 0:
                gsum_ref[0:1, :] += jnp.sum(g.astype(f32), 0, keepdims=True)

        store_gup[s].start()
        store_hidden[s].start()

    @pl.loop(0, rows // size)
    def _(step):
        span = span_of(step)
        branch = dot(att[span, :], weights[FIRST], COLS)
        for s in range(quarters):
            branch = branch + dot(hidden[s, span, :], weights[UP + 2 * s + 1], COLS)
        tokens[span, :] = branch.astype(bf16)

    column = lax.axis_index("tensor")
    store_part = [
        copy(
            tokens.at[:, pl.ds(pl.multiple_of(lax.bitwise_xor(column, k) * local, local), local)],
            out, part_sem.at[k],
        )
        for k, out in enumerate(part_outs)
    ]
    for store in store_part:
        store.start()

    @pl.loop(0, steps)
    def _(step):
        store_one(step).wait()
        store_two(step).wait()
        copy(att.at[at(step)], att_out.at[at(step)], store_sem.at[2, step]).wait()
        copy(gq.at[1:3, at(step), :], gq_out.at[1:3, at(step), :], store_sem.at[3, step]).wait()

    for store in [store_attn, final] + store_gup + store_hidden + store_up + store_part:
        store.wait()


HOPS = (
    tuple((3, 1, k) for k in (1, 2, 3)) + tuple((6, 2, k) for k in (1, 2, 3)),
    tuple((1, 3, k) for k in (1, 2, 3)) + tuple((3, 4, k) for k in (1, 2, 3)),
)


def attention_stage(
    relays, weights, bias_ref, cot, one, gq, att, att_out, gq_out, tables_refs, key_aug, query_aug, load_g, store_sem,
    queries, keys, vals, grads, keys_t, turn,
):
    cos_ref, sa_ref, sb_ref = tables_refs
    rows = one.shape[0]
    steps = rows // BLOCK
    local = weights.shape[2]
    heads = local // HEAD_DIM
    copy = pltpu.make_async_copy
    at = lambda step: pl.ds(pl.multiple_of(step * BLOCK, BLOCK), BLOCK)

    def hops(stage, step):
        for when, which, k in HOPS[stage]:
            if relays:
                pl.when(step == when)(functools.partial(relays[which].hop, k))

    lane = lane_of(BLOCK)
    spot = lane & (HEAD_DIM - 1)
    low = lane < HEAD_DIM
    own_of = (low, lane >= HEAD_DIM)
    line = lambda dim: lax.broadcasted_iota(jnp.int32, (BLOCK, BLOCK), dim)
    load_att = lambda step: copy(att.at[at(step)], att_out.at[at(step)], store_sem.at[2, step])
    load_gq = lambda step: copy(gq.at[1:3, at(step), :], gq_out.at[1:3, at(step), :], store_sem.at[3, step])

    @pl.loop(0, steps)
    def _(step):
        hops(0, step)
        load_g(step).wait()
        row = pl.multiple_of(step * BLOCK, BLOCK)
        mine_rows = pl.ds(row, BLOCK)
        x = one[mine_rows, :]
        proj = [dot(x, weights[s]) + bias_ref[s : s + 1, :] for s in range(3)]
        grad_out = dot(cot[mine_rows, :], weights[FIRST]).astype(bf16).astype(f32)
        tables = cos_ref[mine_rows, :], sa_ref[mine_rows, :], sb_ref[mine_rows, :]
        for tile in range(heads // 2):
            cols = slice(tile * LANES, (tile + 1) * LANES)
            q = turned(proj[0][:, cols], *tables) * QUERY_SCALE
            k = turned(proj[1][:, cols], *tables)
            v = proj[2][:, cols]
            keys_t[cols, mine_rows] = k.astype(bf16).T
            for odd in range(2):
                own = own_of[odd]
                head = 2 * tile + odd
                queries[head, mine_rows, :] = jnp.where(own, q, query_aug[mine_rows, :]).astype(bf16)
                keys[head, mine_rows, :] = jnp.where(own, k, key_aug[mine_rows, :]).astype(bf16)
                vals[head, mine_rows, :] = jnp.where(own, v, 1.0).astype(bf16)

        def attend(blocks):
            for tile in range(heads // 2):
                cols = slice(tile * LANES, (tile + 1) * LANES)
                outs, logs = [], []
                for odd in range(2):
                    head = 2 * tile + odd
                    q = queries[head, mine_rows, :]
                    near = jnp.where(line(0) >= line(1), dot(q, keys[head, mine_rows, :], COLS), -FAR)
                    top = jnp.max(near, 1, keepdims=True)
                    if blocks > 1:
                        span = pl.ds(pl.multiple_of(row - (blocks - 1) * BLOCK, BLOCK), (blocks - 1) * BLOCK)
                        far = dot(q, keys[head, span, :], COLS)
                        top = jnp.maximum(top, jnp.max(far, 1, keepdims=True))
                    out = dot(jnp.exp2(near - top).astype(bf16), vals[head, mine_rows, :])
                    if blocks > 1:
                        out = out + dot(jnp.exp2(far - top).astype(bf16), vals[head, span, :])
                    outs.append(out / pltpu.roll(out, HEAD_DIM, 1))
                    logs.append(top + jnp.log2(out))
                out = jnp.where(low, outs[0], outs[1])
                att[mine_rows, cols] = out.astype(bf16)
                do = grad_out[:, cols]
                both = do * out
                for odd in range(2):
                    own = own_of[odd]
                    head = 2 * tile + odd
                    log_h = logs[odd].astype(bf16).astype(f32)
                    log_m = (logs[odd] - log_h).astype(bf16).astype(f32)
                    log_l = logs[odd] - log_h - log_m
                    parts = jnp.where(spot == 4, log_h, jnp.where(spot == 5, log_m, log_l))
                    taken = (~own) & (spot >= 4) & (spot < 7)
                    queries[head, mine_rows, :] = jnp.where(
                        taken, -parts, queries[head, mine_rows, :].astype(f32)
                    ).astype(bf16)
                    delta = jnp.sum(jnp.where(own, both, 0.0), 1, keepdims=True)
                    delta_h = delta.astype(bf16).astype(f32)
                    delta_m = (delta - delta_h).astype(bf16).astype(f32)
                    delta_l = delta - delta_h - delta_m
                    parts = jnp.where(
                        spot == 0, -delta_h, jnp.where(spot == 1, -delta_m, jnp.where(spot == 2, -delta_l, 0.0))
                    )
                    grads[head, mine_rows, :] = jnp.where(own, do, parts).astype(bf16)

        for blocks in range(1, MOST_BLOCKS + 1):
            pl.when(jnp.minimum(step + 1, MOST_BLOCKS) == blocks)(functools.partial(attend, blocks))
        load_att(step).start()

    turn[...] = jnp.zeros_like(turn)

    @pl.loop(0, steps)
    def _(back):
        hops(1, back)
        step = steps - 1 - back
        row = pl.multiple_of(step * BLOCK, BLOCK)
        mine_rows = pl.ds(row, BLOCK)
        tables = cos_ref[mine_rows, :], -sa_ref[mine_rows, :], -sb_ref[mine_rows, :]

        def attend(blocks):
            for tile in range(heads // 2):
                cols = slice(tile * LANES, (tile + 1) * LANES)
                results = []
                for odd in range(2):
                    head = 2 * tile + odd
                    turn_rows = slice(head * HEAD_DIM, (head + 1) * HEAD_DIM)
                    total = None
                    for first, size in ((0, 1), (1, blocks - 1)):
                        if size == 0:
                            continue
                        span = pl.ds(pl.multiple_of(row + first * BLOCK, BLOCK), size * BLOCK)
                        q, do = queries[head, span, :], grads[head, span, :]
                        p = jnp.exp2(dot(keys[head, mine_rows, :], q, COLS))
                        if first == 0:
                            p = jnp.where(line(0) <= line(1), p, 0.0)
                        ds = (p * dot(vals[head, mine_rows, :], do, COLS)).astype(bf16)
                        part = dot(ds, q), dot(p.astype(bf16), do)
                        total = part if total is None else (total[0] + part[0], total[1] + part[1])
                        turn[turn_rows, span] += dot(keys_t[turn_rows, mine_rows], ds)
                    results.append(total)
                dk = jnp.where(low, results[0][0], results[1][0]) * LN2
                gq[1, mine_rows, cols] = turned(dk, *tables).astype(bf16)
                gq[2, mine_rows, cols] = jnp.where(low, results[0][1], results[1][1]).astype(bf16)

        for blocks in range(1, MOST_BLOCKS + 1):
            pl.when(jnp.minimum(back + 1, MOST_BLOCKS) == blocks)(functools.partial(attend, blocks))
        load_gq(step).start()

    @pl.loop(0, steps)
    def _(step):
        mine_rows = at(step)
        for tile in range(heads // 2):
            cols = slice(tile * LANES, (tile + 1) * LANES)
            dq = turn[cols, mine_rows].T * 0.125
            gq[0, mine_rows, cols] = turned(
                dq, cos_ref[mine_rows, :], -sa_ref[mine_rows, :], -sb_ref[mine_rows, :]
            ).astype(bf16)


def front(linked, w_in, w_out, tokens, cot, vec, bias, segments):
    rows, width = tokens.shape
    local = bias.shape[1]
    heads = local // HEAD_DIM
    quarters = bias.shape[0] - FIRST
    steps = rows // BLOCK
    share = width // local
    anywhere = pl.BlockSpec(memory_space=pl.ANY)
    vmem = pl.BlockSpec(memory_space=pltpu.VMEM)
    shape = jax.ShapeDtypeStruct
    masters = [w_in.shape, w_out.shape] if linked else [(8, LANES), (8, LANES)]
    shard = lambda *dims: pltpu.VMEM(dims, bf16)
    return pl.pallas_call(
        functools.partial(front_kernel, linked),
        in_specs=[anywhere] * 4 + [vmem] * 3,
        out_specs=[anywhere] * (8 + share) + [vmem],
        out_shape=[
            shape((quarters, width, local), bf16), shape((FIRST, width, local), bf16),
            shape((rows, width), bf16), shape((rows, width), bf16),
            shape((rows, local), bf16), shape((3, rows, local), bf16),
        ]
        + [shape((rows, local), bf16)] * share
        + [shape((quarters, rows, local), bf16)] * 2
        + [shape((8, width), f32)],
        scratch_shapes=[
            pltpu.VMEM(masters[0], f32), pltpu.VMEM(masters[1], f32),
            shard(UP + 2 * quarters, width, local),
            shard(rows, width), shard(rows, width), shard(rows, width), shard(rows, width),
            shard(3, rows, local), shard(rows, local),
            shard(quarters, rows, local), shard(quarters, rows, local),
        ]
        + [pltpu.VMEM((rows, LANES), f32)] * 5
        + [shard(heads, rows, LANES)] * 4
        + [
            shard(local, rows), pltpu.VMEM((local, rows), f32),
            pltpu.SemaphoreType.DMA((2,)), pltpu.SemaphoreType.DMA((2, steps)),
            pltpu.SemaphoreType.DMA((4, steps)), pltpu.SemaphoreType.DMA((2,)),
            pltpu.SemaphoreType.DMA((3, quarters)), pltpu.SemaphoreType.DMA((share,)),
            pltpu.SemaphoreType.DMA((1 + quarters, 2, 3, 7)),
        ],
        compiler_params=params(60, collective_id=0, has_side_effects=True) if linked else params(60),
        name="front",
    )(w_in, w_out, tokens, cot, vec, bias, segments)


def normal_cdf(value):
    bell = jnp.exp2(value * value * (-0.5 * LOG2E))
    t = 1.0 / (1.0 + (0.3275911 / 1.4142135623730951) * jnp.abs(value))
    poly = 0.5 * 1.061405429
    for coefficient in (-1.453152027, 1.421413741, -0.284496736, 0.254829592):
        poly = poly * t + 0.5 * coefficient
    tail = poly * t * bell
    return jnp.where(value >= 0.0, 1.0 - tail, tail), bell


def norm_grad_kernel(
    gq_ref, gu_ref, wa_ref, wu_ref, x_ref, vec_ref, *refs
):
    *part_refs, stat_ref, vec_grad_ref, held = refs
    me = lax.axis_index("tensor")
    @pl.when(pl.program_id(0) == 0)
    def _():
        vec_grad_ref[...] = jnp.zeros_like(vec_grad_ref)

    x = x_ref[...].astype(f32)
    mean = jnp.mean(x, 1, keepdims=True)
    shifted = x - mean
    rstd = lax.rsqrt(jnp.mean(shifted * shifted, 1, keepdims=True) + EPSILON)
    normed = shifted * rstd
    local = gq_ref.shape[2]
    sums = dots = 0.0
    for c in range(len(part_refs)):
        cols = slice(c * local, (c + 1) * local)
        one = sum(dot(gq_ref[s], wa_ref[s, cols, :], COLS) for s in range(gq_ref.shape[0]))
        two = sum(dot(gu_ref[s], wu_ref[s, cols, :], COLS) for s in range(gu_ref.shape[0]))
        scaled = one * vec_ref[0:1, cols] + two * vec_ref[2:3, cols]
        held[lax.bitwise_xor(me, c)] = scaled.astype(bf16)
        sums = sums + jnp.sum(scaled, 1, keepdims=True)
        dots = dots + jnp.sum(scaled * normed[:, cols], 1, keepdims=True)
        vec_grad_ref[0:1, cols] += jnp.sum(one * normed[:, cols], 0, keepdims=True)
        vec_grad_ref[1:2, cols] += jnp.sum(one, 0, keepdims=True)
        vec_grad_ref[2:3, cols] += jnp.sum(two * normed[:, cols], 0, keepdims=True)
        vec_grad_ref[3:4, cols] += jnp.sum(two, 0, keepdims=True)
    for k, out in enumerate(part_refs):
        out[...] = held[k]
    lane = lane_of(x.shape[0])
    stats = jnp.where(lane == 0, sums, jnp.where(lane == 1, dots, jnp.where(lane == 2, mean, rstd)))
    stat_ref[...] = stats.T[0:8, :]


def norm_grad(grad_qkv, grad_up, w_attn, w_up, tokens, vec):
    rows, width = tokens.shape
    local = w_up.shape[2]
    share = width // local
    size = 2 * BLOCK
    block = lambda cols: pl.BlockSpec((size, cols), lambda i: (i, 0))
    slotted = lambda slots: pl.BlockSpec((slots, size, local), lambda i: (0, i, 0))
    return pl.pallas_call(
        norm_grad_kernel,
        grid=(rows // size,),
        in_specs=[
            slotted(3), slotted(w_up.shape[0]), full(w_attn.shape), full(w_up.shape),
            block(width), full(vec.shape),
        ],
        out_specs=[block(local)] * share + [pl.BlockSpec((8, size), lambda i: (0, i)), full((8, width))],
        scratch_shapes=[pltpu.VMEM((share, size, local), bf16)],
        out_shape=[jax.ShapeDtypeStruct((rows, local), bf16)] * share
        + [
            jax.ShapeDtypeStruct((8, rows), f32),
            jax.ShapeDtypeStruct((8, width), f32),
        ],
        compiler_params=params(),
        cost_estimate=pl.CostEstimate(
            flops=2 * rows * width * local * 7, bytes_accessed=8 * rows * width, transcendentals=0
        ),
        name="norm_grad",
    )(grad_qkv, grad_up, w_attn, w_up, tokens, vec)


def two_parts(value, high_ref, low_ref):
    high = value.astype(bf16)
    low = (value - high.astype(f32)).astype(bf16)
    high_ref[0], low_ref[0] = high, low
    return high, low


def clear_first(*refs):
    @pl.when(pl.program_id(0) == 0)
    def _():
        for ref in refs:
            ref[...] = jnp.zeros_like(ref)


def matrix_in_kernel(one_ref, two_ref, gq_ref, gu_ref, e_ref, q_ref, high_ref, low_ref, left_ref, bias_ref):
    clear_first(left_ref)
    slot = pl.program_id(0)

    def run(x_ref, grad_ref):
        grad = grad_ref[0]
        high, low = two_parts(dot(x_ref[...], grad, ROWS) + e_ref[0], high_ref, low_ref)
        q = stacked(q_ref[0])
        left_ref[...] += folded(dot(q, high, COLS)) + folded(dot(q, low, COLS))
        bias_ref[0] = jnp.sum(grad.astype(f32), 0, keepdims=True)

    pl.when(slot < 3)(lambda: run(one_ref, gq_ref))
    pl.when(slot >= 3)(lambda: run(two_ref, gu_ref))


def matrix_out_kernel(att_ref, hid_ref, g_ref, e_ref, q_ref, high_ref, low_ref, left_ref):
    clear_first(left_ref)
    slot = pl.program_id(0)

    def run(mixed):
        high, low = two_parts(dot(mixed, g_ref[...], ROWS) + e_ref[0], high_ref, low_ref)
        q = stacked(q_ref[0])
        left_ref[...] += folded(dot(q, high)) + folded(dot(q, low))

    pl.when(slot < 1)(lambda: run(att_ref[...]))
    pl.when(slot >= 1)(lambda: run(hid_ref[0]))


def slot_spec(shape, index=lambda i: i):
    return pl.BlockSpec((1,) + tuple(shape[1:]), lambda i: (index(i), 0, 0))


def matrix_in(norm_one, norm_two, grad_qkv, grad_up, error, q):
    slots, width, local = error.shape
    rows = norm_one.shape[0]
    big = jax.ShapeDtypeStruct(error.shape, bf16)
    return pl.pallas_call(
        matrix_in_kernel,
        grid=(slots,),
        in_specs=[
            full(norm_one.shape), full(norm_two.shape),
            slot_spec(grad_qkv.shape, lambda i: jnp.minimum(i, 2)),
            slot_spec(grad_up.shape, lambda i: jnp.maximum(i - 3, 0)),
            slot_spec(error.shape), slot_spec(q.shape),
        ],
        out_specs=[slot_spec(error.shape), slot_spec(error.shape), full((8, width)), slot_spec((slots, 1, local))],
        out_shape=[big, big, jax.ShapeDtypeStruct((8, width), f32), jax.ShapeDtypeStruct((slots, 1, local), f32)],
        compiler_params=params(),
        cost_estimate=pl.CostEstimate(
            flops=2 * slots * rows * width * local, bytes_accessed=10 * error.size, transcendentals=0
        ),
        name="matrix_in",
    )(norm_one, norm_two, grad_qkv, grad_up, error, q)


def matrix_out(att, hidden, cot, error, q):
    slots, local, width = error.shape
    rows = cot.shape[0]
    big = jax.ShapeDtypeStruct(error.shape, bf16)
    return pl.pallas_call(
        matrix_out_kernel,
        grid=(slots,),
        in_specs=[
            full(att.shape), slot_spec(hidden.shape, lambda i: jnp.maximum(i - 1, 0)), full(cot.shape),
            slot_spec(error.shape), slot_spec(q.shape),
        ],
        out_specs=[slot_spec(error.shape), slot_spec(error.shape), full((8, width))],
        out_shape=[big, big, jax.ShapeDtypeStruct((8, width), f32)],
        compiler_params=params(),
        cost_estimate=pl.CostEstimate(
            flops=2 * slots * rows * width * local, bytes_accessed=10 * error.size, transcendentals=0
        ),
        name="matrix_out",
    )(att, hidden, cot, error, q)


def orthonormal_rows(matrix):
    index = lax.broadcasted_iota(jnp.int32, (matrix.shape[0], 1), 0)
    for r in range(matrix.shape[0]):
        row = matrix[r : r + 1, :]
        row = row * lax.rsqrt(jnp.sum(row * row, 1, keepdims=True) + 1e-06)
        along = jnp.sum(matrix * row, 1, keepdims=True)
        matrix = jnp.where(index == r, row, jnp.where(index > r, matrix - along * row, matrix))
    return matrix


def basis_kernel(left_in_ref, left_out_ref, basis_in_ref, basis_out_ref):
    basis_in_ref[...] = orthonormal_rows(left_in_ref[...])
    basis_out_ref[...] = orthonormal_rows(left_out_ref[...])


def bases(left_in, left_out):
    shape = jax.ShapeDtypeStruct(left_in.shape, f32)
    return pl.pallas_call(
        basis_kernel, out_shape=[shape, shape], compiler_params=params(), name="bases"
    )(left_in, left_out)


def right_kernel(dims, basis_ref, high_ref, low_ref, out_ref):
    basis = stacked(basis_ref[...])
    out_ref[0] = folded(dot(basis, high_ref[0], dims)) + folded(dot(basis, low_ref[0], dims))


def right_factor(basis, matrix, dims, columns):
    slots = matrix[0].shape[0]
    return pl.pallas_call(
        functools.partial(right_kernel, dims),
        grid=(slots,),
        in_specs=[full(basis.shape), slot_spec(matrix[0].shape), slot_spec(matrix[1].shape)],
        out_specs=pl.BlockSpec((1, 8, columns), lambda i: (i, 0, 0)),
        out_shape=jax.ShapeDtypeStruct((slots, 8, columns), f32),
        compiler_params=params(),
        cost_estimate=pl.CostEstimate(flops=0, bytes_accessed=matrix[0].size * 4, transcendentals=0),
        name="right_factor",
    )(basis, *matrix)


def outer(a, b):
    ah, am, al = (part.astype(f32) for part in pieces(a))
    bh, bm, bl = (part.astype(f32) for part in pieces(b))
    left = jnp.concatenate([ah, ah, am, ah, am, al], 0).astype(bf16)
    right = jnp.concatenate([bh, bm, bh, bl, bm, bh], 0).astype(bf16)
    return dot(left, right, ROWS)


def finish_kernel(
    basis_in_ref, basis_out_ref, own_ref, bundle_ref, vec_ref, vec_mom_ref, bias_ref, bias_mom_ref,
    mi_ref, mo_ref, momi_ref, momo_ref, wi_ref, wo_ref,
    ei_out, eo_out, momi_out, momo_out, wi_out, wo_out,
    vec_out, vec_mom_out, bias_out, bias_mom_out, right_in_out, right_out_out,
    mi, mo, momi, momo, wi, wo, load_sem, store_sem,
):
    copy = pltpu.make_async_copy
    slots_in, slots_out = mi.shape[0], mo.shape[0]
    local = vec_mom_ref.shape[1]
    work = []
    for s in range(slots_in + slots_out):
        wide = s < slots_in
        slot = s if wide else s - slots_in
        group = ((mi_ref, mi, ei_out), (momi_ref, momi, momi_out), (wi_ref, wi, wi_out)) if wide else (
            (mo_ref, mo, eo_out), (momo_ref, momo, momo_out), (wo_ref, wo, wo_out))
        work.append(
            (wide, slot,
             [copy(src.at[slot], held.at[slot], load_sem.at[s, n]) for n, (src, held, _) in enumerate(group)],
             [copy(held.at[slot], out.at[slot], store_sem.at[s, n]) for n, (_, held, out) in enumerate(group)])
        )
    for _, _, loads, _ in work:
        for load in loads:
            load.start()
    basis_in, basis_out = basis_in_ref[...], basis_out_ref[...]
    own_in, own_out = own_ref[0:8, :], own_ref[8:16, :]
    first_bias, first_out, first_vec, _ = bundle_rows(slots_in, slots_out)
    start = pl.ds(pl.multiple_of(lax.axis_index("tensor") * local, local), local)
    mom = MOMENTUM_DECAY * vec_mom_ref[...] + bundle_ref[first_vec : first_vec + vec_mom_ref.shape[0], :]
    vec_mom_out[...] = mom
    vec_out[...] = vec_ref[:, start] - VECTOR_RATE * mom
    mom = MOMENTUM_DECAY * bias_mom_ref[...] + bundle_ref[first_bias : first_bias + slots_in, :]
    bias_mom_out[...] = mom
    bias_out[...] = bias_ref[...] - VECTOR_RATE * mom
    for wide, slot, loads, stores in work:
        right = bundle_ref[8 * slot : 8 * slot + 8, :] if wide else bundle_ref[
            first_out + 8 * slot : first_out + 8 * slot + 8, :]
        if wide:
            right_in_out[slot] = right
        else:
            right_out_out[slot] = right
        matrix, momentum, master = (mi, momi, wi) if wide else (mo, momo, wo)
        pair = (lambda b: outer(b, right)) if wide else (lambda b: outer(right, b))
        for load in loads:
            load.wait()
        matrix[slot] = matrix[slot] - pair(basis_in if wide else basis_out)
        stores[0].start()
        mom = MOMENTUM_DECAY * momentum[slot] + pair(own_in if wide else own_out)
        momentum[slot] = mom
        master[slot] = master[slot] - LEARN_RATE * mom
        stores[1].start()
        stores[2].start()
    for _, _, _, stores in work:
        for store in stores:
            store.wait()


def finish(basis_in, basis_out, own, bundle, vec, vec_mom, bias, bias_mom, *matrices):
    anywhere = pl.BlockSpec(memory_space=pl.ANY)
    vmem = pl.BlockSpec(memory_space=pltpu.VMEM)
    like = lambda a: jax.ShapeDtypeStruct(a.shape, f32)
    slots_in, slots_out = matrices[0].shape[0], matrices[1].shape[0]
    local = vec_mom.shape[1]
    return pl.pallas_call(
        finish_kernel,
        in_specs=[vmem] * 8 + [anywhere] * 6,
        out_specs=[anywhere] * 6 + [vmem] * 6,
        out_shape=[like(a) for a in matrices]
        + [like(vec_mom), like(vec_mom), like(bias_mom), like(bias_mom)]
        + [jax.ShapeDtypeStruct((slots, 8, local), f32) for slots in (slots_in, slots_out)],
        scratch_shapes=[pltpu.VMEM(a.shape, f32) for a in matrices]
        + [pltpu.SemaphoreType.DMA((slots_in + slots_out, 3)), pltpu.SemaphoreType.DMA((slots_in + slots_out, 3))],
        compiler_params=params(),
        name="finish",
    )(basis_in, basis_out, own, bundle, vec, vec_mom, bias, bias_mom, *matrices)


def trade(axis, send, take, sems):
    me, size = lax.axis_index(axis), lax.axis_size(axis)
    copies = []
    for k in range(1, size):
        peer = lax.bitwise_xor(me, k)
        copies.append(
            pltpu.make_async_remote_copy(
                src_ref=send(peer, k), dst_ref=take(peer, k),
                send_sem=sems.at[0, k], recv_sem=sems.at[1, k],
                device_id={axis: peer}, device_id_type=MESH,
            )
        )
    for copy in copies:
        copy.start()
    return copies


def bundle_rows(slots_in, slots_out):
    biases = slots_in * 8
    outputs = 64 * pl.cdiv(biases + slots_in, 64)
    vectors = outputs + slots_out * 8
    return biases, outputs, vectors, outputs + 64 * pl.cdiv(slots_out * 8 + 8, 64)


def back_kernel(
    one_ref, two_ref, g_ref, gq_ref, gu_ref, att_ref, hid_ref, ei_ref, eo_ref,
    branch_pair, branch_far, branch_both, grad_pair, grad_far, grad_both, stat_ref,
    qi_ref, qo_ref, vec_ref, gsum_ref,
    branch_near_out, branch_far_out, grad_near_out, grad_far_out, stats_out, mi_out, mo_out,
    basis_in_ref, basis_out_ref, own_ref, bundle_ref,
    one, two, cot, gq, gu, att, hid, mi, mo, left, left_take, left_sum, vec_take, bundle, bundle_take, bundle_sum,
    sums, sum_take,
    load_sem, slot_sem, store_sem, link_sem, tensor_sem, stat_sem, pair_sem, pair_load_sem,
):
    copy = pltpu.make_async_copy
    me, column = lax.axis_index("dp"), lax.axis_index("tensor")
    workers, parts = lax.axis_size("dp"), lax.axis_size("tensor")
    slots_in, width, local = mi.shape
    slots_out = mo.shape[0]
    lanes = width // workers
    first_bias, first_out, first_vec, end = bundle_rows(slots_in, slots_out)

    barrier = pltpu.get_barrier_semaphore()
    for axis, size in (("dp", workers), ("tensor", parts)):
        for k in range(1, size):
            peer = lax.bitwise_xor(lax.axis_index(axis), k)
            pl.semaphore_signal(barrier, inc=1, device_id={axis: peer}, device_id_type=MESH)
    loads = {
        name: copy(src, dst, load_sem.at[index])
        for index, (name, src, dst) in enumerate(
            (("g", g_ref, cot), ("att", att_ref, att), ("one", one_ref, one), ("gq", gq_ref, gq), ("two", two_ref, two))
        )
    }
    load_hid = [copy(hid_ref.at[s], hid.at[s], slot_sem.at[0, s]) for s in range(slots_out - 1)]
    load_gu = [copy(gu_ref.at[s], gu.at[s], slot_sem.at[1, s]) for s in range(slots_in - 3)]
    load_mo = [copy(eo_ref.at[s], mo.at[s], slot_sem.at[2, s]) for s in range(slots_out)]
    load_mi = [copy(ei_ref.at[s], mi.at[s], slot_sem.at[3, s]) for s in range(slots_in)]
    store_mo = [copy(mo.at[s], mo_out.at[s], store_sem.at[0, s]) for s in range(slots_out)]
    store_mi = [copy(mi.at[s], mi_out.at[s], store_sem.at[1, s]) for s in range(slots_in)]
    sibling, opposite = lax.bitwise_xor(column, 1), lax.bitwise_xor(column, 2)

    def pass_to(peer, src, dst, index):
        return pltpu.make_async_remote_copy(
            src_ref=src, dst_ref=dst, send_sem=pair_sem.at[0, index], recv_sem=pair_sem.at[1, index],
            device_id={"tensor": peer}, device_id_type=MESH,
        )

    exchanges = []
    for n, (pair, far, both, near_out, far_out) in enumerate(
        ((branch_pair, branch_far, branch_both, branch_near_out, branch_far_out),
         (grad_pair, grad_far, grad_both, grad_near_out, grad_far_out))
    ):
        exchanges.append(
            (copy(far, sums.at[n], pair_load_sem.at[n]),
             pass_to(sibling, both, sum_take.at[n], 3 * n),
             pass_to(sibling, pair, near_out, 3 * n + 1),
             pass_to(opposite, sums.at[n], far_out, 3 * n + 2))
        )
    for load, _, _, _ in exchanges:
        load.start()
    loads["g"].start()
    loads["att"].start()
    load_mo[0].start()
    pl.semaphore_wait(barrier, workers + parts - 2)
    block = lambda index: pl.ds(pl.multiple_of(index * local, local), local)
    vec_copies = trade(
        "tensor", lambda peer, k: vec_ref.at[:, block(peer)], lambda peer, k: vec_take.at[k], tensor_sem
    )
    stat_copies = trade("tensor", lambda peer, k: stat_ref, lambda peer, k: stats_out.at[k - 1], stat_sem)
    for _, first, _, _ in exchanges:
        first.start()
    for _, _, second, _ in exchanges:
        second.start()
    for s in range(1, slots_out):
        load_hid[s - 1].start()
        load_mo[s].start()
    loads["one"].start()
    loads["gq"].start()
    for s in range(3):
        load_mi[s].start()
    loads["two"].start()
    for s in range(3, slots_in):
        load_gu[s - 3].start()
        load_mi[s].start()

    def send_sums(n):
        load, first, _, last = exchanges[n]
        load.wait()
        first.wait()
        sums[n] = (sums[n].astype(f32) + sum_take[n].astype(f32)).astype(bf16)
        last.start()

    part = lambda index: pl.ds(pl.multiple_of(index * lanes, lanes), lanes)
    sides = (pl.ds(0, 8), pl.ds(8, 8))
    bundles = ((0, first_out // workers), (first_out, (end - first_out) // workers))

    def left_send(n):
        return trade(
            "dp", lambda peer, k: left.at[sides[n], part(peer)], lambda peer, k: left_take.at[n, k], link_sem.at[0, n]
        )

    def left_spread(n, copies):
        for c in copies:
            c.wait()
        value = left[sides[n], part(me)]
        for k in range(1, workers):
            value = value + left_take[n, k]
        left_sum[sides[n], part(me)] = value / workers
        mine = left_sum.at[sides[n], part(me)]
        return trade("dp", lambda peer, k: mine, lambda peer, k: mine, link_sem.at[1, n])

    def basis_of(n, copies, basis_ref):
        for c in copies:
            c.wait()
        basis_ref[...] = orthonormal_rows(left_sum[sides[n], :])
        own_ref[sides[n], :] = basis_ref[:, part(me)]
        return stacked(basis_ref[...])

    def lot(n, index):
        start, size = bundles[n]
        return pl.ds(pl.multiple_of(start + index * size, size), size)

    def right_send(n):
        return trade(
            "dp", lambda peer, k: bundle.at[lot(n, peer), :],
            lambda peer, k: bundle_take.at[n, k], link_sem.at[2, n],
        )

    def right_spread(n, copies):
        for c in copies:
            c.wait()
        value = bundle[lot(n, me), :]
        for k in range(1, workers):
            value = value + bundle_take[n, k]
        bundle_sum[lot(n, me), :] = value / workers
        mine = bundle_sum.at[lot(n, me), :]
        return trade("dp", lambda peer, k: mine, lambda peer, k: mine, link_sem.at[3, n])

    bundle[...] = jnp.zeros_like(bundle)
    total = jnp.zeros((8, width), f32)
    loads["g"].wait()
    loads["att"].wait()
    for s in range(slots_out):
        if s:
            load_hid[s - 1].wait()
        if s == 1:
            send_sums(0)
        if s == 2:
            send_sums(1)
        load_mo[s].wait()
        value = dot(hid[s - 1] if s else att[...], cot[...], ROWS) + mo[s]
        mo[s] = value
        store_mo[s].start()
        high, low, _ = pieces(value)
        q = stacked(qo_ref[s])
        total = total + folded(dot(q, high)) + folded(dot(q, low))
    left[8:16, :] = total
    out_left = left_send(1)
    total = jnp.zeros((8, width), f32)
    loads["one"].wait()
    loads["gq"].wait()
    for s in range(slots_in):
        if s == 3:
            loads["two"].wait()
        if s >= 3:
            load_gu[s - 3].wait()
        if s == slots_in - 2:
            out_left = left_spread(1, out_left)
        load_mi[s].wait()
        grad = gq[s] if s < 3 else gu[s - 3]
        value = dot(one[...] if s < 3 else two[...], grad, ROWS) + mi[s]
        mi[s] = value
        store_mi[s].start()
        high, low, _ = pieces(value)
        q = stacked(qi_ref[s])
        total = total + folded(dot(q, high, COLS)) + folded(dot(q, low, COLS))
        bundle[first_bias + s : first_bias + s + 1, :] = jnp.sum(grad.astype(f32), 0, keepdims=True)
    left[0:8, :] = total
    in_left = left_send(0)

    side = basis_of(1, out_left, basis_out_ref)
    for s in range(slots_out):
        high, low, _ = pieces(mo[s])
        row = first_out + 8 * s
        bundle[row : row + 8, :] = folded(dot(side, high, COLS)) + folded(dot(side, low, COLS))
    for c in vec_copies:
        c.wait()
    vec = vec_ref[:, block(column)]
    for k in range(1, parts):
        vec = vec + vec_take[k]
    rows8 = lax.broadcasted_iota(jnp.int32, (8, local), 0)
    bundle[first_vec : first_vec + 8, :] = jnp.where(
        rows8 < 4, vec, jnp.where(rows8 == 4, gsum_ref[0:1, block(column)], 0.0)
    )
    in_left = left_spread(0, in_left)
    out_right = right_send(1)
    side = basis_of(0, in_left, basis_in_ref)
    for s in range(slots_in):
        if s == 3:
            out_right = right_spread(1, out_right)
        high, low, _ = pieces(mi[s])
        bundle[8 * s : 8 * s + 8, :] = folded(dot(side, high)) + folded(dot(side, low))
    in_right = right_spread(0, right_send(0))
    for c in out_right + in_right:
        c.wait()
    bundle_ref[...] = bundle_sum[...]
    for store in store_mo + store_mi:
        store.wait()
    for c in stat_copies:
        c.wait()
    for _, _, second, last in exchanges:
        second.wait()
        last.wait()


def back(norm_one, norm_two, cot, grad_qkv, grad_up, att, hidden, error_in, error_out, branch, grad, stats,
    q_in, q_out, vec, gsum):
    slots_in, width, local = error_in.shape
    slots_out = error_out.shape[0]
    workers, parts = lax.axis_size("dp"), lax.axis_size("tensor")
    anywhere = pl.BlockSpec(memory_space=pl.ANY)
    vmem = pl.BlockSpec(memory_space=pltpu.VMEM)
    shape = jax.ShapeDtypeStruct
    rows = bundle_rows(slots_in, slots_out)[-1]
    group = rows // 2 // workers
    like = lambda a: pltpu.VMEM(a.shape, a.dtype)
    return pl.pallas_call(
        back_kernel,
        in_specs=[anywhere] * 16 + [vmem] * 4,
        out_specs=[anywhere] * 7 + [vmem] * 4,
        out_shape=[shape(branch[0].shape, bf16)] * 4 + [
            shape((parts - 1,) + stats.shape, f32),
            shape(error_in.shape, f32), shape(error_out.shape, f32),
            shape((8, width), f32), shape((8, width), f32), shape((16, width // workers), f32),
            shape((rows, local), f32),
        ],
        scratch_shapes=[
            like(a) for a in (norm_one, norm_two, cot, grad_qkv, grad_up, att, hidden, error_in, error_out)
        ] + [
            pltpu.VMEM((16, width), f32), pltpu.VMEM((2, workers, 8, width // workers), f32),
            pltpu.VMEM((16, width), f32), pltpu.VMEM((parts, 8, local), f32),
            pltpu.VMEM((rows, local), f32), pltpu.VMEM((2, workers, group, local), f32), pltpu.VMEM((rows, local), f32),
            pltpu.VMEM((2,) + branch[0].shape, bf16), pltpu.VMEM((2,) + branch[0].shape, bf16),
            pltpu.SemaphoreType.DMA((5,)), pltpu.SemaphoreType.DMA((4, slots_in)),
            pltpu.SemaphoreType.DMA((2, slots_in)), pltpu.SemaphoreType.DMA((4, 2, 2, workers)),
            pltpu.SemaphoreType.DMA((2, parts)), pltpu.SemaphoreType.DMA((2, parts)),
            pltpu.SemaphoreType.DMA((2, 6)), pltpu.SemaphoreType.DMA((2,)),
        ],
        compiler_params=params(collective_id=1, has_side_effects=True),
        name="back",
    )(norm_one, norm_two, cot, grad_qkv, grad_up, att, hidden, error_in, error_out,
      *branch[1:], *grad[1:], stats, q_in, q_out, vec, gsum)


def ends_kernel(column_ref, x_ref, g_ref, bias_ref, *refs):
    *refs, out_ref, in_grad_ref = refs
    branch, grad, stats = refs[:3], refs[3:6], refs[6:]
    total = lambda parts: sum(part[...].astype(f32) for part in parts)
    x = x_ref[...].astype(f32)
    out_ref[...] = (x + total(branch) + bias_ref[...]).astype(bf16)
    own = stats[0][...].T
    means = total(stats).T / (len(stats) * x.shape[1])
    normed = (x - own[:, 2:3]) * own[:, 3:4]
    in_grad_ref[...] = g_ref[...].astype(f32) + own[:, 3:4] * (total(grad) - means[:, 0:1] - normed * means[:, 1:2])


def ends(column, tokens, cot, bias, branch, grad, stats):
    rows, local = branch[0].shape
    size = 4 * BLOCK
    block = pl.BlockSpec((size, local), lambda i, column: (i, 0))
    mine = pl.BlockSpec((size, local), lambda i, column: (i, column[0]))
    stat = pl.BlockSpec((8, size), lambda i, column: (0, i))
    return pl.pallas_call(
        ends_kernel,
        grid_spec=pltpu.PrefetchScalarGridSpec(
            num_scalar_prefetch=1,
            grid=(rows // size,),
            in_specs=[mine, mine, pl.BlockSpec((1, local), lambda i, column: (0, column[0]))]
            + [block] * (len(branch) + len(grad)) + [stat] * len(stats),
            out_specs=[block, block],
        ),
        out_shape=[jax.ShapeDtypeStruct((rows, local), bf16), jax.ShapeDtypeStruct((rows, local), f32)],
        compiler_params=params(),
        name="ends",
    )(column[None], tokens, cot, bias, *branch, *grad, *stats)


def swapped(value, axis, bits):
    size = lax.axis_size(axis)
    return lax.ppermute(value, axis, [(i, i ^ bits) for i in range(size)])


def spread(parts):
    return [parts[0]] + [swapped(part, "tensor", k) for k, part in enumerate(parts) if k]


def on_device(
    tokens, cotangent, segments, w_in_master, w_out_master, vec_master, bias_in_master,
    w_in_mom, w_out_mom, vec_mom, bias_in_mom, w_in_error, w_out_error, q_in, q_out,
):
    workers = lax.axis_size("dp")
    tensor_index = lax.axis_index("tensor")
    worker_index = lax.axis_index("dp")
    rows, width = tokens.shape
    local = bias_in_master.shape[1]
    start_col = tensor_index * local
    cut = lambda a: lax.dynamic_slice_in_dim(a, start_col, local, 1)

    w_in = w_in_master.transpose(1, 0, 2)
    linked = workers == 8
    if linked:
        shards = w_in, w_out_master.reshape(5 * local, -1)
    else:
        w_in_low = lax.all_gather(w_in.astype(bf16), "dp", axis=1, tiled=True)
        w_out_low = lax.all_gather(w_out_master.astype(bf16), "dp", axis=2, tiled=True).transpose(0, 2, 1)
        pairs = jnp.stack([w_in_low[FIRST:], w_out_low[1:]], 1).reshape(-1, width, local)
        shards = jnp.concatenate([w_in_low[:FIRST], w_out_low[:1], pairs], 0), w_out_master.reshape(5 * local, -1)
    w_up, w_attn, norm_one, norm_two, att, grad_qkv, *branch_parts, grad_up, hidden, cot_sum = front(
        linked, *shards, tokens, cotangent, vec_master, bias_in_master, segments
    )

    factors_in, factors_out = q_in.transpose(0, 2, 1), q_out.transpose(0, 2, 1)
    error_in = w_in_error[0].transpose(1, 0, 2)
    error_out = w_out_error[0]
    *grad_parts, stats, vec_local = norm_grad(grad_qkv, grad_up, w_attn, w_up, tokens, vec_master)

    if linked:
        (
            branch_near, branch_far, grad_near, grad_far, far_stats,
            matrix_in_f32, matrix_out_f32, basis_in, basis_out, own, bundle,
        ) = back(
            norm_one, norm_two, cotangent, grad_qkv, grad_up, att, hidden, error_in, error_out,
            branch_parts, grad_parts, stats, factors_in, factors_out, vec_local, cot_sum,
        )
        branch = branch_parts[0], branch_near, branch_far
        grad = grad_parts[0], grad_near, grad_far
        stats = [stats] + [far_stats[k] for k in range(3)]
    else:
        branch, grad = (
            (parts[0], swapped(parts[1], "tensor", 1), swapped(parts[2], "tensor", 2) + swapped(parts[3], "tensor", 3))
            for parts in (branch_parts, grad_parts)
        )
        stats = spread([stats] * 4)
        *parts_out, left_out = matrix_out(att, hidden, cotangent, error_out, factors_out)
        *parts_in, left_in, bias_local = matrix_in(norm_one, norm_two, grad_qkv, grad_up, error_in, factors_in)
        left = lax.psum(jnp.concatenate([left_in, left_out], 0), "dp") / workers
        basis_in, basis_out = bases(left[:8], left[8:])
        vec_rows = cut(jnp.concatenate([lax.psum(vec_local[:4], "tensor"), cot_sum[:1]], 0))
        bundle = jnp.zeros((bundle_rows(7, 5)[-1], local), f32)
        for start, rows_of in zip(
            (0,) + bundle_rows(7, 5)[:3],
            (
                right_factor(basis_in, parts_in, PLAIN, local).reshape(-1, local), bias_local[:, 0, :],
                right_factor(basis_out, parts_out, COLS, local).reshape(-1, local), vec_rows,
            ),
        ):
            bundle = lax.dynamic_update_slice_in_dim(bundle, rows_of, start, 0)
        bundle = lax.psum(bundle, "dp") / workers
        matrix_in_f32, matrix_out_f32 = (
            high.astype(f32) + low.astype(f32) for high, low in (parts_in, parts_out)
        )
        owned = w_in.shape[1]
        own = jnp.concatenate([basis_in, basis_out], 0)
        own = lax.dynamic_slice_in_dim(own, worker_index * owned, owned, 1)
    (
        new_error_in, new_error_out, new_mom_in, new_mom_out, new_w_in, new_w_out,
        vec_new, vec_mom_new, bias_in_new, bias_in_mom_new, right_in, right_out,
    ) = finish(
        basis_in, basis_out, own, bundle, vec_master, vec_mom, bias_in_master, bias_in_mom,
        matrix_in_f32, matrix_out_f32, w_in_mom.transpose(1, 0, 2), w_out_mom, w_in, w_out_master,
    )
    block_out, input_grad = ends(
        tensor_index, tokens, cotangent, vec_master[4:5], branch, grad, stats
    )
    return (
        block_out,
        input_grad,
        new_w_in.transpose(1, 0, 2),
        new_w_out,
        vec_new,
        bias_in_new,
        new_mom_in.transpose(1, 0, 2),
        new_mom_out,
        vec_mom_new,
        bias_in_mom_new,
        new_error_in.transpose(1, 0, 2)[None],
        new_error_out[None],
        right_in.transpose(0, 2, 1),
        right_out.transpose(0, 2, 1),
    )


def solution(mesh):
    return jax.shard_map(
        on_device,
        mesh=mesh,
        in_specs=(
            P("dp", None), P("dp", None), P("dp", None), P("dp", None, "tensor"),
            P(None, "tensor", "dp"), P(), P(None, "tensor"), P("dp", None, "tensor"),
            P(None, "tensor", "dp"), P(None, "tensor"), P(None, "tensor"),
            P("dp", None, None, "tensor"), P("dp", None, "tensor", None),
            P(None, "tensor", None), P(None, "tensor", None),
        ),
        out_specs=(
            P("dp", "tensor"), P("dp", "tensor"), P("dp", None, "tensor"), P(None, "tensor", "dp"),
            P(None, "tensor"), P(None, "tensor"), P("dp", None, "tensor"), P(None, "tensor", "dp"),
            P(None, "tensor"), P(None, "tensor"), P("dp", None, None, "tensor"),
            P("dp", None, "tensor", None), P(None, "tensor", None), P(None, "tensor", None),
        ),
        check_vma=False,
    )
```

```python
import functools

import jax
import jax.numpy as jnp
from jax import lax
from jax.experimental import pallas as pl
from jax.experimental.pallas import tpu as pltpu
from jax.sharding import PartitionSpec as P

HEAD_DIM = 64
ROT = 16
EPSILON = 1e-05
MOMENTUM_DECAY = 0.9
LEARN_RATE = 0.05
VECTOR_RATE = 0.05
LN2 = 0.6931471805599453
LOG2E = 1.4426950408889634
QUERY_SCALE = 0.125 * LOG2E
FAR = 2.0**30
BLOCK = 256
LANES = 128
MOST_BLOCKS = 5

f32 = jnp.float32
bf16 = jnp.bfloat16
ROWS = (((0,), (0,)), ((), ()))
COLS = (((1,), (1,)), ((), ()))
PLAIN = (((1,), (0,)), ((), ()))
MESH = pl.DeviceIdType.MESH


def dot(a, b, dims=PLAIN):
    return lax.dot_general(a, b, dims, preferred_element_type=f32)


def params(megabytes=56, **more):
    return pltpu.CompilerParams(vmem_limit_bytes=megabytes * 1024 * 1024, **more)


def pieces(value):
    high = value.astype(bf16)
    rest = value - high.astype(f32)
    middle = rest.astype(bf16)
    low = (rest - middle.astype(f32)).astype(bf16)
    return high, middle, low


def stacked(value):
    return jnp.concatenate([part.astype(f32) for part in pieces(value)], 0).astype(bf16)


def folded(total, rows=8):
    return total[:rows] + total[rows : 2 * rows] + total[2 * rows : 3 * rows]


def full(shape):
    return pl.BlockSpec(shape, lambda i: (0,) * len(shape))


class Relay:
    LANES = ("up", "down", "x")

    def __init__(self, place, sems):
        self.place, self.sems = place, sems
        me = lax.axis_index("dp")
        self.z, self.x = lax.div(me, 2), lax.rem(me, 2)
        self.last = lax.axis_size("dp") // 2 - 1

    def copy(self, distance, lane):
        index = self.LANES.index(lane)
        step = (1, -1, 0)[index]
        worker = (self.z + distance) * 2 + self.x
        to = (self.z + step) * 2 + (1 - self.x if lane == "x" else self.x)
        return pltpu.make_async_remote_copy(
            src_ref=self.place(worker),
            dst_ref=self.place(worker),
            send_sem=self.sems.at[0, index, distance + 3],
            recv_sem=self.sems.at[1, index, distance - step + 3],
            device_id={"dp": to},
            device_id_type=MESH,
        )

    def arrival(self, distance, lane):
        index = self.LANES.index(lane)
        ref = self.place((self.z + distance) * 2 + (1 - self.x if lane == "x" else self.x))
        return pltpu.make_async_remote_copy(
            src_ref=ref,
            dst_ref=ref,
            send_sem=self.sems.at[0, index, 3],
            recv_sem=self.sems.at[1, index, distance + 3],
            device_id={"dp": self.z * 2 + 1 - self.x},
            device_id_type=MESH,
        )

    def each(self, distance, lanes, act):
        for lane in lanes:
            run = functools.partial(act, self.copy(distance, lane))
            if lane == "up":
                pl.when(self.z < self.last)(run)
            elif lane == "down":
                pl.when(self.z > 0)(run)
            else:
                run()

    def start(self):
        self.each(0, self.LANES, lambda copy: copy.start())

    def hop(self, k):
        @pl.when(self.z >= k)
        def _():
            self.arrival(-k, "up").wait_recv()
            self.each(-k, ("up", "x"), lambda copy: copy.start())

        @pl.when(self.z + k <= self.last)
        def _():
            self.arrival(k, "down").wait_recv()
            self.each(k, ("down", "x"), lambda copy: copy.start())

    def finish(self):
        def close(distance, lanes):
            self.arrival(distance, "x").wait_recv()
            self.each(distance, lanes, lambda copy: copy.wait_send())

        close(0, self.LANES)
        for k in range(1, self.last + 1):
            pl.when(self.z >= k)(functools.partial(close, -k, ("up", "x")))
            pl.when(self.z + k <= self.last)(functools.partial(close, k, ("down", "x")))


class Direct(Relay):
    def along(self, distance):
        return pltpu.make_async_remote_copy(
            src_ref=self.place(self.z * 2 + self.x),
            dst_ref=self.place(self.z * 2 + self.x),
            send_sem=self.sems.at[0, 0, distance + 3],
            recv_sem=self.sems.at[1, 0, 3 - distance],
            device_id={"dp": (self.z + distance) * 2 + self.x},
            device_id_type=MESH,
        )

    def reach(self, k, act):
        pl.when(self.z >= k)(functools.partial(act, -k))
        pl.when(self.z + k <= self.last)(functools.partial(act, k))

    def start(self):
        for k in range(1, self.last + 1):
            self.reach(k, lambda distance: self.along(distance).start())
        self.copy(0, "x").start()

    def hop(self, k):
        def pass_on(distance):
            self.arrival(distance, "up").wait_recv()
            self.copy(distance, "x").start()

        self.reach(k, pass_on)

    def finish(self):
        def close(distance):
            self.arrival(distance, "x").wait_recv()
            self.copy(distance, "x").wait_send()
            if isinstance(distance, int) and distance:
                self.along(distance).wait_send()

        close(0)
        for k in range(1, self.last + 1):
            self.reach(k, close)


def greet():
    me, workers = lax.axis_index("dp"), lax.axis_size("dp")
    barrier = pltpu.get_barrier_semaphore()
    peers = [1] + list(range(2, workers, 2))
    for bits in peers:
        pl.semaphore_signal(
            barrier, inc=1, device_id={"dp": lax.bitwise_xor(me, bits)}, device_id_type=MESH
        )
    pl.semaphore_wait(barrier, len(peers))


def lane_of(rows):
    return lax.broadcasted_iota(jnp.int32, (rows, LANES), 1)


def turned(value, cosine, sine_a, sine_b):
    return (
        value * cosine
        + pltpu.roll(value, LANES - ROT // 2, 1) * sine_a
        + pltpu.roll(value, ROT // 2, 1) * sine_b
    )


def norm_step(x, vec):
    mean = jnp.mean(x, 1, keepdims=True)
    shifted = x - mean
    normed = shifted * lax.rsqrt(jnp.mean(shifted * shifted, 1, keepdims=True) + EPSILON)
    return (
        (normed * vec[0:1, :] + vec[1:2, :]).astype(bf16),
        (normed * vec[2:3, :] + vec[3:4, :]).astype(bf16),
    )


def token_tables(seg_ref, cos_ref, sa_ref, sb_ref, key_aug, query_aug):
    segs = seg_ref[...]
    rows = segs.shape[1]
    half = ROT // 2
    position = lax.broadcasted_iota(jnp.int32, (1, rows), 1)
    for c in range(3):
        amount = jnp.sum(jnp.where(segs == c, 1, 0), 1, keepdims=True)
        position = position - jnp.where(segs > c, amount, 0)
    which = lax.broadcasted_iota(jnp.int32, (half, 1), 0)
    rate = jnp.zeros((half, 1), f32)
    for i in range(half):
        rate = jnp.where(which == i, 10000.0 ** (-2.0 * i / ROT), rate)
    angle = rate * position.astype(f32)
    values = jnp.concatenate([jnp.cos(angle), jnp.sin(angle)], 0)
    values = jnp.concatenate([part.astype(f32) for part in pieces(values)], 0).astype(bf16)
    source = lax.broadcasted_iota(jnp.int32, (3 * ROT, LANES), 0) & (ROT - 1)
    spot = lax.broadcasted_iota(jnp.int32, (3 * ROT, LANES), 1) & (HEAD_DIM - 1)
    hit = (spot & (half - 1)) == (source & (half - 1))
    pick = lambda low, high, sine, sign: jnp.where(
        hit & (spot >= low) & (spot < high) & ((source >= half) == sine), sign, 0.0
    ).astype(bf16)
    lane = lane_of(BLOCK) & (HEAD_DIM - 1)
    rest = jnp.where(lane < ROT, 0.0, 1.0)
    kinds = lax.broadcasted_iota(jnp.int32, (8, rows), 0)
    member = jnp.where(kinds == segs, 1.0, 0.0).astype(bf16)
    kind = lax.broadcasted_iota(jnp.int32, (8, LANES), 0)
    where = lax.broadcasted_iota(jnp.int32, (8, LANES), 1) & (HEAD_DIM - 1)
    key_pick = jnp.where((where >= 4) | (where == kind), 1.0, 0.0).astype(bf16)
    query_pick = jnp.where((where < 4) & (where != kind), -FAR, 0.0).astype(bf16)
    cos_pick = pick(0, ROT, False, 1.0)
    sa_pick, sb_pick = pick(0, half, True, -1.0), pick(half, ROT, True, 1.0)
    for part in range(rows // BLOCK):
        span = slice(part * BLOCK, (part + 1) * BLOCK)
        cos_ref[span, :] = dot(values[:, span], cos_pick, ROWS) + rest
        sa_ref[span, :] = dot(values[:, span], sa_pick, ROWS)
        sb_ref[span, :] = dot(values[:, span], sb_pick, ROWS)
        key_aug[span, :] = dot(member[:, span], key_pick, ROWS)
        query_aug[span, :] = dot(member[:, span], query_pick, ROWS)


FIRST = 3
UP = 4


def front_kernel(linked, *refs):
    (w_in_ref, w_out_ref, x_ref, g_ref, vec_ref, bias_ref, seg_ref, *refs) = refs
    (w_up_out, w_attn_out, one_out, two_out, att_out, gq_out, *refs) = refs
    part_outs, refs = refs[:4], refs[4:]
    (gup_out, hidden_out, gsum_ref,
     master_in, master_out, weights, tokens, cot, one, two, gq, att, gup, hidden,
     cos_ref, sa_ref, sb_ref, key_aug, query_aug, *attention_refs,
     load_sem, chunk_sem, store_sem, last_sem, slot_sem, part_sem, relay_sem) = refs
    rows, width = tokens.shape
    steps = rows // BLOCK
    local = weights.shape[2]
    quarters = gup.shape[0]
    copy = pltpu.make_async_copy
    at = lambda step: pl.ds(pl.multiple_of(step * BLOCK, BLOCK), BLOCK)

    loads = [copy(w_in_ref, master_in, load_sem.at[0]), copy(w_out_ref, master_out, load_sem.at[1])]
    if not linked:
        loads = [copy(w_in_ref, weights, load_sem.at[0])]
    for load in loads:
        load.start()
    load_x = lambda step: copy(x_ref.at[at(step)], tokens.at[at(step)], chunk_sem.at[0, step])
    load_g = lambda step: copy(g_ref.at[at(step)], cot.at[at(step)], chunk_sem.at[1, step])
    for step in range(steps):
        load_x(step).start()
    relays = []
    if linked:
        me = lax.axis_index("dp")
        depth = master_in.shape[1]
        shard = lambda w: pl.ds(pl.multiple_of(w * depth, depth), depth)
        for load in loads:
            load.wait()
        turned_out = lambda s: master_out[s * local : (s + 1) * local, :].T.astype(bf16)
        for s in range(FIRST):
            weights[s, shard(me), :] = master_in[s].astype(bf16)
        weights[FIRST, shard(me), :] = turned_out(0)
        greet()
        for index in range(1 + quarters):
            first, last = (0, UP) if index == 0 else (UP + 2 * (index - 1), UP + 2 * index)
            relays.append(
                (Direct if index else Relay)(lambda w, first=first, last=last: weights.at[first:last, shard(w), :], relay_sem.at[index])
            )
        relays[0].start()
        for s in range(quarters):
            weights[UP + 2 * s, shard(me), :] = master_in[FIRST + s].astype(bf16)
            weights[UP + 2 * s + 1, shard(me), :] = turned_out(1 + s)
    for step in range(steps):
        load_g(step).start()
    token_tables(seg_ref, cos_ref, sa_ref, sb_ref, key_aug, query_aug)

    store_one = lambda step: copy(one.at[at(step)], one_out.at[at(step)], store_sem.at[0, step])
    store_two = lambda step: copy(two.at[at(step)], two_out.at[at(step)], store_sem.at[1, step])

    @pl.loop(0, steps)
    def _(step):
        load_x(step).wait()
        one[at(step), :], two[at(step), :] = norm_step(tokens[at(step), :].astype(f32), vec_ref[...])
        store_one(step).start()
        store_two(step).start()
        if linked:
            for k in (1, 2, 3):
                @pl.when(step == 2 * k)
                def _(k=k):
                    relays[0].hop(k)
                    if k == 3:
                        for relay in relays[1:]:
                            relay.start()

    if linked:
        relays[0].finish()
    else:
        for load in loads:
            load.wait()
    store_attn = copy(weights.at[0:FIRST], w_attn_out, last_sem.at[0])
    store_attn.start()
    attention_stage(
        relays, weights, bias_ref, cot, one, gq, att, att_out, gq_out,
        (cos_ref, sa_ref, sb_ref), key_aug, query_aug, load_g, store_sem, *attention_refs,
    )
    final = copy(gq.at[0], gq_out.at[0], last_sem.at[1])
    final.start()

    gsum_ref[...] = jnp.zeros_like(gsum_ref)
    store_gup = [copy(gup.at[s], gup_out.at[s], slot_sem.at[0, s]) for s in range(quarters)]
    store_hidden = [copy(hidden.at[s], hidden_out.at[s], slot_sem.at[1, s]) for s in range(quarters)]
    store_up = [copy(weights.at[UP + 2 * s], w_up_out.at[s], slot_sem.at[2, s]) for s in range(quarters)]
    size = 2 * BLOCK
    span_of = lambda step: pl.ds(pl.multiple_of(step * size, size), size)
    for s in range(quarters):
        if linked:
            relays[1 + s].finish()
        store_up[s].start()

        @pl.loop(0, rows // size)
        def _(step, s=s):
            span = span_of(step)
            g = cot[span, :]
            up = dot(two[span, :], weights[UP + 2 * s]) + bias_ref[FIRST + s : FIRST + s + 1, :]
            grad_hidden = dot(g, weights[UP + 2 * s + 1])
            cdf, bell = normal_cdf(up)
            hidden[s, span, :] = (up * cdf).astype(bf16)
            gup[s, span, :] = (grad_hidden * (cdf + up * bell * 0.3989422804014327)).astype(bf16)
            if s == 0:
                gsum_ref[0:1, :] += jnp.sum(g.astype(f32), 0, keepdims=True)

        store_gup[s].start()
        store_hidden[s].start()

    @pl.loop(0, rows // size)
    def _(step):
        span = span_of(step)
        branch = dot(att[span, :], weights[FIRST], COLS)
        for s in range(quarters):
            branch = branch + dot(hidden[s, span, :], weights[UP + 2 * s + 1], COLS)
        tokens[span, :] = branch.astype(bf16)

    column = lax.axis_index("tensor")
    store_part = [
        copy(
            tokens.at[:, pl.ds(pl.multiple_of(lax.bitwise_xor(column, k) * local, local), local)],
            out, part_sem.at[k],
        )
        for k, out in enumerate(part_outs)
    ]
    for store in store_part:
        store.start()

    @pl.loop(0, steps)
    def _(step):
        store_one(step).wait()
        store_two(step).wait()
        copy(att.at[at(step)], att_out.at[at(step)], store_sem.at[2, step]).wait()
        copy(gq.at[1:3, at(step), :], gq_out.at[1:3, at(step), :], store_sem.at[3, step]).wait()

    for store in [store_attn, final] + store_gup + store_hidden + store_up + store_part:
        store.wait()


HOPS = (
    tuple((3, 1, k) for k in (1, 2, 3)) + tuple((6, 2, k) for k in (1, 2, 3)),
    tuple((1, 3, k) for k in (1, 2, 3)) + tuple((3, 4, k) for k in (1, 2, 3)),
)


def attention_stage(
    relays, weights, bias_ref, cot, one, gq, att, att_out, gq_out, tables_refs, key_aug, query_aug, load_g, store_sem,
    queries, keys, vals, grads, keys_t, turn,
):
    cos_ref, sa_ref, sb_ref = tables_refs
    rows = one.shape[0]
    steps = rows // BLOCK
    local = weights.shape[2]
    heads = local // HEAD_DIM
    copy = pltpu.make_async_copy
    at = lambda step: pl.ds(pl.multiple_of(step * BLOCK, BLOCK), BLOCK)

    def hops(stage, step):
        for when, which, k in HOPS[stage]:
            if relays:
                pl.when(step == when)(functools.partial(relays[which].hop, k))

    lane = lane_of(BLOCK)
    spot = lane & (HEAD_DIM - 1)
    low = lane < HEAD_DIM
    own_of = (low, lane >= HEAD_DIM)
    line = lambda dim: lax.broadcasted_iota(jnp.int32, (BLOCK, BLOCK), dim)
    load_att = lambda step: copy(att.at[at(step)], att_out.at[at(step)], store_sem.at[2, step])
    load_gq = lambda step: copy(gq.at[1:3, at(step), :], gq_out.at[1:3, at(step), :], store_sem.at[3, step])

    @pl.loop(0, steps)
    def _(step):
        hops(0, step)
        load_g(step).wait()
        row = pl.multiple_of(step * BLOCK, BLOCK)
        mine_rows = pl.ds(row, BLOCK)
        x = one[mine_rows, :]
        proj = [dot(x, weights[s]) + bias_ref[s : s + 1, :] for s in range(3)]
        grad_out = dot(cot[mine_rows, :], weights[FIRST]).astype(bf16).astype(f32)
        tables = cos_ref[mine_rows, :], sa_ref[mine_rows, :], sb_ref[mine_rows, :]
        for tile in range(heads // 2):
            cols = slice(tile * LANES, (tile + 1) * LANES)
            q = turned(proj[0][:, cols], *tables) * QUERY_SCALE
            k = turned(proj[1][:, cols], *tables)
            v = proj[2][:, cols]
            keys_t[cols, mine_rows] = k.astype(bf16).T
            for odd in range(2):
                own = own_of[odd]
                head = 2 * tile + odd
                queries[head, mine_rows, :] = jnp.where(own, q, query_aug[mine_rows, :]).astype(bf16)
                keys[head, mine_rows, :] = jnp.where(own, k, key_aug[mine_rows, :]).astype(bf16)
                vals[head, mine_rows, :] = jnp.where(own, v, 1.0).astype(bf16)

        def attend(blocks):
            for tile in range(heads // 2):
                cols = slice(tile * LANES, (tile + 1) * LANES)
                outs, logs = [], []
                for odd in range(2):
                    head = 2 * tile + odd
                    q = queries[head, mine_rows, :]
                    near = jnp.where(line(0) >= line(1), dot(q, keys[head, mine_rows, :], COLS), -FAR)
                    top = jnp.max(near, 1, keepdims=True)
                    if blocks > 1:
                        span = pl.ds(pl.multiple_of(row - (blocks - 1) * BLOCK, BLOCK), (blocks - 1) * BLOCK)
                        far = dot(q, keys[head, span, :], COLS)
                        top = jnp.maximum(top, jnp.max(far, 1, keepdims=True))
                    out = dot(jnp.exp2(near - top).astype(bf16), vals[head, mine_rows, :])
                    if blocks > 1:
                        out = out + dot(jnp.exp2(far - top).astype(bf16), vals[head, span, :])
                    outs.append(out / pltpu.roll(out, HEAD_DIM, 1))
                    logs.append(top + jnp.log2(out))
                out = jnp.where(low, outs[0], outs[1])
                att[mine_rows, cols] = out.astype(bf16)
                do = grad_out[:, cols]
                both = do * out
                for odd in range(2):
                    own = own_of[odd]
                    head = 2 * tile + odd
                    log_h = logs[odd].astype(bf16).astype(f32)
                    log_m = (logs[odd] - log_h).astype(bf16).astype(f32)
                    log_l = logs[odd] - log_h - log_m
                    parts = jnp.where(spot == 4, log_h, jnp.where(spot == 5, log_m, log_l))
                    taken = (~own) & (spot >= 4) & (spot < 7)
                    queries[head, mine_rows, :] = jnp.where(
                        taken, -parts, queries[head, mine_rows, :].astype(f32)
                    ).astype(bf16)
                    delta = jnp.sum(jnp.where(own, both, 0.0), 1, keepdims=True)
                    delta_h = delta.astype(bf16).astype(f32)
                    delta_m = (delta - delta_h).astype(bf16).astype(f32)
                    delta_l = delta - delta_h - delta_m
                    parts = jnp.where(
                        spot == 0, -delta_h, jnp.where(spot == 1, -delta_m, jnp.where(spot == 2, -delta_l, 0.0))
                    )
                    grads[head, mine_rows, :] = jnp.where(own, do, parts).astype(bf16)

        for blocks in range(1, MOST_BLOCKS + 1):
            pl.when(jnp.minimum(step + 1, MOST_BLOCKS) == blocks)(functools.partial(attend, blocks))
        load_att(step).start()

    turn[...] = jnp.zeros_like(turn)

    @pl.loop(0, steps)
    def _(back):
        hops(1, back)
        step = steps - 1 - back
        row = pl.multiple_of(step * BLOCK, BLOCK)
        mine_rows = pl.ds(row, BLOCK)
        tables = cos_ref[mine_rows, :], -sa_ref[mine_rows, :], -sb_ref[mine_rows, :]

        def attend(blocks):
            for tile in range(heads // 2):
                cols = slice(tile * LANES, (tile + 1) * LANES)
                results = []
                for odd in range(2):
                    head = 2 * tile + odd
                    turn_rows = slice(head * HEAD_DIM, (head + 1) * HEAD_DIM)
                    total = None
                    for first, size in ((0, 1), (1, blocks - 1)):
                        if size == 0:
                            continue
                        span = pl.ds(pl.multiple_of(row + first * BLOCK, BLOCK), size * BLOCK)
                        q, do = queries[head, span, :], grads[head, span, :]
                        p = jnp.exp2(dot(keys[head, mine_rows, :], q, COLS))
                        if first == 0:
                            p = jnp.where(line(0) <= line(1), p, 0.0)
                        ds = (p * dot(vals[head, mine_rows, :], do, COLS)).astype(bf16)
                        part = dot(ds, q), dot(p.astype(bf16), do)
                        total = part if total is None else (total[0] + part[0], total[1] + part[1])
                        turn[turn_rows, span] += dot(keys_t[turn_rows, mine_rows], ds)
                    results.append(total)
                dk = jnp.where(low, results[0][0], results[1][0]) * LN2
                gq[1, mine_rows, cols] = turned(dk, *tables).astype(bf16)
                gq[2, mine_rows, cols] = jnp.where(low, results[0][1], results[1][1]).astype(bf16)

        for blocks in range(1, MOST_BLOCKS + 1):
            pl.when(jnp.minimum(back + 1, MOST_BLOCKS) == blocks)(functools.partial(attend, blocks))
        load_gq(step).start()

    @pl.loop(0, steps)
    def _(step):
        mine_rows = at(step)
        for tile in range(heads // 2):
            cols = slice(tile * LANES, (tile + 1) * LANES)
            dq = turn[cols, mine_rows].T * 0.125
            gq[0, mine_rows, cols] = turned(
                dq, cos_ref[mine_rows, :], -sa_ref[mine_rows, :], -sb_ref[mine_rows, :]
            ).astype(bf16)


def front(linked, w_in, w_out, tokens, cot, vec, bias, segments):
    rows, width = tokens.shape
    local = bias.shape[1]
    heads = local // HEAD_DIM
    quarters = bias.shape[0] - FIRST
    steps = rows // BLOCK
    share = width // local
    anywhere = pl.BlockSpec(memory_space=pl.ANY)
    vmem = pl.BlockSpec(memory_space=pltpu.VMEM)
    shape = jax.ShapeDtypeStruct
    masters = [w_in.shape, w_out.shape] if linked else [(8, LANES), (8, LANES)]
    shard = lambda *dims: pltpu.VMEM(dims, bf16)
    return pl.pallas_call(
        functools.partial(front_kernel, linked),
        in_specs=[anywhere] * 4 + [vmem] * 3,
        out_specs=[anywhere] * (8 + share) + [vmem],
        out_shape=[
            shape((quarters, width, local), bf16), shape((FIRST, width, local), bf16),
            shape((rows, width), bf16), shape((rows, width), bf16),
            shape((rows, local), bf16), shape((3, rows, local), bf16),
        ]
        + [shape((rows, local), bf16)] * share
        + [shape((quarters, rows, local), bf16)] * 2
        + [shape((8, width), f32)],
        scratch_shapes=[
            pltpu.VMEM(masters[0], f32), pltpu.VMEM(masters[1], f32),
            shard(UP + 2 * quarters, width, local),
            shard(rows, width), shard(rows, width), shard(rows, width), shard(rows, width),
            shard(3, rows, local), shard(rows, local),
            shard(quarters, rows, local), shard(quarters, rows, local),
        ]
        + [pltpu.VMEM((rows, LANES), f32)] * 5
        + [shard(heads, rows, LANES)] * 4
        + [
            shard(local, rows), pltpu.VMEM((local, rows), f32),
            pltpu.SemaphoreType.DMA((2,)), pltpu.SemaphoreType.DMA((2, steps)),
            pltpu.SemaphoreType.DMA((4, steps)), pltpu.SemaphoreType.DMA((2,)),
            pltpu.SemaphoreType.DMA((3, quarters)), pltpu.SemaphoreType.DMA((share,)),
            pltpu.SemaphoreType.DMA((1 + quarters, 2, 3, 7)),
        ],
        compiler_params=params(60, collective_id=0, has_side_effects=True) if linked else params(60),
        name="front",
    )(w_in, w_out, tokens, cot, vec, bias, segments)


def normal_cdf(value):
    bell = jnp.exp2(value * value * (-0.5 * LOG2E))
    t = 1.0 / (1.0 + (0.3275911 / 1.4142135623730951) * jnp.abs(value))
    poly = 0.5 * 1.061405429
    for coefficient in (-1.453152027, 1.421413741, -0.284496736, 0.254829592):
        poly = poly * t + 0.5 * coefficient
    tail = poly * t * bell
    return jnp.where(value >= 0.0, 1.0 - tail, tail), bell


def norm_grad_kernel(
    gq_ref, gu_ref, wa_ref, wu_ref, x_ref, vec_ref, *refs
):
    *part_refs, stat_ref, vec_grad_ref, held = refs
    me = lax.axis_index("tensor")
    @pl.when(pl.program_id(0) == 0)
    def _():
        vec_grad_ref[...] = jnp.zeros_like(vec_grad_ref)

    x = x_ref[...].astype(f32)
    mean = jnp.mean(x, 1, keepdims=True)
    shifted = x - mean
    rstd = lax.rsqrt(jnp.mean(shifted * shifted, 1, keepdims=True) + EPSILON)
    normed = shifted * rstd
    local = gq_ref.shape[2]
    sums = dots = 0.0
    for c in range(len(part_refs)):
        cols = slice(c * local, (c + 1) * local)
        one = sum(dot(gq_ref[s], wa_ref[s, cols, :], COLS) for s in range(gq_ref.shape[0]))
        two = sum(dot(gu_ref[s], wu_ref[s, cols, :], COLS) for s in range(gu_ref.shape[0]))
        scaled = one * vec_ref[0:1, cols] + two * vec_ref[2:3, cols]
        held[lax.bitwise_xor(me, c)] = scaled.astype(bf16)
        sums = sums + jnp.sum(scaled, 1, keepdims=True)
        dots = dots + jnp.sum(scaled * normed[:, cols], 1, keepdims=True)
        vec_grad_ref[0:1, cols] += jnp.sum(one * normed[:, cols], 0, keepdims=True)
        vec_grad_ref[1:2, cols] += jnp.sum(one, 0, keepdims=True)
        vec_grad_ref[2:3, cols] += jnp.sum(two * normed[:, cols], 0, keepdims=True)
        vec_grad_ref[3:4, cols] += jnp.sum(two, 0, keepdims=True)
    for k, out in enumerate(part_refs):
        out[...] = held[k]
    lane = lane_of(x.shape[0])
    stats = jnp.where(lane == 0, sums, jnp.where(lane == 1, dots, jnp.where(lane == 2, mean, rstd)))
    stat_ref[...] = stats.T[0:8, :]


def norm_grad(grad_qkv, grad_up, w_attn, w_up, tokens, vec):
    rows, width = tokens.shape
    local = w_up.shape[2]
    share = width // local
    size = 2 * BLOCK
    block = lambda cols: pl.BlockSpec((size, cols), lambda i: (i, 0))
    slotted = lambda slots: pl.BlockSpec((slots, size, local), lambda i: (0, i, 0))
    return pl.pallas_call(
        norm_grad_kernel,
        grid=(rows // size,),
        in_specs=[
            slotted(3), slotted(w_up.shape[0]), full(w_attn.shape), full(w_up.shape),
            block(width), full(vec.shape),
        ],
        out_specs=[block(local)] * share + [pl.BlockSpec((8, size), lambda i: (0, i)), full((8, width))],
        scratch_shapes=[pltpu.VMEM((share, size, local), bf16)],
        out_shape=[jax.ShapeDtypeStruct((rows, local), bf16)] * share
        + [
            jax.ShapeDtypeStruct((8, rows), f32),
            jax.ShapeDtypeStruct((8, width), f32),
        ],
        compiler_params=params(),
        cost_estimate=pl.CostEstimate(
            flops=2 * rows * width * local * 7, bytes_accessed=8 * rows * width, transcendentals=0
        ),
        name="norm_grad",
    )(grad_qkv, grad_up, w_attn, w_up, tokens, vec)


def two_parts(value, high_ref, low_ref):
    high = value.astype(bf16)
    low = (value - high.astype(f32)).astype(bf16)
    high_ref[0], low_ref[0] = high, low
    return high, low


def clear_first(*refs):
    @pl.when(pl.program_id(0) == 0)
    def _():
        for ref in refs:
            ref[...] = jnp.zeros_like(ref)


def matrix_in_kernel(one_ref, two_ref, gq_ref, gu_ref, e_ref, q_ref, high_ref, low_ref, left_ref, bias_ref):
    clear_first(left_ref)
    slot = pl.program_id(0)

    def run(x_ref, grad_ref):
        grad = grad_ref[0]
        high, low = two_parts(dot(x_ref[...], grad, ROWS) + e_ref[0], high_ref, low_ref)
        q = stacked(q_ref[0])
        left_ref[...] += folded(dot(q, high, COLS)) + folded(dot(q, low, COLS))
        bias_ref[0] = jnp.sum(grad.astype(f32), 0, keepdims=True)

    pl.when(slot < 3)(lambda: run(one_ref, gq_ref))
    pl.when(slot >= 3)(lambda: run(two_ref, gu_ref))


def matrix_out_kernel(att_ref, hid_ref, g_ref, e_ref, q_ref, high_ref, low_ref, left_ref):
    clear_first(left_ref)
    slot = pl.program_id(0)

    def run(mixed):
        high, low = two_parts(dot(mixed, g_ref[...], ROWS) + e_ref[0], high_ref, low_ref)
        q = stacked(q_ref[0])
        left_ref[...] += folded(dot(q, high)) + folded(dot(q, low))

    pl.when(slot < 1)(lambda: run(att_ref[...]))
    pl.when(slot >= 1)(lambda: run(hid_ref[0]))


def slot_spec(shape, index=lambda i: i):
    return pl.BlockSpec((1,) + tuple(shape[1:]), lambda i: (index(i), 0, 0))


def matrix_in(norm_one, norm_two, grad_qkv, grad_up, error, q):
    slots, width, local = error.shape
    rows = norm_one.shape[0]
    big = jax.ShapeDtypeStruct(error.shape, bf16)
    return pl.pallas_call(
        matrix_in_kernel,
        grid=(slots,),
        in_specs=[
            full(norm_one.shape), full(norm_two.shape),
            slot_spec(grad_qkv.shape, lambda i: jnp.minimum(i, 2)),
            slot_spec(grad_up.shape, lambda i: jnp.maximum(i - 3, 0)),
            slot_spec(error.shape), slot_spec(q.shape),
        ],
        out_specs=[slot_spec(error.shape), slot_spec(error.shape), full((8, width)), slot_spec((slots, 1, local))],
        out_shape=[big, big, jax.ShapeDtypeStruct((8, width), f32), jax.ShapeDtypeStruct((slots, 1, local), f32)],
        compiler_params=params(),
        cost_estimate=pl.CostEstimate(
            flops=2 * slots * rows * width * local, bytes_accessed=10 * error.size, transcendentals=0
        ),
        name="matrix_in",
    )(norm_one, norm_two, grad_qkv, grad_up, error, q)


def matrix_out(att, hidden, cot, error, q):
    slots, local, width = error.shape
    rows = cot.shape[0]
    big = jax.ShapeDtypeStruct(error.shape, bf16)
    return pl.pallas_call(
        matrix_out_kernel,
        grid=(slots,),
        in_specs=[
            full(att.shape), slot_spec(hidden.shape, lambda i: jnp.maximum(i - 1, 0)), full(cot.shape),
            slot_spec(error.shape), slot_spec(q.shape),
        ],
        out_specs=[slot_spec(error.shape), slot_spec(error.shape), full((8, width))],
        out_shape=[big, big, jax.ShapeDtypeStruct((8, width), f32)],
        compiler_params=params(),
        cost_estimate=pl.CostEstimate(
            flops=2 * slots * rows * width * local, bytes_accessed=10 * error.size, transcendentals=0
        ),
        name="matrix_out",
    )(att, hidden, cot, error, q)


def orthonormal_rows(matrix):
    index = lax.broadcasted_iota(jnp.int32, (matrix.shape[0], 1), 0)
    for r in range(matrix.shape[0]):
        row = matrix[r : r + 1, :]
        row = row * lax.rsqrt(jnp.sum(row * row, 1, keepdims=True) + 1e-06)
        along = jnp.sum(matrix * row, 1, keepdims=True)
        matrix = jnp.where(index == r, row, jnp.where(index > r, matrix - along * row, matrix))
    return matrix


def basis_kernel(left_in_ref, left_out_ref, basis_in_ref, basis_out_ref):
    basis_in_ref[...] = orthonormal_rows(left_in_ref[...])
    basis_out_ref[...] = orthonormal_rows(left_out_ref[...])


def bases(left_in, left_out):
    shape = jax.ShapeDtypeStruct(left_in.shape, f32)
    return pl.pallas_call(
        basis_kernel, out_shape=[shape, shape], compiler_params=params(), name="bases"
    )(left_in, left_out)


def right_kernel(dims, basis_ref, high_ref, low_ref, out_ref):
    basis = stacked(basis_ref[...])
    out_ref[0] = folded(dot(basis, high_ref[0], dims)) + folded(dot(basis, low_ref[0], dims))


def right_factor(basis, matrix, dims, columns):
    slots = matrix[0].shape[0]
    return pl.pallas_call(
        functools.partial(right_kernel, dims),
        grid=(slots,),
        in_specs=[full(basis.shape), slot_spec(matrix[0].shape), slot_spec(matrix[1].shape)],
        out_specs=pl.BlockSpec((1, 8, columns), lambda i: (i, 0, 0)),
        out_shape=jax.ShapeDtypeStruct((slots, 8, columns), f32),
        compiler_params=params(),
        cost_estimate=pl.CostEstimate(flops=0, bytes_accessed=matrix[0].size * 4, transcendentals=0),
        name="right_factor",
    )(basis, *matrix)


def outer(a, b):
    ah, am, al = (part.astype(f32) for part in pieces(a))
    bh, bm, bl = (part.astype(f32) for part in pieces(b))
    left = jnp.concatenate([ah, ah, am, ah, am, al], 0).astype(bf16)
    right = jnp.concatenate([bh, bm, bh, bl, bm, bh], 0).astype(bf16)
    return dot(left, right, ROWS)


def finish_kernel(
    basis_in_ref, basis_out_ref, own_ref, bundle_ref, vec_ref, vec_mom_ref, bias_ref, bias_mom_ref,
    stat_ref, far_ref, x_ref, g_ref, *refs,
):
    part_refs, refs = refs[:6], refs[6:]
    (
        mi_ref, mo_ref, momi_ref, momo_ref, wi_ref, wo_ref,
        ei_out, eo_out, momi_out, momo_out, wi_out, wo_out, out_out, in_grad_out,
        vec_out, vec_mom_out, bias_out, bias_mom_out, right_in_out, right_out_out,
        mi, mo, momi, momo, wi, wo, cols, out, in_grad, load_sem, store_sem, cols_sem, ends_sem,
    ) = refs
    copy = pltpu.make_async_copy
    slots_in, slots_out = mi.shape[0], mo.shape[0]
    work = []
    for s in range(slots_in + slots_out):
        wide = s < slots_in
        slot = s if wide else s - slots_in
        group = ((mi_ref, mi, ei_out), (momi_ref, momi, momi_out), (wi_ref, wi, wi_out)) if wide else (
            (mo_ref, mo, eo_out), (momo_ref, momo, momo_out), (wo_ref, wo, wo_out))
        work.append(
            (wide, slot,
             [copy(src.at[slot], held.at[slot], load_sem.at[s, n]) for n, (src, held, _) in enumerate(group)],
             [copy(held.at[slot], out.at[slot], store_sem.at[s, n]) for n, (_, held, out) in enumerate(group)])
        )
    local = vec_mom_ref.shape[1]
    start = pl.ds(pl.multiple_of(lax.axis_index("tensor") * local, local), local)
    load_cols = [copy(x_ref.at[:, start], cols.at[0], cols_sem.at[0]), copy(g_ref.at[:, start], cols.at[1], cols_sem.at[1])]
    load_cols += [copy(ref, cols.at[2 + n], cols_sem.at[2 + n]) for n, ref in enumerate(part_refs)]
    store_ends = [copy(out, out_out, ends_sem.at[0]), copy(in_grad, in_grad_out, ends_sem.at[1])]
    for index, (_, _, loads, _) in enumerate(work):
        if index == slots_in:
            for load in load_cols:
                load.start()
        for load in loads:
            load.start()
    basis_in, basis_out = basis_in_ref[...], basis_out_ref[...]
    own_in, own_out = own_ref[0:8, :], own_ref[8:16, :]
    first_bias, first_out, first_vec, _ = bundle_rows(slots_in, slots_out)
    mom = MOMENTUM_DECAY * vec_mom_ref[...] + bundle_ref[first_vec : first_vec + vec_mom_ref.shape[0], :]
    vec_mom_out[...] = mom
    vec_out[...] = vec_ref[:, start] - VECTOR_RATE * mom
    mom = MOMENTUM_DECAY * bias_mom_ref[...] + bundle_ref[first_bias : first_bias + slots_in, :]
    bias_mom_out[...] = mom
    bias_out[...] = bias_ref[...] - VECTOR_RATE * mom
    for wide, slot, loads, stores in work:
        if not wide and slot == 0:
            for load in load_cols:
                load.wait()
            end_outputs(cols, stat_ref, far_ref, vec_ref[4:5, start], out, in_grad)
            for store in store_ends:
                store.start()
        right = bundle_ref[8 * slot : 8 * slot + 8, :] if wide else bundle_ref[
            first_out + 8 * slot : first_out + 8 * slot + 8, :]
        if wide:
            right_in_out[slot] = right
        else:
            right_out_out[slot] = right
        matrix, momentum, master = (mi, momi, wi) if wide else (mo, momo, wo)
        pair = (lambda b: outer(b, right)) if wide else (lambda b: outer(right, b))
        for load in loads:
            load.wait()
        matrix[slot] = matrix[slot] - pair(basis_in if wide else basis_out)
        stores[0].start()
        mom = MOMENTUM_DECAY * momentum[slot] + pair(own_in if wide else own_out)
        momentum[slot] = mom
        master[slot] = master[slot] - LEARN_RATE * mom
        stores[1].start()
        stores[2].start()
    for _, _, _, stores in work:
        for store in stores:
            store.wait()
    for store in store_ends:
        store.wait()


def end_outputs(cols, stat_ref, far_ref, bias, out, in_grad):
    rows, local = out.shape
    size = 2 * BLOCK
    count = far_ref.shape[0] + 1

    @pl.loop(0, rows // size)
    def _(step):
        span = pl.ds(pl.multiple_of(step * size, size), size)
        total = lambda first: sum(cols[first + n, span, :].astype(f32) for n in range(3))
        x = cols[0, span, :].astype(f32)
        out[span, :] = (x + total(2) + bias).astype(bf16)
        own = stat_ref[:, span]
        means = (own + sum(far_ref[k, :, span] for k in range(count - 1))).T / (count * local)
        own = own.T
        normed = (x - own[:, 2:3]) * own[:, 3:4]
        in_grad[span, :] = cols[1, span, :].astype(f32) + own[:, 3:4] * (
            total(5) - means[:, 0:1] - normed * means[:, 1:2]
        )


def finish(basis_in, basis_out, own, bundle, vec, vec_mom, bias, bias_mom, stats, far_stats, tokens, cot, parts, *matrices):
    anywhere = pl.BlockSpec(memory_space=pl.ANY)
    vmem = pl.BlockSpec(memory_space=pltpu.VMEM)
    like = lambda a: jax.ShapeDtypeStruct(a.shape, f32)
    slots_in, slots_out = matrices[0].shape[0], matrices[1].shape[0]
    local = vec_mom.shape[1]
    return pl.pallas_call(
        finish_kernel,
        in_specs=[vmem] * 10 + [anywhere] * (8 + len(parts)),
        out_specs=[anywhere] * 8 + [vmem] * 6,
        out_shape=[like(a) for a in matrices]
        + [jax.ShapeDtypeStruct(parts[0].shape, bf16), like(parts[0])]
        + [like(vec_mom), like(vec_mom), like(bias_mom), like(bias_mom)]
        + [jax.ShapeDtypeStruct((slots, 8, local), f32) for slots in (slots_in, slots_out)],
        scratch_shapes=[pltpu.VMEM(a.shape, f32) for a in matrices]
        + [
            pltpu.VMEM((8,) + parts[0].shape, bf16), pltpu.VMEM(parts[0].shape, bf16), pltpu.VMEM(parts[0].shape, f32),
            pltpu.SemaphoreType.DMA((slots_in + slots_out, 3)), pltpu.SemaphoreType.DMA((slots_in + slots_out, 3)),
            pltpu.SemaphoreType.DMA((8,)), pltpu.SemaphoreType.DMA((2,)),
        ],
        compiler_params=params(),
        name="finish",
    )(basis_in, basis_out, own, bundle, vec, vec_mom, bias, bias_mom, stats, far_stats, tokens, cot, *parts, *matrices)


def trade(axis, send, take, sems):
    me, size = lax.axis_index(axis), lax.axis_size(axis)
    copies = []
    for k in range(1, size):
        peer = lax.bitwise_xor(me, k)
        copies.append(
            pltpu.make_async_remote_copy(
                src_ref=send(peer, k), dst_ref=take(peer, k),
                send_sem=sems.at[0, k], recv_sem=sems.at[1, k],
                device_id={axis: peer}, device_id_type=MESH,
            )
        )
    for copy in copies:
        copy.start()
    return copies


def bundle_rows(slots_in, slots_out):
    biases = slots_in * 8
    outputs = 64 * pl.cdiv(biases + slots_in, 64)
    vectors = outputs + slots_out * 8
    return biases, outputs, vectors, outputs + 64 * pl.cdiv(slots_out * 8 + 8, 64)


def back_kernel(
    one_ref, two_ref, g_ref, gq_ref, gu_ref, att_ref, hid_ref, ei_ref, eo_ref,
    branch_pair, branch_far, branch_both, grad_pair, grad_far, grad_both, stat_ref,
    qi_ref, qo_ref, vec_ref, gsum_ref,
    branch_near_out, branch_far_out, grad_near_out, grad_far_out, stats_out, mi_out, mo_out,
    basis_in_ref, basis_out_ref, own_ref, bundle_ref,
    one, two, cot, gq, gu, att, hid, mi, mo, left, left_take, left_sum, vec_take, bundle, bundle_take, bundle_sum,
    sums, sum_take,
    load_sem, slot_sem, store_sem, link_sem, tensor_sem, stat_sem, pair_sem, pair_load_sem,
):
    copy = pltpu.make_async_copy
    me, column = lax.axis_index("dp"), lax.axis_index("tensor")
    workers, parts = lax.axis_size("dp"), lax.axis_size("tensor")
    slots_in, width, local = mi.shape
    slots_out = mo.shape[0]
    lanes = width // workers
    first_bias, first_out, first_vec, end = bundle_rows(slots_in, slots_out)

    barrier = pltpu.get_barrier_semaphore()
    for axis, size in (("dp", workers), ("tensor", parts)):
        for k in range(1, size):
            peer = lax.bitwise_xor(lax.axis_index(axis), k)
            pl.semaphore_signal(barrier, inc=1, device_id={axis: peer}, device_id_type=MESH)
    loads = {
        name: copy(src, dst, load_sem.at[index])
        for index, (name, src, dst) in enumerate(
            (("g", g_ref, cot), ("att", att_ref, att), ("one", one_ref, one), ("gq", gq_ref, gq), ("two", two_ref, two))
        )
    }
    load_hid = [copy(hid_ref.at[s], hid.at[s], slot_sem.at[0, s]) for s in range(slots_out - 1)]
    load_gu = [copy(gu_ref.at[s], gu.at[s], slot_sem.at[1, s]) for s in range(slots_in - 3)]
    load_mo = [copy(eo_ref.at[s], mo.at[s], slot_sem.at[2, s]) for s in range(slots_out)]
    load_mi = [copy(ei_ref.at[s], mi.at[s], slot_sem.at[3, s]) for s in range(slots_in)]
    store_mo = [copy(mo.at[s], mo_out.at[s], store_sem.at[0, s]) for s in range(slots_out)]
    store_mi = [copy(mi.at[s], mi_out.at[s], store_sem.at[1, s]) for s in range(slots_in)]
    sibling, opposite = lax.bitwise_xor(column, 1), lax.bitwise_xor(column, 2)

    def pass_to(peer, src, dst, index):
        return pltpu.make_async_remote_copy(
            src_ref=src, dst_ref=dst, send_sem=pair_sem.at[0, index], recv_sem=pair_sem.at[1, index],
            device_id={"tensor": peer}, device_id_type=MESH,
        )

    exchanges = []
    for n, (pair, far, both, near_out, far_out) in enumerate(
        ((branch_pair, branch_far, branch_both, branch_near_out, branch_far_out),
         (grad_pair, grad_far, grad_both, grad_near_out, grad_far_out))
    ):
        exchanges.append(
            (copy(far, sums.at[n], pair_load_sem.at[n]),
             pass_to(sibling, both, sum_take.at[n], 3 * n),
             pass_to(sibling, pair, near_out, 3 * n + 1),
             pass_to(opposite, sums.at[n], far_out, 3 * n + 2))
        )
    for load, _, _, _ in exchanges:
        load.start()
    loads["g"].start()
    loads["att"].start()
    load_mo[0].start()
    pl.semaphore_wait(barrier, workers + parts - 2)
    block = lambda index: pl.ds(pl.multiple_of(index * local, local), local)
    vec_copies = trade(
        "tensor", lambda peer, k: vec_ref.at[:, block(peer)], lambda peer, k: vec_take.at[k], tensor_sem
    )
    stat_copies = trade("tensor", lambda peer, k: stat_ref, lambda peer, k: stats_out.at[k - 1], stat_sem)
    for _, first, _, _ in exchanges:
        first.start()
    for _, _, second, _ in exchanges:
        second.start()
    for s in range(1, slots_out):
        load_hid[s - 1].start()
        load_mo[s].start()
    loads["one"].start()
    loads["gq"].start()
    for s in range(3):
        load_mi[s].start()
    loads["two"].start()
    for s in range(3, slots_in):
        load_gu[s - 3].start()
        load_mi[s].start()

    def send_sums(n):
        load, first, _, last = exchanges[n]
        load.wait()
        first.wait()
        sums[n] = (sums[n].astype(f32) + sum_take[n].astype(f32)).astype(bf16)
        last.start()

    part = lambda index: pl.ds(pl.multiple_of(index * lanes, lanes), lanes)
    sides = (pl.ds(0, 8), pl.ds(8, 8))
    bundles = ((0, first_out // workers), (first_out, (end - first_out) // workers))

    def left_send(n):
        return trade(
            "dp", lambda peer, k: left.at[sides[n], part(peer)], lambda peer, k: left_take.at[n, k], link_sem.at[0, n]
        )

    def left_spread(n, copies):
        for c in copies:
            c.wait()
        value = left[sides[n], part(me)]
        for k in range(1, workers):
            value = value + left_take[n, k]
        left_sum[sides[n], part(me)] = value / workers
        mine = left_sum.at[sides[n], part(me)]
        return trade("dp", lambda peer, k: mine, lambda peer, k: mine, link_sem.at[1, n])

    def basis_of(n, copies, basis_ref):
        for c in copies:
            c.wait()
        basis_ref[...] = orthonormal_rows(left_sum[sides[n], :])
        own_ref[sides[n], :] = basis_ref[:, part(me)]
        return stacked(basis_ref[...])

    def lot(n, index):
        start, size = bundles[n]
        return pl.ds(pl.multiple_of(start + index * size, size), size)

    def right_send(n):
        return trade(
            "dp", lambda peer, k: bundle.at[lot(n, peer), :],
            lambda peer, k: bundle_take.at[n, k], link_sem.at[2, n],
        )

    def right_spread(n, copies):
        for c in copies:
            c.wait()
        value = bundle[lot(n, me), :]
        for k in range(1, workers):
            value = value + bundle_take[n, k]
        bundle_sum[lot(n, me), :] = value / workers
        mine = bundle_sum.at[lot(n, me), :]
        return trade("dp", lambda peer, k: mine, lambda peer, k: mine, link_sem.at[3, n])

    bundle[...] = jnp.zeros_like(bundle)
    total = jnp.zeros((8, width), f32)
    loads["g"].wait()
    loads["att"].wait()
    for s in range(slots_out):
        if s:
            load_hid[s - 1].wait()
        if s == 1:
            send_sums(0)
        if s == 2:
            send_sums(1)
        load_mo[s].wait()
        value = dot(hid[s - 1] if s else att[...], cot[...], ROWS) + mo[s]
        mo[s] = value
        store_mo[s].start()
        high, low, _ = pieces(value)
        q = stacked(qo_ref[s])
        total = total + folded(dot(q, high)) + folded(dot(q, low))
    left[8:16, :] = total
    out_left = left_send(1)
    total = jnp.zeros((8, width), f32)
    loads["one"].wait()
    loads["gq"].wait()
    for s in range(slots_in):
        if s == 3:
            loads["two"].wait()
        if s >= 3:
            load_gu[s - 3].wait()
        if s == slots_in - 2:
            out_left = left_spread(1, out_left)
        load_mi[s].wait()
        grad = gq[s] if s < 3 else gu[s - 3]
        value = dot(one[...] if s < 3 else two[...], grad, ROWS) + mi[s]
        mi[s] = value
        store_mi[s].start()
        high, low, _ = pieces(value)
        q = stacked(qi_ref[s])
        total = total + folded(dot(q, high, COLS)) + folded(dot(q, low, COLS))
        bundle[first_bias + s : first_bias + s + 1, :] = jnp.sum(grad.astype(f32), 0, keepdims=True)
    left[0:8, :] = total
    in_left = left_send(0)

    side = basis_of(1, out_left, basis_out_ref)
    for s in range(slots_out):
        high, low, _ = pieces(mo[s])
        row = first_out + 8 * s
        bundle[row : row + 8, :] = folded(dot(side, high, COLS)) + folded(dot(side, low, COLS))
    for c in vec_copies:
        c.wait()
    vec = vec_ref[:, block(column)]
    for k in range(1, parts):
        vec = vec + vec_take[k]
    rows8 = lax.broadcasted_iota(jnp.int32, (8, local), 0)
    bundle[first_vec : first_vec + 8, :] = jnp.where(
        rows8 < 4, vec, jnp.where(rows8 == 4, gsum_ref[0:1, block(column)], 0.0)
    )
    in_left = left_spread(0, in_left)
    out_right = right_send(1)
    side = basis_of(0, in_left, basis_in_ref)
    for s in range(slots_in):
        if s == 3:
            out_right = right_spread(1, out_right)
        high, low, _ = pieces(mi[s])
        bundle[8 * s : 8 * s + 8, :] = folded(dot(side, high)) + folded(dot(side, low))
    in_right = right_spread(0, right_send(0))
    for c in out_right + in_right:
        c.wait()
    bundle_ref[...] = bundle_sum[...]
    for store in store_mo + store_mi:
        store.wait()
    for c in stat_copies:
        c.wait()
    for _, _, second, last in exchanges:
        second.wait()
        last.wait()


def back(norm_one, norm_two, cot, grad_qkv, grad_up, att, hidden, error_in, error_out, branch, grad, stats,
    q_in, q_out, vec, gsum):
    slots_in, width, local = error_in.shape
    slots_out = error_out.shape[0]
    workers, parts = lax.axis_size("dp"), lax.axis_size("tensor")
    anywhere = pl.BlockSpec(memory_space=pl.ANY)
    vmem = pl.BlockSpec(memory_space=pltpu.VMEM)
    shape = jax.ShapeDtypeStruct
    rows = bundle_rows(slots_in, slots_out)[-1]
    group = rows // 2 // workers
    like = lambda a: pltpu.VMEM(a.shape, a.dtype)
    return pl.pallas_call(
        back_kernel,
        in_specs=[anywhere] * 16 + [vmem] * 4,
        out_specs=[anywhere] * 7 + [vmem] * 4,
        out_shape=[shape(branch[0].shape, bf16)] * 4 + [
            shape((parts - 1,) + stats.shape, f32),
            shape(error_in.shape, f32), shape(error_out.shape, f32),
            shape((8, width), f32), shape((8, width), f32), shape((16, width // workers), f32),
            shape((rows, local), f32),
        ],
        scratch_shapes=[
            like(a) for a in (norm_one, norm_two, cot, grad_qkv, grad_up, att, hidden, error_in, error_out)
        ] + [
            pltpu.VMEM((16, width), f32), pltpu.VMEM((2, workers, 8, width // workers), f32),
            pltpu.VMEM((16, width), f32), pltpu.VMEM((parts, 8, local), f32),
            pltpu.VMEM((rows, local), f32), pltpu.VMEM((2, workers, group, local), f32), pltpu.VMEM((rows, local), f32),
            pltpu.VMEM((2,) + branch[0].shape, bf16), pltpu.VMEM((2,) + branch[0].shape, bf16),
            pltpu.SemaphoreType.DMA((5,)), pltpu.SemaphoreType.DMA((4, slots_in)),
            pltpu.SemaphoreType.DMA((2, slots_in)), pltpu.SemaphoreType.DMA((4, 2, 2, workers)),
            pltpu.SemaphoreType.DMA((2, parts)), pltpu.SemaphoreType.DMA((2, parts)),
            pltpu.SemaphoreType.DMA((2, 6)), pltpu.SemaphoreType.DMA((2,)),
        ],
        compiler_params=params(collective_id=1, has_side_effects=True),
        name="back",
    )(norm_one, norm_two, cot, grad_qkv, grad_up, att, hidden, error_in, error_out,
      *branch[1:], *grad[1:], stats, q_in, q_out, vec, gsum)


def swapped(value, axis, bits):
    size = lax.axis_size(axis)
    return lax.ppermute(value, axis, [(i, i ^ bits) for i in range(size)])


def spread(parts):
    return [parts[0]] + [swapped(part, "tensor", k) for k, part in enumerate(parts) if k]


def on_device(
    tokens, cotangent, segments, w_in_master, w_out_master, vec_master, bias_in_master,
    w_in_mom, w_out_mom, vec_mom, bias_in_mom, w_in_error, w_out_error, q_in, q_out,
):
    workers = lax.axis_size("dp")
    tensor_index = lax.axis_index("tensor")
    worker_index = lax.axis_index("dp")
    rows, width = tokens.shape
    local = bias_in_master.shape[1]
    start_col = tensor_index * local
    cut = lambda a: lax.dynamic_slice_in_dim(a, start_col, local, 1)

    w_in = w_in_master.transpose(1, 0, 2)
    linked = workers == 8
    if linked:
        shards = w_in, w_out_master.reshape(5 * local, -1)
    else:
        w_in_low = lax.all_gather(w_in.astype(bf16), "dp", axis=1, tiled=True)
        w_out_low = lax.all_gather(w_out_master.astype(bf16), "dp", axis=2, tiled=True).transpose(0, 2, 1)
        pairs = jnp.stack([w_in_low[FIRST:], w_out_low[1:]], 1).reshape(-1, width, local)
        shards = jnp.concatenate([w_in_low[:FIRST], w_out_low[:1], pairs], 0), w_out_master.reshape(5 * local, -1)
    w_up, w_attn, norm_one, norm_two, att, grad_qkv, *branch_parts, grad_up, hidden, cot_sum = front(
        linked, *shards, tokens, cotangent, vec_master, bias_in_master, segments
    )

    factors_in, factors_out = q_in.transpose(0, 2, 1), q_out.transpose(0, 2, 1)
    error_in = w_in_error[0].transpose(1, 0, 2)
    error_out = w_out_error[0]
    *grad_parts, stats, vec_local = norm_grad(grad_qkv, grad_up, w_attn, w_up, tokens, vec_master)

    if linked:
        (
            branch_near, branch_far, grad_near, grad_far, far_stats,
            matrix_in_f32, matrix_out_f32, basis_in, basis_out, own, bundle,
        ) = back(
            norm_one, norm_two, cotangent, grad_qkv, grad_up, att, hidden, error_in, error_out,
            branch_parts, grad_parts, stats, factors_in, factors_out, vec_local, cot_sum,
        )
        branch = branch_parts[0], branch_near, branch_far
        grad = grad_parts[0], grad_near, grad_far
    else:
        branch, grad = (
            (parts[0], swapped(parts[1], "tensor", 1), swapped(parts[2], "tensor", 2) + swapped(parts[3], "tensor", 3))
            for parts in (branch_parts, grad_parts)
        )
        far_stats = jnp.stack(spread([stats] * 4)[1:])
        *parts_out, left_out = matrix_out(att, hidden, cotangent, error_out, factors_out)
        *parts_in, left_in, bias_local = matrix_in(norm_one, norm_two, grad_qkv, grad_up, error_in, factors_in)
        left = lax.psum(jnp.concatenate([left_in, left_out], 0), "dp") / workers
        basis_in, basis_out = bases(left[:8], left[8:])
        vec_rows = cut(jnp.concatenate([lax.psum(vec_local[:4], "tensor"), cot_sum[:1]], 0))
        bundle = jnp.zeros((bundle_rows(7, 5)[-1], local), f32)
        for start, rows_of in zip(
            (0,) + bundle_rows(7, 5)[:3],
            (
                right_factor(basis_in, parts_in, PLAIN, local).reshape(-1, local), bias_local[:, 0, :],
                right_factor(basis_out, parts_out, COLS, local).reshape(-1, local), vec_rows,
            ),
        ):
            bundle = lax.dynamic_update_slice_in_dim(bundle, rows_of, start, 0)
        bundle = lax.psum(bundle, "dp") / workers
        matrix_in_f32, matrix_out_f32 = (
            high.astype(f32) + low.astype(f32) for high, low in (parts_in, parts_out)
        )
        owned = w_in.shape[1]
        own = jnp.concatenate([basis_in, basis_out], 0)
        own = lax.dynamic_slice_in_dim(own, worker_index * owned, owned, 1)
    (
        new_error_in, new_error_out, new_mom_in, new_mom_out, new_w_in, new_w_out, block_out, input_grad,
        vec_new, vec_mom_new, bias_in_new, bias_in_mom_new, right_in, right_out,
    ) = finish(
        basis_in, basis_out, own, bundle, vec_master, vec_mom, bias_in_master, bias_in_mom,
        stats, far_stats, tokens, cotangent, [*branch, *grad],
        matrix_in_f32, matrix_out_f32, w_in_mom.transpose(1, 0, 2), w_out_mom, w_in, w_out_master,
    )
    return (
        block_out,
        input_grad,
        new_w_in.transpose(1, 0, 2),
        new_w_out,
        vec_new,
        bias_in_new,
        new_mom_in.transpose(1, 0, 2),
        new_mom_out,
        vec_mom_new,
        bias_in_mom_new,
        new_error_in.transpose(1, 0, 2)[None],
        new_error_out[None],
        right_in.transpose(0, 2, 1),
        right_out.transpose(0, 2, 1),
    )


def solution(mesh):
    return jax.shard_map(
        on_device,
        mesh=mesh,
        in_specs=(
            P("dp", None), P("dp", None), P("dp", None), P("dp", None, "tensor"),
            P(None, "tensor", "dp"), P(), P(None, "tensor"), P("dp", None, "tensor"),
            P(None, "tensor", "dp"), P(None, "tensor"), P(None, "tensor"),
            P("dp", None, None, "tensor"), P("dp", None, "tensor", None),
            P(None, "tensor", None), P(None, "tensor", None),
        ),
        out_specs=(
            P("dp", "tensor"), P("dp", "tensor"), P("dp", None, "tensor"), P(None, "tensor", "dp"),
            P(None, "tensor"), P(None, "tensor"), P("dp", None, "tensor"), P(None, "tensor", "dp"),
            P(None, "tensor"), P(None, "tensor"), P("dp", None, None, "tensor"),
            P("dp", None, "tensor", None), P(None, "tensor", None), P(None, "tensor", None),
        ),
        check_vma=False,
    )
```
